32 devices in a mesh: fsdp: 2 (over x), ctx: 8 (over z, y), tp: 2 (over core).
Axes of the slice: x: 2, y: 2, z: 4, core: 2. Of those that a mesh axis runs over, the one named last changes fastest.
Arguments:
- tokens: bfloat16 [4096, 1024], P(('fsdp', 'ctx', 'tp')), may hold values from -6 to 6
- qkv_weight: bfloat16 [2, 1024, 3, 1024], P(None, 'fsdp', None, 'tp'), may hold values from -0.1875 to 0.1875
- out_weight: bfloat16 [2, 1024, 1024], P(None, 'tp', 'fsdp'), may hold values from -0.5 to 0.5
- up_weight: bfloat16 [2, 1024, 4096], P(None, 'fsdp', 'tp'), may hold values from -0.1875 to 0.1875
- down_weight: bfloat16 [2, 4096, 1024], P(None, 'tp', 'fsdp'), may hold values from -0.125 to 0.125
- qv_bias: float32 [2, 2, 1024], P(None, None, 'tp'), may hold values from -3 to 3
- up_bias: float32 [2, 4096], P(None, 'tp'), may hold values from -2 to 2
- norm_gains: float32 [2, 2, 1024], replicated, may hold values from 0.25 to 1.75
- row_biases: float32 [2, 4, 1024], replicated, may hold values from -2 to 2
- parent_ids: int32 [32], replicated, may hold values from 0 to 30, as said below
- depth_offsets: int32 [32], replicated, may hold values from 0 to 1920, as said below
- cotangent: bfloat16 [4096, 1024], P(('fsdp', 'ctx', 'tp')), may hold values from -6 to 6
Outputs:
- output: bfloat16 [4096, 1024], P(('fsdp', 'ctx', 'tp'))
- input_grad: float32 [4096, 1024], P(('fsdp', 'ctx', 'tp'))
- qkv_weight_grad: float32 [2, 1024, 3, 1024], P(None, 'fsdp', None, 'tp')
- out_weight_grad: float32 [2, 1024, 1024], P(None, 'tp', 'fsdp')
- up_weight_grad: float32 [2, 1024, 4096], P(None, 'fsdp', 'tp')
- down_weight_grad: float32 [2, 4096, 1024], P(None, 'tp', 'fsdp')
- qv_bias_grad: float32 [2, 2, 1024], P(None, None, 'tp')
- up_bias_grad: float32 [2, 4096], P(None, 'tp')
- gain_grad: float32 [2, 2, 1024], replicated
- bias_grad: float32 [2, 4, 1024], replicated
The draws below stay inside these ranges and needn't reach their ends.
Inputs may be any that keep to these rules, and one draw needn't show every extreme that they name: `parent_ids`: segments form trees of 16 consecutive segments, starting at multiples of 16; a tree's first segment is its root and its own parent; any other segment's parent is an earlier segment of the same tree. In the last tree every other segment's parent is the segment just before it. `depth_offsets`: A root's depth offset is 0; any other segment's is its parent's plus 128.
All inputs are finite; a program needn't handle non-finite values.
Results may differ from the reference program's by a relative error of at most 0.023.
Values may be sent and summed in bfloat16 or wider, within the bound.
No kernel may reach another device: no remote copies, remote signals or barrier semaphores. Data moves between devices by JAX's collectives and lax.ppermute only.
A program may use at most 384 MiB of HBM per device.

```python
import jax
import jax.numpy as jnp
from jax import lax

D = 1024
HEADS = 8
HEAD_DIM = 128
FF = 4096
LAYERS = 2
SEG = 128
TREE_SEGS = 16
SEGS = 32
TOKENS = 4096


def tree_tables(key):
    pick_key = jax.random.fold_in(key, 17)
    coin_key = jax.random.fold_in(key, 29)
    tree_count = SEGS // TREE_SEGS
    trunk_len = max(1, TREE_SEGS // 4)
    positions = jnp.arange(TREE_SEGS, dtype=jnp.int32)
    span = jnp.maximum(positions - trunk_len + 1, 1)
    raw_pick = jax.random.randint(pick_key, (tree_count, TREE_SEGS), 0, 1 << 20)
    picked = trunk_len - 1 + raw_pick % span[None, :]
    coin = jax.random.randint(coin_key, (tree_count, TREE_SEGS), 0, 2)
    branch_parent = jnp.where(coin == 0, trunk_len - 1, picked)
    chain = jnp.maximum(positions - 1, 0)
    parents_local = jnp.where(positions[None, :] >= trunk_len, branch_parent, chain[None, :])
    tree_rank = jnp.arange(tree_count, dtype=jnp.int32)[:, None]
    parents_local = jnp.where(tree_rank == tree_count - 1, chain[None, :], parents_local).astype(jnp.int32)

    def settle(step_index, levels):
        column = lax.dynamic_index_in_dim(parents_local, step_index, 1, keepdims=False)
        parent_level = jnp.take_along_axis(levels, column[:, None], axis=1)[:, 0]
        return levels.at[:, step_index].set(parent_level + 1)
    levels = lax.fori_loop(1, TREE_SEGS, settle, jnp.zeros((tree_count, TREE_SEGS), jnp.int32))
    tree_base = (jnp.arange(tree_count, dtype=jnp.int32) * TREE_SEGS)[:, None]
    return ((parents_local + tree_base).reshape(-1), (levels * SEG).reshape(-1).astype(jnp.int32))


def draw_parent_ids(key, part):
    return tree_tables(key)[0]


def draw_depth_offsets(key, part):
    return tree_tables(key)[1]


def block_scale(stream_key, extent, shards, least, top_value):
    level = 1.0
    for position, shards_of in shards:
        heights = jax.random.uniform(jax.random.fold_in(jax.random.fold_in(stream_key, 6), position), (shards_of,), jnp.float32, least / len(shards), top_value / len(shards))
        level = level * jnp.repeat(jnp.exp(heights), extent[position] // shards_of).reshape((-1,) + (1,) * (len(extent) - 1 - position))
    return level


def gaussian(rng, shape, deviation, bound, pieces=(), held_as=jnp.bfloat16):
    drawn = jax.random.normal(rng, shape, jnp.float32) * deviation
    if len(pieces) > 0:
        drawn = block_scale(rng, shape, pieces, -0.22, 0.18) * drawn
    return jnp.clip(drawn, min=-bound, max=bound).astype(held_as)


def setup_inputs(seed: int = 0) -> dict:
    key_list = jax.random.split(jax.random.key(seed), 13)
    tokens = gaussian(key_list[0], (TOKENS, D), 1.0, 6.0, ((0, 32),))
    qkv_weight = gaussian(key_list[1], (LAYERS, D, 3, D), D ** -0.5, 0.1875, ((1, 2), (3, 2)))
    out_weight = gaussian(key_list[2], (LAYERS, D, D), (D // 8) ** -0.5, 0.5, ((1, 2), (2, 2)))
    up_weight = gaussian(key_list[3], (LAYERS, D, FF), D ** -0.5, 0.1875, ((1, 2), (2, 2)))
    down_weight = gaussian(key_list[4], (LAYERS, FF, D), (FF // 2) ** -0.5, 0.125, ((1, 2), (2, 2)))
    qv_bias = gaussian(key_list[5], (LAYERS, 2, D), 0.5, 3.0, ((2, 2),), jnp.float32)
    up_bias = gaussian(key_list[6], (LAYERS, FF), 0.3, 2.0, ((1, 2),), jnp.float32)
    norm_gains = jnp.clip(1.0 + 0.15 * jax.random.normal(key_list[7], (LAYERS, 2, D), jnp.float32), 0.25, 1.75)
    row_biases = gaussian(key_list[8], (LAYERS, 4, D), 0.3, 2.0, (), jnp.float32)
    parent_ids = draw_parent_ids(jax.random.fold_in(key_list[12], 71), 0)
    depth_offsets = draw_depth_offsets(jax.random.fold_in(key_list[12], 71), 0)
    cotangent = gaussian(key_list[11], (TOKENS, D), 1.0, 6.0, ((0, 32),))
    return {"tokens": tokens, "qkv_weight": qkv_weight, "out_weight": out_weight, "up_weight": up_weight, "down_weight": down_weight, "qv_bias": qv_bias, "up_bias": up_bias, "norm_gains": norm_gains, "row_biases": row_biases, "parent_ids": parent_ids, "depth_offsets": depth_offsets, "cotangent": cotangent}


EPSILON = 1e-05
MASKED = -1e+30
HIGHEST = lax.Precision.HIGHEST

@jax.custom_vjp
def low(v):
    return lax.optimization_barrier(v.astype(jnp.bfloat16)).astype(jnp.float32)

@jax.custom_vjp
def low_back(v):
    return v

def low_keep(v):
    return (low(v), None)

def low_pass(kept, grad):
    return (grad,)

def back_keep(v):
    return (v, None)

def back_low(kept, grad):
    return (low(grad),)
low.defvjp(low_keep, low_pass)
low_back.defvjp(back_keep, back_low)

def rounded(values):
    return low(low_back(values))

def smooth_act(values):
    return jax.nn.gelu(values, approximate=True)

def layer_norm(values, gain, shift):
    centered = values - lax.optimization_barrier(jnp.mean(values, axis=-1, keepdims=True))
    variance = lax.optimization_barrier(jnp.mean(centered * centered, axis=-1, keepdims=True))
    return centered * lax.rsqrt(variance + EPSILON) * gain + shift

def matmul(left, right):
    return jnp.dot(left, right, precision=HIGHEST, preferred_element_type=jnp.float32)

def tree_attention(members):
    query, keys, values, parents_tree, depths_tree = members
    tree_tokens = query.shape[0]
    seg_count = parents_tree.shape[0]
    segment_ids = jnp.arange(seg_count, dtype=jnp.int32)

    def climb(step_index, state):
        current, member = state
        upward = parents_tree[current]
        return (upward, member | (upward[:, None] == segment_ids[None, :]))
    same_segment = segment_ids[:, None] == segment_ids[None, :]
    ignored, member = lax.fori_loop(0, seg_count, climb, (segment_ids, same_segment))
    strict = member & jnp.logical_not(same_segment)
    token_ids = jnp.arange(tree_tokens, dtype=jnp.int32)
    token_segment = token_ids // SEG
    token_position = token_ids % SEG
    allowed = strict[token_segment][:, token_segment] | (token_segment[:, None] == token_segment[None, :]) & (token_position[None, :] <= token_position[:, None])
    token_depth = depths_tree[token_segment] + token_position
    distance = (token_depth[:, None] - token_depth[None, :]).astype(jnp.float32)
    slopes = jnp.exp2(-(jnp.arange(HEADS, dtype=jnp.int32) + 1).astype(jnp.float32))

    def one_head(head_members):
        head_query, head_keys, head_values, slope = head_members
        scores = matmul(head_query, head_keys.T) * HEAD_DIM ** (-0.5) - slope * distance
        scores = low_back(jnp.where(allowed, scores, MASKED))
        probs = low(jax.nn.softmax(scores, axis=-1))
        return matmul(probs, head_values)
    heads_out = lax.map(one_head, (query.transpose(1, 0, 2), keys.transpose(1, 0, 2), values.transpose(1, 0, 2), slopes))
    return heads_out.transpose(1, 0, 2)

def forward(hidden, qkv_weight, out_weight, up_weight, down_weight, qv_bias, up_bias, norm_gains, row_biases, parent_ids, depth_offsets):
    tree_count = parent_ids.shape[0] // TREE_SEGS
    tree_tokens = TREE_SEGS * SEG
    parents_local = parent_ids.reshape(tree_count, TREE_SEGS) - (jnp.arange(tree_count, dtype=jnp.int32) * TREE_SEGS)[:, None]
    depths_local = depth_offsets.reshape(tree_count, TREE_SEGS)
    attend_tree = jax.checkpoint(tree_attention)

    def to_trees(values):
        return values.reshape(tree_count, tree_tokens, HEADS, HEAD_DIM)
    for layer_index in range(LAYERS):
        normed = low(layer_norm(hidden, norm_gains[layer_index, 0], row_biases[layer_index, 0]))
        projected = jnp.einsum('td,dcf->tcf', normed, qkv_weight[layer_index], precision=HIGHEST)
        query = rounded(projected[:, 0] + qv_bias[layer_index, 0])
        keys = rounded(projected[:, 1])
        values = rounded(projected[:, 2] + qv_bias[layer_index, 1])
        context = lax.map(attend_tree, (to_trees(query), to_trees(keys), to_trees(values), parents_local, depths_local))
        context = rounded(context.reshape(hidden.shape[0], -1))
        attended = low_back(matmul(context, out_weight[layer_index]) + row_biases[layer_index, 1])
        middle = hidden + attended
        normed_two = low(layer_norm(middle, norm_gains[layer_index, 1], row_biases[layer_index, 2]))
        pre_act = low_back(matmul(normed_two, up_weight[layer_index]) + up_bias[layer_index])
        activity = low(smooth_act(pre_act))
        branch = low_back(matmul(activity, down_weight[layer_index]) + row_biases[layer_index, 3])
        hidden = middle + branch
    return hidden

def reference(tokens, qkv_weight, out_weight, up_weight, down_weight, qv_bias, up_bias, norm_gains, row_biases, parent_ids, depth_offsets, cotangent):

    def run(hidden, w_qkv, w_out, w_up, w_down, b_qv, b_up, gains, shifts):
        return forward(hidden, w_qkv, w_out, w_up, w_down, b_qv, b_up, gains, shifts, parent_ids, depth_offsets)
    output, pullback = jax.vjp(run, tokens.astype(jnp.float32), qkv_weight.astype(jnp.float32), out_weight.astype(jnp.float32), up_weight.astype(jnp.float32), down_weight.astype(jnp.float32), qv_bias.astype(jnp.float32), up_bias.astype(jnp.float32), norm_gains.astype(jnp.float32), row_biases.astype(jnp.float32))
    grads = pullback(cotangent.astype(jnp.float32))
    return (output.astype(jnp.bfloat16), grads[0], grads[1], grads[2], grads[3], grads[4], grads[5], grads[6], grads[7], grads[8])
```

```python
import functools

import jax
import jax.numpy as jnp
from jax import lax
from jax.experimental import pallas as pl
from jax.experimental.pallas import tpu as pltpu
from jax.sharding import PartitionSpec as P

HEAD_DIM = 128
LAYERS = 2
SEG = 128
EPSILON = 1e-05
MASKED = -1e30
SCALE = HEAD_DIM ** (-0.5)
GELU_A = 0.7978845608028654
GELU_B = 0.044715
BF = jnp.bfloat16
F32 = jnp.float32
VLIM = 56 * 1024 * 1024

NN = (((1,), (0,)), ((), ()))
NT = (((1,), (1,)), ((), ()))
TN = (((0,), (0,)), ((), ()))


def mm(a, b, dims=NN):
    return lax.dot_general(a, b, dims, preferred_element_type=F32)


def sds(shape, dtype):
    return jax.ShapeDtypeStruct(shape, dtype)


VSPEC = pl.BlockSpec(memory_space=pltpu.VMEM)
SSPEC = pl.BlockSpec(memory_space=pltpu.SMEM)


def cost(flops, nbytes):
    return pl.CostEstimate(flops=int(flops), bytes_accessed=int(nbytes), transcendentals=0)


def norm_rows(v):
    centered = v - jnp.mean(v, axis=-1, keepdims=True)
    rstd = lax.rsqrt(jnp.mean(centered * centered, axis=-1, keepdims=True) + EPSILON)
    return centered * rstd, rstd


def norm_back(d, v, gain):
    xhat, rstd = norm_rows(v)
    dx = d * gain
    back = rstd * (
        dx
        - jnp.mean(dx, axis=-1, keepdims=True)
        - xhat * jnp.mean(dx * xhat, axis=-1, keepdims=True)
    )
    d_gain = jnp.sum(d * xhat, axis=0, keepdims=True)
    d_shift = jnp.sum(d, axis=0, keepdims=True)
    return back, d_gain, d_shift


class Dims:
    def __init__(self, tokens, qkv_weight, up_weight):
        self.tp = lax.axis_size("tp")
        self.C = lax.axis_size("ctx")
        self.T = tokens.shape[0] * self.tp
        self.D = tokens.shape[1]
        self.H = self.D // lax.axis_size("fsdp")
        self.Q = self.H // 2
        self.W = qkv_weight.shape[3]
        self.F = up_weight.shape[2]
        self.lh = self.W // HEAD_DIM
        self.g = self.C // self.lh
        self.rq = self.T // self.g
        self.chunk = self.rq + 2 * self.T
        self.bits = self.C.bit_length() - 1


def offs(sc, d):
    x = sc[0]
    y = sc[1]
    own = pl.multiple_of(x * d.H, d.H)
    oth = pl.multiple_of((1 - x) * d.H, d.H)
    first = pl.multiple_of((1 - x) * d.H + y * d.Q, d.Q)
    second = pl.multiple_of((1 - x) * d.H + (1 - y) * d.Q, d.Q)
    return own, oth, first, second


def qkv_body(d, first, *refs):
    if first:
        sc, hid, gain, shift, w, w1, w2, qvb = refs[:8]
        rest = refs[8:]
        hidden = hid[...].astype(F32)
    else:
        sc, mid, pa, pb, bias, gain, shift, w, w1, w2, qvb = refs[:11]
        rest = refs[11:]
        hidden = mid[...] + ((pa[...].astype(F32) + pb[...].astype(F32)) + bias[...])
    h_out, n_out, ns_out = rest[:3]
    chunks = rest[3 : 3 + d.C]
    scr = rest[3 + d.C]
    own, oth, p1, p2 = offs(sc, d)
    h_out[...] = hidden
    xhat, _ = norm_rows(hidden)
    n_out[...] = (xhat * gain[...] + shift[...]).astype(BF)
    ns_out[...] = n_out[:, pl.ds(oth, d.H)]
    a0 = n_out[:, pl.ds(own, d.H)]
    a1 = n_out[:, pl.ds(p1, d.Q)]
    a2 = n_out[:, pl.ds(p2, d.Q)]
    for n in range(3):
        proj = mm(a0, w[n]) + mm(a1, w1[n]) + mm(a2, w2[n])
        if n == 0:
            proj = proj + qvb[0:1, :]
        if n == 2:
            proj = proj + qvb[1:2, :]
        scr[n] = proj.astype(BF)
    c = sc[2]
    for o in range(d.C):
        to = lax.rem(c + o, d.C)
        col = pl.multiple_of(lax.div(to, d.g) * HEAD_DIM, HEAD_DIM)
        row = pl.multiple_of(lax.rem(to, d.g) * d.rq, d.rq)
        chunks[o][0 : d.rq, :] = scr[0, pl.ds(row, d.rq), pl.ds(col, HEAD_DIM)]
        chunks[o][d.rq : d.rq + d.T, :] = scr[1, :, pl.ds(col, HEAD_DIM)]
        chunks[o][d.rq + d.T :, :] = scr[2, :, pl.ds(col, HEAD_DIM)]


def whole(shape):
    return pl.BlockSpec(shape, lambda *_: (0,) * len(shape))


def qkv_forward(d, layer, sc, hid, gain, shift, w, pieces, qvb):
    first = not isinstance(hid, tuple)
    hid = (hid,) if first else hid
    wspec = pl.BlockSpec((None, 3, d.H, d.W), lambda i: (layer, 0, 0, 0))
    in_specs = [SSPEC] + [whole(a.shape) for a in hid]
    in_specs += [whole(gain.shape), whole(shift.shape), wspec]
    in_specs += [whole(a.shape) for a in pieces] + [whole(qvb.shape)]
    outs = [sds((d.T, d.D), F32), sds((d.T, d.D), BF), sds((d.T, d.H), BF)]
    outs += [sds((d.chunk, HEAD_DIM), BF)] * d.C
    return pl.pallas_call(
        functools.partial(qkv_body, d, first),
        grid=(1,),
        in_specs=in_specs,
        out_specs=[whole(o.shape) for o in outs],
        out_shape=outs,
        scratch_shapes=[pltpu.VMEM((3, d.T, d.W), BF)],
        compiler_params=pltpu.CompilerParams(vmem_limit_bytes=VLIM),
        cost_estimate=cost(2 * d.T * d.D * 3 * d.W, 8e6),
        name="qkv_forward",
    )(sc, *hid, gain, shift, w, *pieces, qvb)


def load_chunks(d, sc, chunks, qs, ks, vs):
    c = sc[2]
    for o in range(d.C):
        src = lax.rem(c - o + d.C, d.C)
        qs[src] = chunks[o][0 : d.rq, :]
        ks[src] = chunks[o][d.rq : d.rq + d.T, :]
        vs[src] = chunks[o][d.rq + d.T :, :]


def score_block(d, sc, kb, q, k, s, ext):
    part = lax.rem(sc[2], d.g)
    seg = s * (d.T // SEG) + lax.div(part * d.rq, SEG)
    scores = mm(q, k, NT) * SCALE + kb[pl.ds(seg, 1), 0:ext]
    col = lax.broadcasted_iota(jnp.int32, (d.rq, ext), 1) - s * d.T
    row = lax.broadcasted_iota(jnp.int32, (d.rq, ext), 0) + part * d.rq
    return jnp.where(col <= row, scores, MASKED)


UNROLL = 8


def each_source(d, one):
    if d.C <= UNROLL:
        for s in range(d.C):
            one(s, s + 1)
    else:
        lax.fori_loop(0, d.C, lambda s, carry: (one(s, d.C), carry)[1], 0)


def attend_body(d, *refs):
    sc, kb = refs[:2]
    chunks = refs[2 : 2 + d.C]
    outs = refs[2 + d.C : 2 + 2 * d.C]
    qs, ks, vs, cs = refs[2 + 2 * d.C :]
    load_chunks(d, sc, chunks, qs, ks, vs)
    def one(s, seen):
        ext = seen * d.T
        k = ks[0:seen].reshape(ext, HEAD_DIM)
        v = vs[0:seen].reshape(ext, HEAD_DIM)
        scores = score_block(d, sc, kb, qs[s], k, s, ext)
        e = jnp.exp(scores - jnp.max(scores, axis=-1, keepdims=True))
        total = jnp.sum(e, axis=-1, keepdims=True)
        cs[s] = (mm(e.astype(BF), v) / total).astype(BF)

    each_source(d, one)
    c = sc[2]
    for o in range(d.C):
        outs[o][...] = cs[lax.rem(c + o, d.C)]


def attend_forward(d, sc, kb, chunks):
    return pl.pallas_call(
        functools.partial(attend_body, d),
        in_specs=[SSPEC] + [VSPEC] * (1 + d.C),
        out_specs=[VSPEC] * d.C,
        out_shape=[sds((d.rq, HEAD_DIM), BF)] * d.C,
        scratch_shapes=[
            pltpu.VMEM((d.C, d.rq, HEAD_DIM), BF),
            pltpu.VMEM((d.C, d.T, HEAD_DIM), BF),
            pltpu.VMEM((d.C, d.T, HEAD_DIM), BF),
            pltpu.VMEM((d.C, d.rq, HEAD_DIM), BF),
        ],
        compiler_params=pltpu.CompilerParams(vmem_limit_bytes=VLIM),
        cost_estimate=cost(2 * d.C * d.rq * d.C * d.T * HEAD_DIM * 2, 3e6),
        name="attend_forward",
    )(sc, kb, *chunks)


def out_body(d, *refs):
    sc, w, w1, w2 = refs[:4]
    chunks = refs[4 : 4 + d.C]
    ctx, part = refs[4 + d.C :]
    c = sc[2]
    for o in range(d.C):
        src = lax.rem(c - o + d.C, d.C)
        col = pl.multiple_of(lax.div(src, d.g) * HEAD_DIM, HEAD_DIM)
        row = pl.multiple_of(lax.rem(src, d.g) * d.rq, d.rq)
        ctx[pl.ds(row, d.rq), pl.ds(col, HEAD_DIM)] = chunks[o][...]
    own, oth, _, _ = offs(sc, d)
    half = d.W // 2
    k1 = pl.multiple_of(sc[1] * half, half)
    k2 = pl.multiple_of((1 - sc[1]) * half, half)
    part[:, pl.ds(own, d.H)] = mm(ctx[...], w[...]).astype(BF)
    part[:, pl.ds(oth, d.H)] = (
        mm(ctx[:, pl.ds(k1, half)], w1[...]) + mm(ctx[:, pl.ds(k2, half)], w2[...])
    ).astype(BF)


def out_forward(d, layer, sc, w, pieces, chunks):
    wspec = pl.BlockSpec((None, d.W, d.H), lambda i: (layer, 0, 0))
    outs = [sds((d.T, d.W), BF), sds((d.T, d.D), BF)]
    return pl.pallas_call(
        functools.partial(out_body, d),
        grid=(1,),
        in_specs=[SSPEC, wspec] + [whole(a.shape) for a in (*pieces, *chunks)],
        out_specs=[whole(o.shape) for o in outs],
        out_shape=outs,
        compiler_params=pltpu.CompilerParams(vmem_limit_bytes=VLIM),
        cost_estimate=cost(2 * d.T * d.D * d.W, 3e6),
        name="out_forward",
    )(sc, w, *pieces, *chunks)


def ffn_body(d, tiles, sc, hid, pa, pb, bias, gain, shift, u, u1, u2, ub, w, w1, w2,
             mid, n2, ns, act, dg, part, acc):
    f = pl.program_id(0)
    own, oth, p1, p2 = offs(sc, d)

    @pl.when(f == 0)
    def _():
        m = hid[...] + ((pa[...].astype(F32) + pb[...].astype(F32)) + bias[...])
        mid[...] = m
        xhat, _ = norm_rows(m)
        n2[...] = (xhat * gain[...] + shift[...]).astype(BF)
        ns[...] = n2[:, pl.ds(oth, d.H)]
        acc[...] = jnp.zeros_like(acc)

    pre = (
        mm(n2[:, pl.ds(own, d.H)], u[...])
        + mm(n2[:, pl.ds(p1, d.Q)], u1[...])
        + mm(n2[:, pl.ds(p2, d.Q)], u2[...])
        + ub[...]
    )
    sq = pre * pre
    th = jnp.tanh(GELU_A * pre * (1.0 + GELU_B * sq))
    half = 0.5 * (1.0 + th)
    a = (pre * half).astype(BF)
    act[...] = a
    dg[...] = (
        half + 0.5 * pre * (1.0 - th * th) * (GELU_A * (1.0 + 3.0 * GELU_B * sq))
    ).astype(BF)
    acc[:, pl.ds(own, d.H)] += mm(a, w[...])
    mine = lax.div(f, tiles // 2) == sc[1]

    @pl.when(mine)
    def _():
        acc[:, pl.ds(oth, d.H)] += mm(a, w1[...])

    @pl.when(jnp.logical_not(mine))
    def _():
        acc[:, pl.ds(oth, d.H)] += mm(a, w2[...])

    @pl.when(f == tiles - 1)
    def _():
        part[...] = acc[...].astype(BF)


FT = 512


def ffn_specs(d, layer, tiles):
    u = pl.BlockSpec((None, d.H, FT), lambda f: (layer, 0, f))
    up = pl.BlockSpec((d.Q, FT), lambda f: (0, f))
    w = pl.BlockSpec((None, FT, d.H), lambda f: (layer, f, 0))
    wp = pl.BlockSpec((FT, d.H), lambda f: (lax.rem(f, tiles // 2), 0))
    return u, up, w, wp


def ffn_forward(d, layer, sc, hid, pa, pb, bias, gain, shift, up_w, up_p, ub, dn_w, dn_p):
    tiles = d.F // FT
    u, up, w, wp = ffn_specs(d, layer, tiles)
    col = pl.BlockSpec((d.T, FT), lambda f: (0, f))
    row = whole((1, d.D))
    full = whole((d.T, d.D))
    return pl.pallas_call(
        functools.partial(ffn_body, d, tiles),
        grid=(tiles,),
        in_specs=[SSPEC, full, full, full, row, row, row, u, up, up,
                  pl.BlockSpec((1, FT), lambda f: (0, f)), w, wp, wp],
        out_specs=[full, full, whole((d.T, d.H)), col, col, full],
        out_shape=[sds((d.T, d.D), F32), sds((d.T, d.D), BF), sds((d.T, d.H), BF),
                   sds((d.T, d.F), BF), sds((d.T, d.F), BF), sds((d.T, d.D), BF)],
        scratch_shapes=[pltpu.VMEM((d.T, d.D), F32)],
        compiler_params=pltpu.CompilerParams(vmem_limit_bytes=VLIM),
        cost_estimate=cost(4 * d.T * d.D * d.F, 14e6),
        name="ffn_forward",
    )(sc, hid, pa, pb, bias, gain, shift, up_w, *up_p, ub, dn_w, *dn_p)


def ffn_back_body(d, tiles, sc, grad, dg, u, u1, u2, w, w1, w2,
                  db, dbs, dpre, usum, bsum, part, acc, dact):
    f = pl.program_id(0)
    own, oth, p1, p2 = offs(sc, d)

    @pl.when(f == 0)
    def _():
        db[...] = grad[...].astype(BF)
        dbs[...] = db[:, pl.ds(oth, d.H)]
        bsum[...] = jnp.sum(db[...].astype(F32), axis=0, keepdims=True)
        acc[...] = jnp.zeros_like(acc)

    mine = lax.div(f, tiles // 2) == sc[1]

    @pl.when(mine)
    def _():
        dact[...] = mm(db[:, pl.ds(oth, d.H)], w1[...], NT)

    @pl.when(jnp.logical_not(mine))
    def _():
        dact[...] = mm(db[:, pl.ds(oth, d.H)], w2[...], NT)

    da = dact[...] + mm(db[:, pl.ds(own, d.H)], w[...], NT)
    dp = (da * dg[...].astype(F32)).astype(BF)
    dpre[...] = dp
    usum[...] = jnp.sum(dp.astype(F32), axis=0, keepdims=True)
    acc[:, pl.ds(own, d.H)] += mm(dp, u[...], NT)
    acc[:, pl.ds(p1, d.Q)] += mm(dp, u1[...], NT)
    acc[:, pl.ds(p2, d.Q)] += mm(dp, u2[...], NT)

    @pl.when(f == tiles - 1)
    def _():
        part[...] = acc[...].astype(BF)


def ffn_backward(d, layer, sc, grad, dg, up_w, up_p, dn_w, dn_p):
    tiles = d.F // FT
    u, up, w, wp = ffn_specs(d, layer, tiles)
    col = pl.BlockSpec((d.T, FT), lambda f: (0, f))
    full = whole((d.T, d.D))
    return pl.pallas_call(
        functools.partial(ffn_back_body, d, tiles),
        grid=(tiles,),
        in_specs=[SSPEC, full, col, u, up, up, w, wp, wp],
        out_specs=[full, whole((d.T, d.H)), col, pl.BlockSpec((1, FT), lambda f: (0, f)),
                   whole((1, d.D)), full],
        out_shape=[sds((d.T, d.D), BF), sds((d.T, d.H), BF), sds((d.T, d.F), BF),
                   sds((1, d.F), F32), sds((1, d.D), F32), sds((d.T, d.D), BF)],
        scratch_shapes=[pltpu.VMEM((d.T, d.D), F32), pltpu.VMEM((d.T, FT), F32)],
        compiler_params=pltpu.CompilerParams(vmem_limit_bytes=VLIM),
        cost_estimate=cost(4 * d.T * d.D * d.F, 14e6),
        name="ffn_backward",
    )(sc, grad, dg, up_w, *up_p, dn_w, *dn_p)


def context_back_body(d, *refs):
    sc, grad, pa, pb, mid, gain, w, w1, w2 = refs[:9]
    dmid, da, das, gsum, ssum, asum = refs[9:15]
    chunks = refs[15 : 15 + d.C]
    dctx = refs[15 + d.C]
    own, oth, _, _ = offs(sc, d)
    back, g, s = norm_back(pa[...].astype(F32) + pb[...].astype(F32), mid[...], gain[...])
    gsum[...] = g
    ssum[...] = s
    total = grad[...].astype(F32) + back
    dmid[...] = total
    da[...] = total.astype(BF)
    das[...] = da[:, pl.ds(oth, d.H)]
    asum[...] = jnp.sum(da[...].astype(F32), axis=0, keepdims=True)
    half = d.W // 2
    k1 = pl.multiple_of(sc[1] * half, half)
    k2 = pl.multiple_of((1 - sc[1]) * half, half)
    dctx[...] = mm(da[:, pl.ds(own, d.H)], w[...], NT)
    dctx[:, pl.ds(k1, half)] += mm(da[:, pl.ds(oth, d.H)], w1[...], NT)
    dctx[:, pl.ds(k2, half)] += mm(da[:, pl.ds(oth, d.H)], w2[...], NT)
    c = sc[2]
    for o in range(d.C):
        to = lax.rem(c + o, d.C)
        col = pl.multiple_of(lax.div(to, d.g) * HEAD_DIM, HEAD_DIM)
        row = pl.multiple_of(lax.rem(to, d.g) * d.rq, d.rq)
        chunks[o][...] = dctx[pl.ds(row, d.rq), pl.ds(col, HEAD_DIM)].astype(BF)


def context_backward(d, layer, sc, grad, pa, pb, mid, gain, w, pieces):
    wspec = pl.BlockSpec((None, d.W, d.H), lambda i: (layer, 0, 0))
    outs = [sds((d.T, d.D), F32), sds((d.T, d.D), BF), sds((d.T, d.H), BF)]
    outs += [sds((1, d.D), F32)] * 3 + [sds((d.rq, HEAD_DIM), BF)] * d.C
    return pl.pallas_call(
        functools.partial(context_back_body, d),
        grid=(1,),
        in_specs=[SSPEC] + [whole(a.shape) for a in (grad, pa, pb, mid, gain)]
        + [wspec] + [whole(a.shape) for a in pieces],
        out_specs=[whole(o.shape) for o in outs],
        out_shape=outs,
        scratch_shapes=[pltpu.VMEM((d.T, d.W), F32)],
        compiler_params=pltpu.CompilerParams(vmem_limit_bytes=VLIM),
        cost_estimate=cost(2 * d.T * d.D * d.W, 6e6),
        name="context_backward",
    )(sc, grad, pa, pb, mid, gain, w, *pieces)


def attend_back_body(d, *refs):
    sc, kb = refs[:2]
    chunks = refs[2 : 2 + d.C]
    dchunks = refs[2 + d.C : 2 + 2 * d.C]
    outs = refs[2 + 2 * d.C : 2 + 3 * d.C]
    qs, ks, vs, cs, dqs, dks, dvs = refs[2 + 3 * d.C :]
    load_chunks(d, sc, chunks, qs, ks, vs)
    c = sc[2]
    for o in range(d.C):
        cs[lax.rem(c - o + d.C, d.C)] = dchunks[o][...]
    dks[...] = jnp.zeros_like(dks)
    dvs[...] = jnp.zeros_like(dvs)
    def one(s, seen):
        ext = seen * d.T
        k = ks[0:seen].reshape(ext, HEAD_DIM)
        v = vs[0:seen].reshape(ext, HEAD_DIM)
        q = qs[s]
        dc = cs[s]
        scores = score_block(d, sc, kb, q, k, s, ext)
        e = jnp.exp(scores - jnp.max(scores, axis=-1, keepdims=True))
        p = e / jnp.sum(e, axis=-1, keepdims=True)
        dp = mm(dc, v, NT)
        ds = (p * (dp - jnp.sum(p * dp, axis=-1, keepdims=True))).astype(BF)
        dqs[s] = (mm(ds, k) * SCALE).astype(BF)
        dks[0:seen] += mm(ds, q, TN).reshape(seen, d.T, HEAD_DIM)
        dvs[0:seen] += mm(p.astype(BF), dc, TN).reshape(seen, d.T, HEAD_DIM)

    each_source(d, one)
    for o in range(d.C):
        to = lax.rem(c + o, d.C)
        outs[o][0 : d.rq, :] = dqs[to]
        outs[o][d.rq : d.rq + d.T, :] = (dks[to] * SCALE).astype(BF)
        outs[o][d.rq + d.T :, :] = dvs[to].astype(BF)


def attend_backward(d, sc, kb, chunks, dchunks):
    return pl.pallas_call(
        functools.partial(attend_back_body, d),
        in_specs=[SSPEC] + [VSPEC] * (1 + 2 * d.C),
        out_specs=[VSPEC] * d.C,
        out_shape=[sds((d.chunk, HEAD_DIM), BF)] * d.C,
        scratch_shapes=[
            pltpu.VMEM((d.C, d.rq, HEAD_DIM), BF),
            pltpu.VMEM((d.C, d.T, HEAD_DIM), BF),
            pltpu.VMEM((d.C, d.T, HEAD_DIM), BF),
            pltpu.VMEM((d.C, d.rq, HEAD_DIM), BF),
            pltpu.VMEM((d.C, d.rq, HEAD_DIM), BF),
            pltpu.VMEM((d.C, d.T, HEAD_DIM), F32),
            pltpu.VMEM((d.C, d.T, HEAD_DIM), F32),
        ],
        compiler_params=pltpu.CompilerParams(vmem_limit_bytes=VLIM),
        cost_estimate=cost(5 * d.C * d.rq * d.C * d.T * HEAD_DIM * 2, 4e6),
        name="attend_backward",
    )(sc, kb, *chunks, *dchunks)


def qkv_back_body(d, *refs):
    sc, w, w1, w2 = refs[:4]
    chunks = refs[4 : 4 + d.C]
    dproj, qvsum, part, dk, dv = refs[4 + d.C :]
    c = sc[2]
    dk[...] = jnp.zeros_like(dk)
    dv[...] = jnp.zeros_like(dv)
    for o in range(d.C):
        src = lax.rem(c - o + d.C, d.C)
        col = pl.multiple_of(lax.div(src, d.g) * HEAD_DIM, HEAD_DIM)
        row = pl.multiple_of(lax.rem(src, d.g) * d.rq, d.rq)
        dproj[0, pl.ds(row, d.rq), pl.ds(col, HEAD_DIM)] = chunks[o][0 : d.rq, :]
        dk[:, pl.ds(col, HEAD_DIM)] += chunks[o][d.rq : d.rq + d.T, :].astype(F32)
        dv[:, pl.ds(col, HEAD_DIM)] += chunks[o][d.rq + d.T :, :].astype(F32)
    dproj[1] = dk[...].astype(BF)
    dproj[2] = dv[...].astype(BF)
    qvsum[0:1, :] = jnp.sum(dproj[0].astype(F32), axis=0, keepdims=True)
    qvsum[1:2, :] = jnp.sum(dproj[2].astype(F32), axis=0, keepdims=True)
    own, _, p1, p2 = offs(sc, d)
    for ref, at, width in ((w, own, d.H), (w1, p1, d.Q), (w2, p2, d.Q)):
        total = mm(dproj[0], ref[0], NT)
        total = total + mm(dproj[1], ref[1], NT)
        total = total + mm(dproj[2], ref[2], NT)
        part[:, pl.ds(at, width)] = total.astype(BF)


def qkv_backward(d, layer, sc, w, pieces, chunks):
    wspec = pl.BlockSpec((None, 3, d.H, d.W), lambda i: (layer, 0, 0, 0))
    outs = [sds((3, d.T, d.W), BF), sds((2, d.W), F32), sds((d.T, d.D), BF)]
    return pl.pallas_call(
        functools.partial(qkv_back_body, d),
        grid=(1,),
        in_specs=[SSPEC, wspec] + [whole(a.shape) for a in (*pieces, *chunks)],
        out_specs=[whole(o.shape) for o in outs],
        out_shape=outs,
        scratch_shapes=[pltpu.VMEM((d.T, d.W), F32)] * 2,
        compiler_params=pltpu.CompilerParams(vmem_limit_bytes=VLIM),
        cost_estimate=cost(2 * d.T * d.D * 3 * d.W, 7e6),
        name="qkv_backward",
    )(sc, w, *pieces, *chunks)


def input_back_body(dmid, pa, pb, hid, gain, grad, gsum, ssum):
    back, g, s = norm_back(pa[...].astype(F32) + pb[...].astype(F32), hid[...], gain[...])
    grad[...] = dmid[...] + back
    gsum[...] = g
    ssum[...] = s


def input_backward(d, dmid, pa, pb, hid, gain):
    return pl.pallas_call(
        input_back_body,
        in_specs=[VSPEC] * 5,
        out_specs=[VSPEC] * 3,
        out_shape=[sds((d.T, d.D), F32)] + [sds((1, d.D), F32)] * 2,
        compiler_params=pltpu.CompilerParams(vmem_limit_bytes=VLIM),
        cost_estimate=cost(3e6, 5e6),
        name="input_backward",
    )(dmid, pa, pb, hid, gain)


def reverse_bits(value, bits):
    out = 0
    for k in range(bits):
        bit = lax.rem(lax.div(value, 1 << k), 2)
        out = out + bit * (1 << (bits - 1 - k))
    return out


def wgrad_body(d, kind, nm, rows, cols, sc, a, a2, b, b2, keep, send):
    x = sc[0]
    c = sc[2]
    own = pl.multiple_of(x * d.H, d.H)
    rb = rows // d.C
    tile = min(512, rows)
    for m in range(nm):
        for r0 in range(0, rows, tile):
            for c0 in range(0, cols, 512):
                if kind in ("up", "qkv"):
                    left = a[:, pl.ds(own, d.H)]
                    left2 = a2[...]
                    if kind == "up":
                        right, right2 = b[:, c0 : c0 + 512], b2[:, c0 : c0 + 512]
                    else:
                        right, right2 = b[m], b2[m]
                else:
                    left, left2 = a[:, r0 : r0 + tile], a2[:, r0 : r0 + tile]
                    right, right2 = b[:, pl.ds(own, d.H)], b2[...]
                total = (mm(left, right, TN) + mm(left2, right2, TN)).astype(BF)
                for k in range(tile // rb):
                    block = r0 // rb + k
                    spot = reverse_bits(lax.bitwise_xor(c, block), d.bits)
                    piece = total[k * rb : (k + 1) * rb, :]

                    @pl.when(spot < d.C // 2)
                    def _():
                        keep[spot, m, :, c0 : c0 + 512] = piece

                    @pl.when(spot >= d.C // 2)
                    def _():
                        send[spot - d.C // 2, m, :, c0 : c0 + 512] = piece


def weight_grad(d, kind, sc, a, a2, b, b2):
    nm = 3 if kind == "qkv" else 1
    rows = a.shape[1] if kind in ("down", "out") else d.H
    cols = d.H if kind in ("down", "out") else b.shape[-1]
    shape = (d.C // 2, nm, rows // d.C, cols)
    return pl.pallas_call(
        functools.partial(wgrad_body, d, kind, nm, rows, cols),
        in_specs=[SSPEC] + [VSPEC] * 4,
        out_specs=[VSPEC] * 2,
        out_shape=[sds(shape, BF)] * 2,
        compiler_params=pltpu.CompilerParams(vmem_limit_bytes=VLIM),
        cost_estimate=cost(4 * d.T * nm * rows * cols, 8e6),
        name="weight_grad_" + kind,
    )(sc, a, a2, b, b2)


def place_body(levels, table, *refs):
    outs = refs[-1]
    ins = refs[: levels + 1]
    r = table[pl.program_id(0)]
    for k in range(levels + 1):
        low = 0 if k == 0 else 1 << (k - 1)
        high = 1 << k

        @pl.when(jnp.logical_and(r >= low, r < high))
        def _():
            outs[...] = ins[k][0].astype(F32)


def place(d, layer, table, parts, before, name):
    _, nm, rb, cols = parts[0].shape
    rows = rb * d.C

    def spec(k):
        low = 0 if k == 0 else 1 << (k - 1)
        count = 1 if k == 0 else 1 << (k - 1)
        return pl.BlockSpec(
            (1, nm, rb, cols), lambda b, t: (jnp.clip(t[b] - low, 0, count - 1), 0, 0, 0)
        )

    in_specs = [spec(k) for k in range(d.bits + 1)]
    extra = ()
    alias = {}
    if before is not None:
        in_specs.append(pl.BlockSpec(memory_space=pl.ANY))
        extra = (before,)
        alias = {d.bits + 2: 0}
    return pl.pallas_call(
        functools.partial(place_body, d.bits),
        grid_spec=pltpu.PrefetchScalarGridSpec(
            num_scalar_prefetch=1,
            grid=(d.C,),
            in_specs=in_specs,
            out_specs=pl.BlockSpec((None, nm, rb, cols), lambda b, t: (layer, 0, b, 0)),
        ),
        out_shape=sds((LAYERS, nm, rows, cols), F32),
        input_output_aliases=alias,
        compiler_params=pltpu.CompilerParams(vmem_limit_bytes=VLIM),
        cost_estimate=cost(1e6, 12e6),
        name="place_" + name,
    )(table, *parts, *extra)


def swap(values, axis):
    return lax.ppermute(values, axis, [(0, 1), (1, 0)])


def cross(values, bit, size):
    return lax.ppermute(values, "ctx", [(i, i ^ (1 << bit)) for i in range(size)])


def total_over_ctx(d, keep, send):
    for bit in range(d.bits):
        got = cross(send, bit, d.C)
        half = keep.shape[0] // 2
        if half == 0:
            keep = (keep.astype(F32) + got.astype(F32)).astype(BF)
            break
        send = (keep[half:].astype(F32) + got[half:].astype(F32)).astype(BF)
        keep = (keep[:half].astype(F32) + got[:half].astype(F32)).astype(BF)
    parts = [keep]
    for bit in reversed(range(d.bits)):
        full = parts[0] if len(parts) == 1 else jnp.concatenate(parts, axis=0)
        parts.append(cross(full, bit, d.C))
    return parts


def shift_chunks(d, chunks):
    out = [chunks[0]]
    for o in range(1, d.C):
        out.append(lax.ppermute(chunks[o], "ctx", [(i, (i + o) % d.C) for i in range(d.C)]))
    return out


def key_table(d, parent_ids, depth_offsets):
    segs = parent_ids.shape[0] // lax.axis_size("fsdp")
    start = lax.axis_index("fsdp") * segs
    parents = lax.dynamic_slice_in_dim(parent_ids, start, segs) - start
    depths = lax.dynamic_slice_in_dim(depth_offsets, start, segs).astype(F32)
    ids = jnp.arange(segs, dtype=jnp.int32)
    reach = jnp.maximum(
        (parents[:, None] == ids[None, :]).astype(F32), (ids[:, None] == ids[None, :]).astype(F32)
    )
    for _ in range((segs - 1).bit_length()):
        reach = jnp.minimum(jnp.dot(reach, reach), 1.0)
    head = lax.axis_index("tp") * d.lh + lax.axis_index("ctx") // d.g
    slope = jnp.exp2(-(head + 1).astype(F32))
    level = jnp.where(reach > 0.5, slope * (depths[None, :] - depths[:, None]), MASKED)
    spots = slope * jnp.arange(SEG, dtype=jnp.int32).astype(F32)
    return (level[:, :, None] + spots[None, None, :]).reshape(segs, segs * SEG)


def gather_pieces(d, shard, axis, y):
    half = shard.shape[axis] // 2
    mine = lax.dynamic_slice_in_dim(shard, y * half, half, axis)
    first = swap(mine, "fsdp")
    return (first, cross(first, 0, d.C))


def on_device(tokens, qkv_weight, out_weight, up_weight, down_weight, qv_bias, up_bias,
              norm_gains, row_biases, parent_ids, depth_offsets, cotangent):
    d = Dims(tokens, qkv_weight, up_weight)
    x = lax.axis_index("fsdp")
    c = lax.axis_index("ctx")
    t = lax.axis_index("tp")
    y = c % 2
    sc = jnp.stack([x, y, c]).astype(jnp.int32)
    table = jnp.stack([reverse_bits(lax.bitwise_xor(c, b), d.bits) for b in range(d.C)])
    table = table.astype(jnp.int32)
    w_qkv = qkv_weight.transpose(0, 2, 1, 3)
    pieces = []
    for layer in range(LAYERS):
        pieces.append((
            gather_pieces(d, w_qkv[layer], 1, y),
            gather_pieces(d, out_weight[layer], 0, y),
            gather_pieces(d, up_weight[layer], 0, y),
            gather_pieces(d, down_weight[layer], 0, y),
        ))
    kb = key_table(d, parent_ids, depth_offsets)

    def both(rows):
        got = swap(rows, "tp")
        return jnp.where(
            t == 0,
            jnp.concatenate([rows, got], axis=0),
            jnp.concatenate([got, rows], axis=0),
        )

    def row(values):
        return values.reshape(1, -1)

    state = both(tokens)
    saved = []
    for layer in range(LAYERS):
        p_qkv, p_out, p_up, p_down = pieces[layer]
        res = qkv_forward(d, layer, sc, state, row(norm_gains[layer, 0]),
                          row(row_biases[layer, 0]), w_qkv, p_qkv, qv_bias[layer])
        hidden, normed, normed_s = res[:3]
        chunks = shift_chunks(d, res[3:])
        outs = shift_chunks(d, attend_forward(d, sc, kb, chunks))
        ctx, part = out_forward(d, layer, sc, out_weight, p_out, outs)
        middle, n2, n2_s, act, dg, part2 = ffn_forward(
            d, layer, sc, hidden, part, swap(part, "tp"), row(row_biases[layer, 1]),
            row(norm_gains[layer, 1]), row(row_biases[layer, 2]), up_weight, p_up,
            row(up_bias[layer]), down_weight, p_down)
        state = (middle, part2, swap(part2, "tp"), row(row_biases[layer, 3]))
        saved.append((hidden, normed, normed_s, chunks, ctx, middle, n2, n2_s, act, dg))
    own_rows = tokens.shape[0]

    def mine(values):
        return lax.dynamic_slice_in_dim(values, t * own_rows, own_rows, 0)

    output = mine(state[0]) + (
        (mine(state[1]).astype(F32) + mine(state[2]).astype(F32)) + state[3]
    )
    output = output.astype(BF)
    grad = both(cotangent)
    sums = [None] * LAYERS
    grads = [None] * 4
    for layer in reversed(range(LAYERS)):
        p_qkv, p_out, p_up, p_down = pieces[layer]
        hidden, normed, normed_s, chunks, ctx, middle, n2, n2_s, act, dg = saved[layer]
        db, db_s, dpre, usum, bsum, part = ffn_backward(
            d, layer, sc, grad, dg, up_weight, p_up, down_weight, p_down)
        other = swap(part, "tp")
        res = context_backward(d, layer, sc, grad, part, other, middle,
                               row(norm_gains[layer, 1]), out_weight, p_out)
        dmid, da, da_s, gsum2, ssum2, asum = res[:6]
        dchunks = shift_chunks(d, res[6:])
        dparts = shift_chunks(d, attend_backward(d, sc, kb, chunks, dchunks))
        dproj, qvsum, part = qkv_backward(d, layer, sc, w_qkv, p_qkv, dparts)
        other = swap(part, "tp")
        grad, gsum1, ssum1 = input_backward(d, dmid, part, other, hidden,
                                            row(norm_gains[layer, 0]))
        jobs = (
            ("qkv", normed, normed_s, dproj, dproj, 0),
            ("out", ctx, ctx, da, da_s, 1),
            ("up", n2, n2_s, dpre, dpre, 2),
            ("down", act, act, db, db_s, 3),
        )
        for kind, a, a_s, b, b_s, slot in reversed(jobs):
            keep, send = weight_grad(d, kind, sc, a, swap(a_s, "fsdp"), b, swap(b_s, "fsdp"))
            parts = total_over_ctx(d, keep, send)
            grads[slot] = place(d, layer, table, parts, grads[slot], kind)
        sums[layer] = (qvsum, usum, gsum1, gsum2, ssum1, asum, ssum2, bsum)
    flat = jnp.concatenate([v.reshape(-1) for layer in sums for v in layer]).reshape(-1, 128)
    flat = flat + swap(flat, "fsdp")
    for bit in range(d.bits):
        flat = flat + cross(flat, bit, d.C)
    flat = flat.reshape(LAYERS, -1)
    n_qv, n_up = 2 * d.W, d.F
    qv_grad = flat[:, :n_qv].reshape(LAYERS, 2, d.W)
    up_grad = flat[:, n_qv : n_qv + n_up]
    rest = flat[:, n_qv + n_up :].reshape(LAYERS, 6, d.D)
    g_qkv, g_out, g_up, g_down = grads
    return (
        output,
        mine(grad),
        g_qkv.transpose(0, 2, 1, 3),
        g_out.reshape(LAYERS, d.W, d.H),
        g_up.reshape(LAYERS, d.H, d.F),
        g_down.reshape(LAYERS, d.F, d.H),
        qv_grad,
        up_grad,
        rest[:, :2],
        rest[:, 2:],
    )


def solution(mesh):
    in_specs = (
        P(("fsdp", "ctx", "tp"), None),
        P(None, "fsdp", None, "tp"),
        P(None, "tp", "fsdp"),
        P(None, "fsdp", "tp"),
        P(None, "tp", "fsdp"),
        P(None, None, "tp"),
        P(None, "tp"),
        P(),
        P(),
        P(),
        P(),
        P(("fsdp", "ctx", "tp"), None),
    )
    out_specs = (
        P(("fsdp", "ctx", "tp"), None),
        P(("fsdp", "ctx", "tp"), None),
        P(None, "fsdp", None, "tp"),
        P(None, "tp", "fsdp"),
        P(None, "fsdp", "tp"),
        P(None, "tp", "fsdp"),
        P(None, None, "tp"),
        P(None, "tp"),
        P(),
        P(),
    )
    return jax.shard_map(
        on_device, mesh=mesh, in_specs=in_specs, out_specs=out_specs, check_vma=False
    )
```

```python
import functools

import jax
import jax.numpy as jnp
from jax import lax
from jax.experimental import pallas as pl
from jax.experimental.pallas import tpu as pltpu
from jax.sharding import PartitionSpec as P

HEAD_DIM = 128
LAYERS = 2
SEG = 128
EPSILON = 1e-05
MASKED = -1e30
SCALE = HEAD_DIM ** (-0.5)
GELU_A = 0.7978845608028654
GELU_B = 0.044715
BF = jnp.bfloat16
F32 = jnp.float32
VLIM = 56 * 1024 * 1024

NN = (((1,), (0,)), ((), ()))
NT = (((1,), (1,)), ((), ()))
TN = (((0,), (0,)), ((), ()))


def mm(a, b, dims=NN):
    return lax.dot_general(a, b, dims, preferred_element_type=F32)


def sds(shape, dtype):
    return jax.ShapeDtypeStruct(shape, dtype)


VSPEC = pl.BlockSpec(memory_space=pltpu.VMEM)
SSPEC = pl.BlockSpec(memory_space=pltpu.SMEM)


def cost(flops, nbytes):
    return pl.CostEstimate(flops=int(flops), bytes_accessed=int(nbytes), transcendentals=0)


def kernel_call(body, args, in_specs, out_specs, out_shape, name, scratch=(), grid=None,
                deps=(), work=None, aliases=None):
    count, extra = len(args), len(deps)

    def ordered(*refs):
        body(*refs[:count], *refs[count + extra :])

    kwargs = {} if grid is None else {"grid": grid}
    return pl.pallas_call(
        ordered,
        in_specs=list(in_specs) + [pl.BlockSpec(memory_space=pl.ANY)] * extra,
        out_specs=out_specs,
        out_shape=out_shape,
        scratch_shapes=list(scratch),
        input_output_aliases=aliases or {},
        compiler_params=pltpu.CompilerParams(vmem_limit_bytes=VLIM),
        cost_estimate=work,
        name=name,
        **kwargs,
    )(*args, *deps)


def norm_rows(v):
    centered = v - jnp.mean(v, axis=-1, keepdims=True)
    rstd = lax.rsqrt(jnp.mean(centered * centered, axis=-1, keepdims=True) + EPSILON)
    return centered * rstd, rstd


def norm_back(d, v, gain):
    xhat, rstd = norm_rows(v)
    dx = d * gain
    back = rstd * (
        dx
        - jnp.mean(dx, axis=-1, keepdims=True)
        - xhat * jnp.mean(dx * xhat, axis=-1, keepdims=True)
    )
    d_gain = jnp.sum(d * xhat, axis=0, keepdims=True)
    d_shift = jnp.sum(d, axis=0, keepdims=True)
    return back, d_gain, d_shift


class Dims:
    def __init__(self, tokens, qkv_weight, up_weight):
        self.tp = lax.axis_size("tp")
        self.C = lax.axis_size("ctx")
        self.T = tokens.shape[0] * self.tp
        self.D = tokens.shape[1]
        self.H = self.D // lax.axis_size("fsdp")
        self.Q = self.H // 2
        self.W = qkv_weight.shape[3]
        self.F = up_weight.shape[2]
        self.lh = self.W // HEAD_DIM
        self.g = self.C // self.lh
        self.rq = self.T // self.g
        self.chunk = self.rq + 2 * self.T
        self.bits = self.C.bit_length() - 1


def offs(sc, d):
    x = sc[0]
    y = sc[1]
    own = pl.multiple_of(x * d.H, d.H)
    oth = pl.multiple_of((1 - x) * d.H, d.H)
    first = pl.multiple_of((1 - x) * d.H + y * d.Q, d.Q)
    second = pl.multiple_of((1 - x) * d.H + (1 - y) * d.Q, d.Q)
    return own, oth, first, second


def spot_of(d, chip):
    row, head = (chip % d.g) * d.rq, (chip // d.g) * HEAD_DIM
    return slice(row, row + d.rq), slice(head, head + HEAD_DIM)


def qkv_body(d, first, *refs):
    if first:
        sc, hid, gain, shift, w, w1, w2, qvb = refs[:8]
        rest = refs[8:]
        hidden = hid[...].astype(F32)
    else:
        sc, mid, pa, pb, bias, gain, shift, w, w1, w2, qvb = refs[:11]
        rest = refs[11:]
        hidden = mid[...] + ((pa[...].astype(F32) + pb[...].astype(F32)) + bias[...])
    h_out, no_out, ns_out, chunks, n_out, scr = rest
    own, oth, p1, p2 = offs(sc, d)
    h_out[...] = hidden
    xhat, _ = norm_rows(hidden)
    n_out[...] = (xhat * gain[...] + shift[...]).astype(BF)
    ns_out[...] = n_out[:, pl.ds(oth, d.H)]
    a0 = n_out[:, pl.ds(own, d.H)]
    no_out[...] = a0
    a1 = n_out[:, pl.ds(p1, d.Q)]
    a2 = n_out[:, pl.ds(p2, d.Q)]
    for n in range(3):
        proj = mm(a0, w[n]) + mm(a1, w1[n]) + mm(a2, w2[n])
        if n == 0:
            proj = proj + qvb[0:1, :]
        if n == 2:
            proj = proj + qvb[1:2, :]
        scr[n] = proj.astype(BF)
    for to in range(d.C):
        row, col = spot_of(d, to)
        chunks[to, 0 : d.rq, :] = scr[0, row, col]
        chunks[to, d.rq : d.rq + d.T, :] = scr[1, :, col]
        chunks[to, d.rq + d.T :, :] = scr[2, :, col]


def whole(shape):
    return pl.BlockSpec(shape, lambda *_: (0,) * len(shape))


def piece_specs(shape, pieces, axis):
    if pieces[0] is not pieces[1]:
        return [whole(shape), whole(shape)]
    second = tuple(1 if k == axis else 0 for k in range(len(shape)))
    return [whole(shape), pl.BlockSpec(shape, lambda *_: second)]


def qkv_forward(d, layer, sc, hid, gain, shift, w, pieces, qvb, deps=()):
    first = not isinstance(hid, tuple)
    hid = (hid,) if first else hid
    wspec = pl.BlockSpec((None, 3, d.H, d.W), lambda i: (layer, 0, 0, 0))
    in_specs = [SSPEC] + [whole(a.shape) for a in hid]
    in_specs += [whole(gain.shape), whole(shift.shape), wspec]
    in_specs += piece_specs((3, d.Q, d.W), pieces, 1) + [whole(qvb.shape)]
    outs = [sds((d.T, d.D), F32), sds((d.T, d.H), BF), sds((d.T, d.H), BF)]
    outs += [sds((d.C, d.chunk, HEAD_DIM), BF)]
    return kernel_call(
        functools.partial(qkv_body, d, first),
        (sc, *hid, gain, shift, w, *pieces, qvb,),
        grid=(1,),
        in_specs=in_specs,
        out_specs=[whole(o.shape) for o in outs],
        out_shape=outs,
        scratch=[pltpu.VMEM((d.T, d.D), BF), pltpu.VMEM((3, d.T, d.W), BF)],
        work=cost(2 * d.T * d.D * 3 * d.W, 8e6),
        name="qkv_forward",
        deps=deps,
    )


def load_chunks(d, sc, chunks, qs, ks, vs):
    qs[...] = chunks[:, 0 : d.rq, :]
    ks[...] = chunks[:, d.rq : d.rq + d.T, :]
    vs[...] = chunks[:, d.rq + d.T :, :]


def score_block(d, sc, kb, q, k, s, ext):
    part = lax.rem(sc[2], d.g)
    seg = s * (d.T // SEG) + lax.div(part * d.rq, SEG)
    scores = mm(q, k, NT) * SCALE + kb[pl.ds(seg, 1), 0:ext]
    col = lax.broadcasted_iota(jnp.int32, (d.rq, ext), 1) - s * d.T
    row = lax.broadcasted_iota(jnp.int32, (d.rq, ext), 0) + part * d.rq
    return jnp.where(col <= row, scores, MASKED)


UNROLL = 8
SHIFT = 3


def each_source(d, one):
    if d.C <= UNROLL:
        for s in range(d.C):
            one(s, s + 1)
    else:
        lax.fori_loop(0, d.C, lambda s, carry: (one(s, d.C), carry)[1], 0)


def attend_body(d, *refs):
    sc, kb, chunks, cs, qs, ks, vs = refs
    load_chunks(d, sc, chunks, qs, ks, vs)
    def one(s, seen):
        ext = seen * d.T
        k = ks[0:seen].reshape(ext, HEAD_DIM)
        v = vs[0:seen].reshape(ext, HEAD_DIM)
        scores = score_block(d, sc, kb, qs[s], k, s, ext)
        e = jnp.exp(scores - jnp.max(scores, axis=-1, keepdims=True))
        total = jnp.sum(e, axis=-1, keepdims=True)
        cs[s] = (mm(e.astype(BF), v) / total).astype(BF)

    each_source(d, one)


def attend_forward(d, sc, kb, chunks, deps=()):
    return kernel_call(
        functools.partial(attend_body, d),
        (sc, kb, chunks,),
        in_specs=[SSPEC] + [VSPEC] * 2,
        out_specs=VSPEC,
        out_shape=sds((d.C, d.rq, HEAD_DIM), BF),
        scratch=[
            pltpu.VMEM((d.C, d.rq, HEAD_DIM), BF),
            pltpu.VMEM((d.C, d.T, HEAD_DIM), BF),
            pltpu.VMEM((d.C, d.T, HEAD_DIM), BF),
        ],
        work=cost(2 * d.C * d.rq * d.C * d.T * HEAD_DIM * 2, 3e6),
        name="attend_forward",
        deps=deps,
    )


def out_body(d, *refs):
    sc, w, w1, w2, chunks, ctx, part = refs
    for src in range(d.C):
        ctx[spot_of(d, src)] = chunks[src]
    own, oth, _, _ = offs(sc, d)
    half = d.W // 2
    k1 = pl.multiple_of(sc[1] * half, half)
    k2 = pl.multiple_of((1 - sc[1]) * half, half)
    part[:, pl.ds(own, d.H)] = mm(ctx[...], w[...]).astype(BF)
    part[:, pl.ds(oth, d.H)] = (
        mm(ctx[:, pl.ds(k1, half)], w1[...]) + mm(ctx[:, pl.ds(k2, half)], w2[...])
    ).astype(BF)


def out_forward(d, layer, sc, w, pieces, chunks, deps=()):
    wspec = pl.BlockSpec((None, d.W, d.H), lambda i: (layer, 0, 0))
    outs = [sds((d.T, d.W), BF), sds((d.T, d.D), BF)]
    return kernel_call(
        functools.partial(out_body, d),
        (sc, w, *pieces, chunks,),
        grid=(1,),
        in_specs=[SSPEC, wspec] + piece_specs((d.W // 2, d.H), pieces, 0)
        + [whole(chunks.shape)],
        out_specs=[whole(o.shape) for o in outs],
        out_shape=outs,
        work=cost(2 * d.T * d.D * d.W, 3e6),
        name="out_forward",
        deps=deps,
    )


FT = 512


def tile_of(f, sc, tiles, refs, use):
    half = tiles // 2
    mine = lax.rem(f, half) == sc[1]
    for number, (came, then) in enumerate((refs[:2], refs[2:])):
        here = lax.div(f, half) == number

        @pl.when(jnp.logical_and(here, mine))
        def _():
            use(came)

        @pl.when(jnp.logical_and(here, jnp.logical_not(mine)))
        def _():
            use(then)


def ffn_body(d, tiles, sc, hid, pa, pb, bias, gain, shift,
             u, u1, u2, u3, u4, ub, w, w1, w2, w3, w4,
             mid, no, act_p, act_q, dg, part, n2, acc, pre):
    f = pl.program_id(0)
    own, oth, _, _ = offs(sc, d)

    @pl.when(f == 0)
    def _():
        m = hid[...] + ((pa[...].astype(F32) + pb[...].astype(F32)) + bias[...])
        mid[...] = m
        xhat, _ = norm_rows(m)
        n2[...] = (xhat * gain[...] + shift[...]).astype(BF)
        no[...] = n2[:, pl.ds(own, d.H)]
        act_p[0] = n2[:, pl.ds(oth, d.H)]
        acc[...] = jnp.zeros_like(acc)

    def up(ref):
        pre[...] = mm(act_p[0], ref[...])

    tile_of(f, sc, tiles, (u1, u2, u3, u4), up)
    v = pre[...] + mm(no[...], u[...]) + ub[...]
    sq = v * v
    th = jnp.tanh(GELU_A * v * (1.0 + GELU_B * sq))
    half = 0.5 * (1.0 + th)
    a = (v * half).astype(BF)

    @pl.when(f < tiles // 2)
    def _():
        act_p[1 + f] = a

    @pl.when(f >= tiles // 2)
    def _():
        act_q[f - tiles // 2] = a

    dg[...] = (
        half + 0.5 * v * (1.0 - th * th) * (GELU_A * (1.0 + 3.0 * GELU_B * sq))
    ).astype(BF)
    acc[0] += mm(a, w[...])

    def down(ref):
        acc[1] += mm(a, ref[...])

    tile_of(f, sc, tiles, (w1, w2, w3, w4), down)

    @pl.when(f == tiles - 1)
    def _():
        part[:, pl.ds(own, d.H)] = acc[0].astype(BF)
        part[:, pl.ds(oth, d.H)] = acc[1].astype(BF)


def ffn_specs(d, layer):
    u = pl.BlockSpec((None, d.H, FT), lambda f: (layer, 0, f))
    w = pl.BlockSpec((None, FT, d.H), lambda f: (layer, f, 0))
    tile = whole((d.H, FT))
    low = pl.BlockSpec((None, FT, d.H), lambda f: (0, 0, 0))
    high = pl.BlockSpec((None, FT, d.H), lambda f: (1, 0, 0))
    return [u] + [tile] * 4, [w, low, low, high, high]


def ffn_forward(d, layer, sc, hid, pa, pb, bias, gain, shift,
                up_w, up_p, ub, dn_w, dn_p, deps=()):
    tiles = d.F // FT
    us, ws = ffn_specs(d, layer)
    side = whole((d.T, d.H))
    col = pl.BlockSpec((d.T, FT), lambda f: (0, f))
    row = whole((1, d.D))
    full = whole((d.T, d.D))
    act_p = sds((1 + tiles // 2, d.T, FT), BF)
    act_q = sds((tiles // 2, d.T, FT), BF)
    return kernel_call(
        functools.partial(ffn_body, d, tiles),
        (sc, hid, pa, pb, bias, gain, shift, up_w, *up_p, ub, dn_w, *dn_p),
        [SSPEC, full, full, full, row, row, row, *us,
         pl.BlockSpec((1, FT), lambda f: (0, f)), *ws],
        [full, side, whole(act_p.shape), whole(act_q.shape), col, full],
        [sds((d.T, d.D), F32), sds((d.T, d.H), BF), act_p, act_q,
         sds((d.T, d.F), BF), sds((d.T, d.D), BF)],
        "ffn_forward",
        scratch=[pltpu.VMEM((d.T, d.D), BF), pltpu.VMEM((2, d.T, d.H), F32),
                 pltpu.VMEM((d.T, FT), F32)],
        grid=(tiles,), deps=deps, work=cost(4 * d.T * d.D * d.F, 14e6))


def ffn_back_body(d, tiles, sc, grad, dg, u, u1, u2, u3, u4, w, w1, w2, w3, w4,
                  dbo, xba, xbb, usum, bsum, part, acc, dact):
    f = pl.program_id(0)
    own, oth, _, _ = offs(sc, d)

    @pl.when(f == 0)
    def _():
        dbo[...] = grad[:, pl.ds(own, d.H)].astype(BF)
        xba[0] = grad[:, pl.ds(oth, d.H)].astype(BF)
        bsum[...] = jnp.sum(grad[...].astype(BF).astype(F32), axis=0, keepdims=True)
        acc[...] = jnp.zeros_like(acc)

    def down(ref):
        dact[...] = mm(xba[0], ref[...], NT)

    tile_of(f, sc, tiles, (w1, w2, w3, w4), down)
    da = dact[...] + mm(dbo[...], w[...], NT)
    dp = (da * dg[...].astype(F32)).astype(BF)

    @pl.when(f == 0)
    def _():
        xba[1] = dp

    @pl.when(f > 0)
    def _():
        xbb[f - 1] = dp

    usum[...] = jnp.sum(dp.astype(F32), axis=0, keepdims=True)
    acc[0] += mm(dp, u[...], NT)

    def up(ref):
        acc[1] += mm(dp, ref[...], NT)

    tile_of(f, sc, tiles, (u1, u2, u3, u4), up)

    @pl.when(f == tiles - 1)
    def _():
        part[:, pl.ds(own, d.H)] = acc[0].astype(BF)
        part[:, pl.ds(oth, d.H)] = acc[1].astype(BF)


def ffn_backward(d, layer, sc, grad, dg, up_w, up_p, dn_w, dn_p, deps=()):
    tiles = d.F // FT
    us, ws = ffn_specs(d, layer)
    side = whole((d.T, d.H))
    col = pl.BlockSpec((d.T, FT), lambda f: (0, f))
    full = whole((d.T, d.D))
    xba = sds((2, d.T, FT), BF)
    xbb = sds((tiles - 1, d.T, FT), BF)
    return kernel_call(
        functools.partial(ffn_back_body, d, tiles),
        (sc, grad, dg, up_w, *up_p, dn_w, *dn_p),
        [SSPEC, full, col, *us, *ws],
        [side, whole(xba.shape), whole(xbb.shape),
         pl.BlockSpec((1, FT), lambda f: (0, f)), whole((1, d.D)), full],
        [sds((d.T, d.H), BF), xba, xbb,
         sds((1, d.F), F32), sds((1, d.D), F32), sds((d.T, d.D), BF)],
        "ffn_backward",
        scratch=[pltpu.VMEM((2, d.T, d.H), F32), pltpu.VMEM((d.T, FT), F32)],
        grid=(tiles,), deps=deps, work=cost(4 * d.T * d.D * d.F, 14e6))


def context_back_body(d, *refs):
    sc, grad, pa, pb, mid, gain, w, w1, w2 = refs[:9]
    dmid, dao, das, gsum, ssum, asum, chunks, da, dctx = refs[9:]
    own, oth, _, _ = offs(sc, d)
    back, g, s = norm_back(pa[...].astype(F32) + pb[...].astype(F32), mid[...], gain[...])
    gsum[...] = g
    ssum[...] = s
    total = grad[...].astype(F32) + back
    dmid[...] = total
    da[...] = total.astype(BF)
    dao[...] = da[:, pl.ds(own, d.H)]
    das[...] = da[:, pl.ds(oth, d.H)]
    asum[...] = jnp.sum(da[...].astype(F32), axis=0, keepdims=True)
    half = d.W // 2
    k1 = pl.multiple_of(sc[1] * half, half)
    k2 = pl.multiple_of((1 - sc[1]) * half, half)
    dctx[...] = mm(da[:, pl.ds(own, d.H)], w[...], NT)
    dctx[:, pl.ds(k1, half)] += mm(da[:, pl.ds(oth, d.H)], w1[...], NT)
    dctx[:, pl.ds(k2, half)] += mm(da[:, pl.ds(oth, d.H)], w2[...], NT)
    for to in range(d.C):
        chunks[to] = dctx[spot_of(d, to)].astype(BF)


def context_backward(d, layer, sc, grad, pa, pb, mid, gain, w, pieces, deps=()):
    wspec = pl.BlockSpec((None, d.W, d.H), lambda i: (layer, 0, 0))
    outs = [sds((d.T, d.D), F32), sds((d.T, d.H), BF), sds((d.T, d.H), BF)]
    outs += [sds((1, d.D), F32)] * 3 + [sds((d.C, d.rq, HEAD_DIM), BF)]
    return kernel_call(
        functools.partial(context_back_body, d),
        (sc, grad, pa, pb, mid, gain, w, *pieces,),
        grid=(1,),
        in_specs=[SSPEC] + [whole(a.shape) for a in (grad, pa, pb, mid, gain)]
        + [wspec] + piece_specs((d.W // 2, d.H), pieces, 0),
        out_specs=[whole(o.shape) for o in outs],
        out_shape=outs,
        scratch=[pltpu.VMEM((d.T, d.D), BF), pltpu.VMEM((d.T, d.W), F32)],
        work=cost(2 * d.T * d.D * d.W, 6e6),
        name="context_backward",
        deps=deps,
    )


def attend_back_body(d, *refs):
    sc, kb, chunks, cs, outs, qs, ks, vs, dks, dvs = refs
    load_chunks(d, sc, chunks, qs, ks, vs)
    dks[...] = jnp.zeros_like(dks)
    dvs[...] = jnp.zeros_like(dvs)
    def one(s, seen):
        ext = seen * d.T
        k = ks[0:seen].reshape(ext, HEAD_DIM)
        v = vs[0:seen].reshape(ext, HEAD_DIM)
        q = qs[s]
        dc = cs[s]
        scores = score_block(d, sc, kb, q, k, s, ext)
        e = jnp.exp(scores - jnp.max(scores, axis=-1, keepdims=True))
        p = e / jnp.sum(e, axis=-1, keepdims=True)
        dp = mm(dc, v, NT)
        ds = (p * (dp - jnp.sum(p * dp, axis=-1, keepdims=True))).astype(BF)
        outs[s, 0 : d.rq, :] = (mm(ds, k) * SCALE).astype(BF)
        dks[0:seen] += mm(ds, q, TN).reshape(seen, d.T, HEAD_DIM)
        dvs[0:seen] += mm(p.astype(BF), dc, TN).reshape(seen, d.T, HEAD_DIM)

    each_source(d, one)
    outs[:, d.rq : d.rq + d.T, :] = (dks[...] * SCALE).astype(BF)
    outs[:, d.rq + d.T :, :] = dvs[...].astype(BF)


def attend_backward(d, sc, kb, chunks, dchunks, deps=()):
    return kernel_call(
        functools.partial(attend_back_body, d),
        (sc, kb, chunks, dchunks,),
        in_specs=[SSPEC] + [VSPEC] * 3,
        out_specs=VSPEC,
        out_shape=sds((d.C, d.chunk, HEAD_DIM), BF),
        scratch=[
            pltpu.VMEM((d.C, d.rq, HEAD_DIM), BF),
            pltpu.VMEM((d.C, d.T, HEAD_DIM), BF),
            pltpu.VMEM((d.C, d.T, HEAD_DIM), BF),
            pltpu.VMEM((d.C, d.T, HEAD_DIM), F32),
            pltpu.VMEM((d.C, d.T, HEAD_DIM), F32),
        ],
        work=cost(5 * d.C * d.rq * d.C * d.T * HEAD_DIM * 2, 4e6),
        name="attend_backward",
        deps=deps,
    )


def qkv_back_body(d, sc, w, w1, w2, chunks, xb, qvsum, part, dk, dv):
    dk[...] = jnp.zeros_like(dk)
    dv[...] = jnp.zeros_like(dv)
    for src in range(d.C):
        row, col = spot_of(d, src)
        xb[0, row, col] = chunks[src, 0 : d.rq, :]
        dk[:, col] += chunks[src, d.rq : d.rq + d.T, :].astype(F32)
        dv[:, col] += chunks[src, d.rq + d.T :, :].astype(F32)
    xb[1] = dk[...].astype(BF)
    xb[2] = dv[...].astype(BF)
    qvsum[0:1, :] = jnp.sum(xb[0].astype(F32), axis=0, keepdims=True)
    qvsum[1:2, :] = jnp.sum(xb[2].astype(F32), axis=0, keepdims=True)
    own, _, p1, p2 = offs(sc, d)
    for ref, at, width in ((w, own, d.H), (w1, p1, d.Q), (w2, p2, d.Q)):
        total = mm(xb[0], ref[0], NT) + mm(xb[1], ref[1], NT) + mm(xb[2], ref[2], NT)
        part[:, pl.ds(at, width)] = total.astype(BF)


def qkv_backward(d, layer, sc, w, pieces, chunks, deps=()):
    wspec = pl.BlockSpec((None, 3, d.H, d.W), lambda i: (layer, 0, 0, 0))
    outs = [sds((3, d.T, d.W), BF), sds((2, d.W), F32), sds((d.T, d.D), BF)]
    return kernel_call(
        functools.partial(qkv_back_body, d),
        (sc, w, *pieces, chunks),
        [SSPEC, wspec] + [whole((3, d.Q, d.W))] * 2 + [whole(chunks.shape)],
        [whole(o.shape) for o in outs],
        outs,
        "qkv_backward",
        scratch=[pltpu.VMEM((d.T, d.W), F32)] * 2,
        grid=(1,), deps=deps, work=cost(2 * d.T * d.D * 3 * d.W, 7e6))


def input_back_body(dmid, pa, pb, hid, gain, grad, gsum, ssum):
    back, g, s = norm_back(pa[...].astype(F32) + pb[...].astype(F32), hid[...], gain[...])
    grad[...] = dmid[...] + back
    gsum[...] = g
    ssum[...] = s


def input_backward(d, dmid, pa, pb, hid, gain, deps=()):
    return kernel_call(
        input_back_body,
        (dmid, pa, pb, hid, gain,),
        in_specs=[VSPEC] * 5,
        out_specs=[VSPEC] * 3,
        out_shape=[sds((d.T, d.D), F32)] + [sds((1, d.D), F32)] * 2,
        work=cost(3e6, 5e6),
        name="input_backward",
        deps=deps,
    )


def spot_bits(value, shifts, bits):
    out = 0
    for k in range(bits):
        bit = lax.bitwise_and(lax.shift_right_logical(value, shifts[k]), 1)
        out = out + bit * (1 << (bits - 1 - k))
    return out


def wgrad_body(d, tiles, sc, *refs):
    ins = refs[:-2]
    keep, send = refs[-2:]
    c = sc[2]
    shifts = [sc[SHIFT + k] for k in range(d.bits)]
    rb = FT // d.C
    spots = [spot_bits(lax.bitwise_xor(c, b), shifts, d.bits) for b in range(d.C)]

    def pick(item):
        ref, at = item
        return ins[ref][...] if at is None else ins[ref][at]

    for m, (a, b, a2, b2) in enumerate(tiles):
        total = mm(pick(a), pick(b), TN) + mm(pick(a2), pick(b2), TN)
        total = total.astype(BF)
        for block, spot in enumerate(spots):
            piece = total[block * rb : (block + 1) * rb, :]

            @pl.when(spot < d.C // 2)
            def _():
                keep[spot, m] = piece

            @pl.when(spot >= d.C // 2)
            def _():
                send[spot - d.C // 2, m] = piece


def wgrad_plain_body(tiles, *refs):
    ins, out = refs[:-1], refs[-1]

    def pick(item):
        ref, at = item
        return ins[ref][...] if at is None else ins[ref][at]

    for m, (a, b, a2, b2) in enumerate(tiles):
        total = mm(pick(a), pick(b), TN) + mm(pick(a2), pick(b2), TN)
        out[m] = total.astype(BF)


def weight_grad_plain(d, name, ins, tiles, deps=()):
    return kernel_call(
        functools.partial(wgrad_plain_body, tiles), ins,
        [VSPEC] * len(ins), VSPEC, sds((len(tiles), FT, FT), BF), "weight_grad_" + name,
        deps=deps, work=cost(4 * d.T * len(tiles) * FT * FT, 8e6))


def weight_grad(d, name, sc, ins, tiles, deps=()):
    shape = (d.C // 2, len(tiles), FT // d.C, FT)
    return kernel_call(
        functools.partial(wgrad_body, d, tiles),
        (sc, *ins,),
        in_specs=[SSPEC] + [VSPEC] * len(ins),
        out_specs=[VSPEC] * 2,
        out_shape=[sds(shape, BF)] * 2,
        work=cost(4 * d.T * len(tiles) * FT * FT, 8e6),
        name="weight_grad_" + name,
        deps=deps,
    )


def place_body(d, wide, count_in, extra, layer, owner, plain, sc, *refs):
    ins = refs[:count_in]
    outs = refs[count_in + extra : -2]
    buf, sems = refs[-2:]
    rb = FT // d.C
    if plain:
        buf[...] = ins[0][...].astype(F32)
    else:
        r = 0
        for part in ins:
            for n in range(part.shape[0]):
                row = pl.multiple_of(owner(sc, r) * rb, rb)
                for m in range(part.shape[1]):
                    buf[m, pl.ds(row, rb), :] = part[n, m].astype(F32)
                r += 1
    copies = []
    m = 0
    for out, (kind, count) in zip(outs, wide):
        if kind == "cols":
            for k in range(count):
                copies.append((buf.at[m + k], out.at[layer, :, pl.ds(k * FT, FT)]))
        else:
            copies.append((buf.at[pl.ds(m, count)], out.at[layer]))
        m += count
    going = [pltpu.make_async_copy(a, b, sems.at[k]) for k, (a, b) in enumerate(copies)]
    for one in going:
        one.start()
    for one in going:
        one.wait()


def place(d, layer, sc, parts, before, wide, name, deps=()):
    plain = not isinstance(parts, list)
    parts = [parts] if plain else parts
    nt = parts[0].shape[0 if plain else 1]
    extra = tuple(before or ()) + tuple(deps)
    alias = {1 + len(parts) + k: k for k in range(len(before or ()))}
    shapes = [
        sds((LAYERS, FT, n * FT) if kind == "cols" else (LAYERS, n, FT, FT), F32)
        for kind, n in wide
    ]
    moves = sum(n if kind == "cols" else 1 for kind, n in wide)

    def owner(scalars, r):
        turned = 0
        for k in range(d.bits):
            if r >> (d.bits - 1 - k) & 1:
                turned = turned + lax.shift_left(jnp.int32(1), scalars[SHIFT + k])
        return lax.bitwise_xor(scalars[2], jnp.int32(turned))

    return pl.pallas_call(
        functools.partial(place_body, d, wide, len(parts), len(extra), layer, owner, plain),
        in_specs=[SSPEC] + [VSPEC] * len(parts) + [pl.BlockSpec(memory_space=pl.ANY)] * len(extra),
        out_specs=[pl.BlockSpec(memory_space=pl.ANY)] * len(wide),
        out_shape=shapes,
        scratch_shapes=[pltpu.VMEM((nt, FT, FT), F32), pltpu.SemaphoreType.DMA((moves,))],
        input_output_aliases=alias,
        compiler_params=pltpu.CompilerParams(vmem_limit_bytes=VLIM),
        name="place_" + name,
    )(sc, *parts, *extra)


def swap(values, axis):
    return lax.ppermute(values, axis, [(0, 1), (1, 0)])


def way(d, core, step):
    if step < 2 and d.bits > 1:
        return step if core == 0 else 1 - step
    return step


def cross(d, values, step):
    pairs = []
    for i in range(d.C):
        for core in range(d.tp):
            to = i ^ (1 << way(d, core, step))
            pairs.append((i * d.tp + core, to * d.tp + core))
    return lax.ppermute(values, ("ctx", "tp"), pairs)


def cross_all(d, values, step):
    return lax.ppermute(values, "ctx", [(i, i ^ (1 << step)) for i in range(d.C)])


def take_body(sc, w, *refs):
    refs[-1][...] = w[...]


def take(sc, w, block, index, shape, steps=1, deps=()):
    out_block = shape if steps == 1 else (None, *shape[1:])
    return pl.pallas_call(
        take_body,
        grid_spec=pltpu.PrefetchScalarGridSpec(
            num_scalar_prefetch=1,
            grid=(steps,),
            in_specs=[pl.BlockSpec(block, lambda n, s: index(n, s[1]))]
            + [pl.BlockSpec(memory_space=pl.ANY)] * len(deps),
            out_specs=pl.BlockSpec(out_block, lambda n, s: (n,) + (0,) * (len(shape) - 1)),
        ),
        out_shape=sds(shape, BF),
        compiler_params=pltpu.CompilerParams(vmem_limit_bytes=VLIM),
        name="take",
    )(sc, w, *deps)


def fold_body(keep, got, *outs):
    total = (keep[...].astype(F32) + got[...].astype(F32)).astype(BF)
    if len(outs) == 1:
        outs[0][...] = total
    else:
        half = total.shape[0] // 2
        outs[0][...] = total[:half]
        outs[1][...] = total[half:]


def fold(keep, got, deps=()):
    count = keep.shape[0]
    shapes = [keep.shape] if count == 1 else [(count // 2, *keep.shape[1:])] * 2
    return kernel_call(
        fold_body, (keep, got), [VSPEC] * 2, [VSPEC] * len(shapes),
        [sds(v, BF) for v in shapes], "fold", deps=deps, work=cost(1e6, 3e6))


def join_body(*refs):
    out = refs[-1]
    at = 0
    for ref in refs[:-1]:
        out[at : at + ref.shape[0]] = ref[...]
        at += ref.shape[0]


def join(parts, deps=()):
    if len(parts) == 1:
        return parts[0]
    count = sum(p.shape[0] for p in parts)
    return kernel_call(
        join_body, tuple(parts), [VSPEC] * len(parts), VSPEC,
        sds((count, *parts[0].shape[1:]), BF), "join", deps=deps, work=cost(1e5, 3e6))


class Sum:
    def __init__(self, d, keep, send):
        self.d = d
        self.keep = keep
        self.got = cross(d, send, 0)
        self.at = 0
        self.parts = None

    def step(self, *deps):
        self.at += 1
        n = self.d.bits
        if self.at < n:
            keep, send = fold(self.keep, self.got, deps)
            self.keep = keep
            self.got = cross(self.d, send, self.at)
            return keep
        if self.at == n:
            (keep,) = fold(self.keep, self.got, deps)
            self.parts = [keep]
            self.got = cross(self.d, keep, n - 1)
            return keep
        self.parts.append(self.got)
        if self.at < 2 * n:
            full = join(self.parts, deps)
            self.got = cross(self.d, full, 2 * n - 1 - self.at)
            return full
        return self.got

    def finish(self):
        while self.at < 2 * self.d.bits:
            self.step()
        return self.parts


def all_to_all(values):
    return lax.all_to_all(values, "ctx", 0, 0)


def key_table(d, parent_ids, depth_offsets):
    segs = parent_ids.shape[0] // lax.axis_size("fsdp")
    start = lax.axis_index("fsdp") * segs
    parents = lax.dynamic_slice_in_dim(parent_ids, start, segs) - start
    depths = lax.dynamic_slice_in_dim(depth_offsets, start, segs).astype(F32)
    ids = jnp.arange(segs, dtype=jnp.int32)
    reach = jnp.maximum(
        (parents[:, None] == ids[None, :]).astype(F32), (ids[:, None] == ids[None, :]).astype(F32)
    )
    for _ in range((segs - 1).bit_length()):
        reach = jnp.minimum(jnp.dot(reach, reach), 1.0)
    head = lax.axis_index("tp") * d.lh + lax.axis_index("ctx") // d.g
    slope = jnp.exp2(-(head + 1).astype(F32))
    level = jnp.where(reach > 0.5, slope * (depths[None, :] - depths[:, None]), MASKED)
    spots = slope * jnp.arange(SEG, dtype=jnp.int32).astype(F32)
    return (level[:, :, None] + spots[None, None, :]).reshape(segs, segs * SEG)


def on_device(tokens, qkv_weight, out_weight, up_weight, down_weight, qv_bias, up_bias,
              norm_gains, row_biases, parent_ids, depth_offsets, cotangent):
    d = Dims(tokens, qkv_weight, up_weight)
    x = lax.axis_index("fsdp")
    c = lax.axis_index("ctx")
    t = lax.axis_index("tp")
    first = [jnp.where(t == 0, way(d, 0, k), way(d, 1, k)) for k in range(d.bits)]
    bit = (c >> first[0]) % 2
    sc = jnp.stack([x, bit, c, *first]).astype(jnp.int32)
    w_qkv = qkv_weight.transpose(0, 2, 1, 3)
    tiles = d.F // FT
    half = tiles // 2

    class Pieces:
        def __init__(self, layer, deps):
            def over(values):
                first = swap(values, "fsdp")
                return first, cross(d, first, 0)

            tile = (None, FT, FT)
            qkv = take(sc, w_qkv, (None, 3, d.Q, d.W), lambda n, b: (layer, 0, b, 0),
                       (3, d.Q, d.W), deps=deps)
            out = take(sc, out_weight, (None, d.W // 2, d.H), lambda n, b: (layer, b, 0),
                       (d.W // 2, d.H), deps=(qkv,))
            up_a = take(sc, up_weight, tile, lambda n, b: (layer, 0, b), (FT, FT), deps=(out,))
            up_b = take(sc, up_weight, tile, lambda n, b: (layer, 0, half + b), (FT, FT),
                        deps=(up_a,))
            dn = take(sc, down_weight, tile, lambda n, b: (layer, n * half + b, 0),
                      (2, FT, FT), 2, deps=(up_b,))
            self.last = dn
            self.qkv, self.out, self.dn = over(qkv), over(out), over(dn)
            self.up_a, self.up_b = over(up_a), over(up_b)
            self.up = (*self.up_a, *self.up_b)
            self.down = (*self.dn, *self.dn)

    p0 = Pieces(0, ())
    p = [p0]
    kb = key_table(d, parent_ids, depth_offsets)

    def both(rows):
        got = swap(rows, "tp")
        return jnp.where(
            t == 0,
            jnp.concatenate([rows, got], axis=0),
            jnp.concatenate([got, rows], axis=0),
        )

    def row(values):
        return values.reshape(1, -1)

    def swapped(values):
        return swap(values, "tp")

    def fsdp(values):
        return swap(values, "fsdp")

    class Kept:
        pass

    def forward(layer, state, needs):
        k = kept[layer]
        before = [needs(n) for n in range(1)]
        k.hidden, k.n_o, n_s, chunks = qkv_forward(
            d, layer, sc, state, row(norm_gains[layer, 0]), row(row_biases[layer, 0]),
            w_qkv, p[layer].qkv, qv_bias[layer], deps=before[0])
        k.n_r = fsdp(n_s)
        if layer == 0:
            p.append(Pieces(1, (k.hidden,)))
        before += [needs(n) for n in range(1, 3)]
        k.chunks = all_to_all(chunks)
        outs = all_to_all(attend_forward(d, sc, kb, k.chunks, deps=before[1]))
        k.ctx, part = out_forward(d, layer, sc, out_weight, p[layer].out, outs, deps=before[2])
        k.ctx_r = fsdp(k.ctx)
        before.append(needs(3))
        k.middle, k.n2_o, k.act_p, k.act_q, k.dg, part2 = ffn_forward(
            d, layer, sc, k.hidden, part, swapped(part), row(row_biases[layer, 1]),
            row(norm_gains[layer, 1]), row(row_biases[layer, 2]), up_weight,
            p[layer].up, row(up_bias[layer]), down_weight, p[layer].down, deps=before[3])
        state = (k.middle, part2, swapped(part2), row(row_biases[layer, 3]))
        k.act_pr, k.act_qr = fsdp(k.act_p), fsdp(k.act_q)
        return state

    state = both(tokens)
    p0 = p[0]
    kept = [Kept() for _ in range(LAYERS)]
    k0, k1 = kept
    state = forward(0, state, lambda n: (
        (p0.out[0], p0.up_a[0], p0.last) if n == 0
        else (p0.out[1], p0.up_a[1], p0.up_b[0], p0.dn[0]) if n == 1
        else (p[1].qkv[0], p[1].out[0], p[1].last) if n == 2
        else ()
    ))
    p1 = p[1]
    state = forward(1, state, lambda n: (
        (p1.up_a[0], p1.up_b[0]) if n == 0
        else (p1.out[1], p1.up_a[1], p1.dn[0], k1.n_r) if n == 1
        else (k0.act_pr,) if n == 2
        else ()
    ))
    own_rows = tokens.shape[0]

    def mine(values):
        return lax.dynamic_slice_in_dim(values, t * own_rows, own_rows, 0)

    output = mine(state[0]) + (
        (mine(state[1]).astype(F32) + mine(state[2]).astype(F32)) + state[3]
    )
    output = output.astype(BF)
    grad = both(cotangent)
    sums = [None] * LAYERS
    def grad_ffn(k, more, deps=()):
        ins = (k.n2_o, k.act_p, k.act_pr, k.act_q, k.act_qr, k.xba, k.xba_r, k.xbb, k.xbb_r,
               k.db_o)
        jobs = []
        for f in range(tiles):
            at = (5, 1) if f == 0 else (7, f - 1)
            jobs.append(((0, None), at, (2, 0), (at[0] + 1, at[1])))
        for f in range(tiles):
            at = (1, 1 + f) if f < half else (3, f - half)
            jobs.append((at, (9, None), (at[0] + 1, at[1]), (6, 0)))
        if more:
            ins += (k.ctx, k.ctx_r, k.da_o, k.da_r)
            jobs += [((10, None), (12, None), (11, None), (13, None))]
        return Sum(d, *weight_grad(d, "ffn", sc, ins, jobs, deps))

    def grad_qkv(k, more, deps=()):
        ins = (k.n_o, k.n_r, k.xc, k.xc_r)
        jobs = [((0, None), (2, n), (1, None), (3, n)) for n in range(3)]
        if more:
            ins += (k.ctx, k.da_o, k.ctx_r, k.da_r)
            jobs += [((4, None), (5, None), (6, None), (7, None))]
        return Sum(d, *weight_grad(d, "qkv", sc, ins, jobs, deps))

    def back_ffn(layer, k, grad, deps=()):
        k.db_o, k.xba, k.xbb, k.usum, k.bsum, part = ffn_backward(
            d, layer, sc, grad, k.dg, up_weight, p[layer].up, down_weight, p[layer].down,
            deps=deps)
        k.xba_r, k.xbb_r = fsdp(k.xba), fsdp(k.xbb)
        return part

    def back_context(layer, k, grad, part, deps=()):
        k.dmid, k.da_o, k.da_s, k.gsum2, k.ssum2, k.asum, dchunks = context_backward(
            d, layer, sc, grad, part, swapped(part), k.middle, row(norm_gains[layer, 1]),
            out_weight, p[layer].out, deps=deps)
        k.da_r = fsdp(k.da_s)
        return dchunks

    def back_qkv(layer, k, dparts, deps=()):
        k.xc, k.qvsum, part = qkv_backward(
            d, layer, sc, w_qkv, p[layer].qkv, dparts, deps=deps)
        k.xc_r = fsdp(k.xc)
        return part

    def back_input(layer, k, part, deps=()):
        grad, k.gsum1, k.ssum1 = input_backward(
            d, k.dmid, part, swapped(part), k.hidden, row(norm_gains[layer, 0]), deps=deps)
        sums[layer] = (k.qvsum, k.usum, k.gsum1, k.gsum2, k.ssum1, k.asum, k.ssum2, k.bsum)
        return grad

    def small_sums():
        return jnp.concatenate(
            [v.reshape(-1) for layer in sums for v in layer]
        ).reshape(-1, 128)

    part = back_ffn(1, k1, grad, (k0.act_qr, k1.ctx_r))
    dchunks = back_context(1, k1, grad, part, (state[2],))
    dback = attend_backward(d, sc, kb, k1.chunks, all_to_all(dchunks),
                            deps=(k1.act_pr, k1.act_qr))
    dparts = all_to_all(dback)
    f1 = grad_ffn(k1, False, (dback,))
    part = back_qkv(1, k1, dparts, (f1.keep, k0.n_r, k0.ctx_r))
    grad = back_input(1, k1, part)
    part = back_ffn(0, k0, grad)
    a = f1.step(part)
    dchunks = back_context(0, k0, grad, part, (a, k1.xc_r, k1.da_r))
    q1 = grad_qkv(k1, True, (dchunks,))
    a = f1.step(q1.keep)
    dback = attend_backward(d, sc, kb, k0.chunks, all_to_all(dchunks), deps=(a, k0.xba_r))
    dparts = all_to_all(dback)
    f0 = grad_ffn(k0, True, (dback,))
    part = back_qkv(0, k0, dparts, (f0.keep,))
    grad = back_input(0, k0, part)
    flat = small_sums()
    flat = flat + swap(flat, "fsdp")
    a = q1.step(grad)
    a = f1.step(a)
    a = f0.step(a, flat)
    q0 = grad_qkv(k0, False, (a,))
    a = q1.step(q0.keep)
    a = q0.step(a)
    a = f0.step(a)
    a = f1.step(a)
    flat = flat + cross_all(d, flat, 0)
    a = q1.step(a, flat)
    a = q0.step(a)
    a = f1.step(a)
    a = q1.step(a)
    flats = list(range(1, d.bits))
    while f1.at < 2 * d.bits - 1:
        a = f1.step(a)
    while any(u.at < 2 * d.bits - 1 for u in (q1, q0, f0)):
        for unit in (f0, q1, q0):
            if unit.at < 2 * d.bits - 1:
                if unit is f0 and flats:
                    flat = flat + cross_all(d, flat, flats.pop(0))
                a = unit.step(a, flat) if unit is f0 else unit.step(a)
    for step in flats:
        flat = flat + cross_all(d, flat, step)
    ffn_kinds = (("cols", tiles), ("mats", tiles))
    g_ffn = place(d, 1, sc, f1.finish(), None, ffn_kinds, "ffn", (a,))
    g_qkv = place(d, 1, sc, q1.finish(), None, (("mats", 3), ("mats", 1)), "qkv", (g_ffn[0],))
    g_up, g_down, g_out = place(d, 0, sc, f0.finish(), (*g_ffn, g_qkv[1]),
                                (*ffn_kinds, ("mats", 1)), "ffn", (a,))
    (g_qkv,) = place(d, 0, sc, q0.finish(), (g_qkv[0],), (("mats", 3),), "qkv", (g_up,))
    flat = flat.reshape(LAYERS, -1)
    n_qv, n_up = 2 * d.W, d.F
    qv_grad = flat[:, :n_qv].reshape(LAYERS, 2, d.W)
    up_grad = flat[:, n_qv : n_qv + n_up]
    rest = flat[:, n_qv + n_up :].reshape(LAYERS, 6, d.D)
    return (
        output,
        mine(grad),
        g_qkv.transpose(0, 2, 1, 3),
        g_out.reshape(LAYERS, d.W, d.H),
        g_up.reshape(LAYERS, d.H, d.F),
        g_down.reshape(LAYERS, d.F, d.H),
        qv_grad,
        up_grad,
        rest[:, :2],
        rest[:, 2:],
    )


def solution(mesh):
    in_specs = (
        P(("fsdp", "ctx", "tp"), None),
        P(None, "fsdp", None, "tp"),
        P(None, "tp", "fsdp"),
        P(None, "fsdp", "tp"),
        P(None, "tp", "fsdp"),
        P(None, None, "tp"),
        P(None, "tp"),
        P(),
        P(),
        P(),
        P(),
        P(("fsdp", "ctx", "tp"), None),
    )
    out_specs = (
        P(("fsdp", "ctx", "tp"), None),
        P(("fsdp", "ctx", "tp"), None),
        P(None, "fsdp", None, "tp"),
        P(None, "tp", "fsdp"),
        P(None, "fsdp", "tp"),
        P(None, "tp", "fsdp"),
        P(None, None, "tp"),
        P(None, "tp"),
        P(),
        P(),
    )
    return jax.shard_map(
        on_device, mesh=mesh, in_specs=in_specs, out_specs=out_specs, check_vma=False
    )
```

```python
import functools

import jax
import jax.numpy as jnp
from jax import lax
from jax.experimental import pallas as pl
from jax.experimental.pallas import tpu as pltpu
from jax.sharding import PartitionSpec as P

HEAD_DIM = 128
LAYERS = 2
SEG = 128
EPSILON = 1e-05
MASKED = -1e30
SCALE = HEAD_DIM ** (-0.5)
GELU_A = 0.7978845608028654
GELU_B = 0.044715
BF = jnp.bfloat16
F32 = jnp.float32
VLIM = 56 * 1024 * 1024

NN = (((1,), (0,)), ((), ()))
NT = (((1,), (1,)), ((), ()))
TN = (((0,), (0,)), ((), ()))


def mm(a, b, dims=NN):
    return lax.dot_general(a, b, dims, preferred_element_type=F32)


def sds(shape, dtype):
    return jax.ShapeDtypeStruct(shape, dtype)


VSPEC = pl.BlockSpec(memory_space=pltpu.VMEM)
SSPEC = pl.BlockSpec(memory_space=pltpu.SMEM)


def cost(flops, nbytes):
    return pl.CostEstimate(flops=int(flops), bytes_accessed=int(nbytes), transcendentals=0)


def kernel_call(body, args, in_specs, out_specs, out_shape, name, scratch=(), grid=None,
                deps=(), work=None, aliases=None):
    count, extra = len(args), len(deps)

    def ordered(*refs):
        body(*refs[:count], *refs[count + extra :])

    kwargs = {} if grid is None else {"grid": grid}
    return pl.pallas_call(
        ordered,
        in_specs=list(in_specs) + [pl.BlockSpec(memory_space=pl.ANY)] * extra,
        out_specs=out_specs,
        out_shape=out_shape,
        scratch_shapes=list(scratch),
        input_output_aliases=aliases or {},
        compiler_params=pltpu.CompilerParams(vmem_limit_bytes=VLIM),
        cost_estimate=work,
        name=name,
        **kwargs,
    )(*args, *deps)


def norm_rows(v):
    centered = v - jnp.mean(v, axis=-1, keepdims=True)
    rstd = lax.rsqrt(jnp.mean(centered * centered, axis=-1, keepdims=True) + EPSILON)
    return centered * rstd, rstd


def norm_back(d, v, gain):
    xhat, rstd = norm_rows(v)
    dx = d * gain
    back = rstd * (
        dx
        - jnp.mean(dx, axis=-1, keepdims=True)
        - xhat * jnp.mean(dx * xhat, axis=-1, keepdims=True)
    )
    d_gain = jnp.sum(d * xhat, axis=0, keepdims=True)
    d_shift = jnp.sum(d, axis=0, keepdims=True)
    return back, d_gain, d_shift


class Dims:
    def __init__(self, tokens, qkv_weight, up_weight):
        self.tp = lax.axis_size("tp")
        self.C = lax.axis_size("ctx")
        self.T = tokens.shape[0] * self.tp
        self.D = tokens.shape[1]
        self.H = self.D // lax.axis_size("fsdp")
        self.Q = self.H // 2
        self.W = qkv_weight.shape[3]
        self.F = up_weight.shape[2]
        self.lh = self.W // HEAD_DIM
        self.g = self.C // self.lh
        self.rq = self.T // self.g
        self.chunk = self.rq + 2 * self.T
        self.bits = self.C.bit_length() - 1


def offs(sc, d):
    x = sc[0]
    y = sc[1]
    own = pl.multiple_of(x * d.H, d.H)
    oth = pl.multiple_of((1 - x) * d.H, d.H)
    first = pl.multiple_of((1 - x) * d.H + y * d.Q, d.Q)
    second = pl.multiple_of((1 - x) * d.H + (1 - y) * d.Q, d.Q)
    return own, oth, first, second


def spot_of(d, chip):
    row, head = (chip % d.g) * d.rq, (chip // d.g) * HEAD_DIM
    return slice(row, row + d.rq), slice(head, head + HEAD_DIM)


def qkv_body(d, first, *refs):
    if first:
        sc, hid, gain, shift, w, w1, w2, qvb = refs[:8]
        rest = refs[8:]
        hidden = hid[...].astype(F32)
    else:
        sc, mid, pa, pb, bias, gain, shift, w, w1, w2, qvb = refs[:11]
        rest = refs[11:]
        hidden = mid[...] + ((pa[...].astype(F32) + pb[...].astype(F32)) + bias[...])
    h_out, no_out, ns_out, chunks, n_out, scr = rest
    own, oth, p1, p2 = offs(sc, d)
    h_out[...] = hidden
    xhat, _ = norm_rows(hidden)
    n_out[...] = (xhat * gain[...] + shift[...]).astype(BF)
    ns_out[...] = n_out[:, pl.ds(oth, d.H)]
    a0 = n_out[:, pl.ds(own, d.H)]
    no_out[...] = a0
    a1 = n_out[:, pl.ds(p1, d.Q)]
    a2 = n_out[:, pl.ds(p2, d.Q)]
    for n in range(3):
        proj = mm(a0, w[n]) + mm(a1, w1[n]) + mm(a2, w2[n])
        if n == 0:
            proj = proj + qvb[0:1, :]
        if n == 2:
            proj = proj + qvb[1:2, :]
        scr[n] = proj.astype(BF)
    for to in range(d.C):
        row, col = spot_of(d, to)
        chunks[to, 0 : d.rq, :] = scr[0, row, col]
        chunks[to, d.rq : d.rq + d.T, :] = scr[1, :, col]
        chunks[to, d.rq + d.T :, :] = scr[2, :, col]


def whole(shape):
    return pl.BlockSpec(shape, lambda *_: (0,) * len(shape))


def piece_specs(shape, pieces, axis):
    if pieces[0] is not pieces[1]:
        return [whole(shape), whole(shape)]
    second = tuple(1 if k == axis else 0 for k in range(len(shape)))
    return [whole(shape), pl.BlockSpec(shape, lambda *_: second)]


def qkv_forward(d, layer, sc, hid, gain, shift, w, pieces, qvb, deps=()):
    first = not isinstance(hid, tuple)
    hid = (hid,) if first else hid
    wspec = pl.BlockSpec((None, 3, d.H, d.W), lambda i: (layer, 0, 0, 0))
    in_specs = [SSPEC] + [whole(a.shape) for a in hid]
    in_specs += [whole(gain.shape), whole(shift.shape), wspec]
    in_specs += piece_specs((3, d.Q, d.W), pieces, 1) + [whole(qvb.shape)]
    outs = [sds((d.T, d.D), F32), sds((d.T, d.H), BF), sds((d.T, d.H), BF)]
    outs += [sds((d.C, d.chunk, HEAD_DIM), BF)]
    return kernel_call(
        functools.partial(qkv_body, d, first),
        (sc, *hid, gain, shift, w, *pieces, qvb,),
        grid=(1,),
        in_specs=in_specs,
        out_specs=[whole(o.shape) for o in outs],
        out_shape=outs,
        scratch=[pltpu.VMEM((d.T, d.D), BF), pltpu.VMEM((3, d.T, d.W), BF)],
        work=cost(2 * d.T * d.D * 3 * d.W, 8e6),
        name="qkv_forward",
        deps=deps,
    )


def load_chunks(d, sc, chunks, qs, ks, vs):
    qs[...] = chunks[:, 0 : d.rq, :]
    ks[...] = chunks[:, d.rq : d.rq + d.T, :]
    vs[...] = chunks[:, d.rq + d.T :, :]


def score_block(d, sc, kb, q, k, s, ext):
    part = lax.rem(sc[2], d.g)
    seg = s * (d.T // SEG) + lax.div(part * d.rq, SEG)
    scores = mm(q, k, NT) * SCALE + kb[pl.ds(seg, 1), 0:ext]
    col = lax.broadcasted_iota(jnp.int32, (d.rq, ext), 1) - s * d.T
    row = lax.broadcasted_iota(jnp.int32, (d.rq, ext), 0) + part * d.rq
    return jnp.where(col <= row, scores, MASKED)


UNROLL = 8
SHIFT = 3


def each_source(d, one):
    if d.C <= UNROLL:
        for s in range(d.C):
            one(s, s + 1)
    else:
        lax.fori_loop(0, d.C, lambda s, carry: (one(s, d.C), carry)[1], 0)


def attend_body(d, *refs):
    sc, kb, chunks, cs, qs, ks, vs = refs
    load_chunks(d, sc, chunks, qs, ks, vs)
    def one(s, seen):
        ext = seen * d.T
        k = ks[0:seen].reshape(ext, HEAD_DIM)
        v = vs[0:seen].reshape(ext, HEAD_DIM)
        scores = score_block(d, sc, kb, qs[s], k, s, ext)
        e = jnp.exp(scores - jnp.max(scores, axis=-1, keepdims=True))
        total = jnp.sum(e, axis=-1, keepdims=True)
        cs[s] = (mm(e.astype(BF), v) / total).astype(BF)

    each_source(d, one)


def attend_forward(d, sc, kb, chunks, deps=()):
    return kernel_call(
        functools.partial(attend_body, d),
        (sc, kb, chunks,),
        in_specs=[SSPEC] + [VSPEC] * 2,
        out_specs=VSPEC,
        out_shape=sds((d.C, d.rq, HEAD_DIM), BF),
        scratch=[
            pltpu.VMEM((d.C, d.rq, HEAD_DIM), BF),
            pltpu.VMEM((d.C, d.T, HEAD_DIM), BF),
            pltpu.VMEM((d.C, d.T, HEAD_DIM), BF),
        ],
        work=cost(2 * d.C * d.rq * d.C * d.T * HEAD_DIM * 2, 3e6),
        name="attend_forward",
        deps=deps,
    )


def out_body(d, *refs):
    sc, w, w1, w2, chunks, ctx, part = refs
    for src in range(d.C):
        ctx[spot_of(d, src)] = chunks[src]
    own, oth, _, _ = offs(sc, d)
    half = d.W // 2
    k1 = pl.multiple_of(sc[1] * half, half)
    k2 = pl.multiple_of((1 - sc[1]) * half, half)
    part[:, pl.ds(own, d.H)] = mm(ctx[...], w[...]).astype(BF)
    part[:, pl.ds(oth, d.H)] = (
        mm(ctx[:, pl.ds(k1, half)], w1[...]) + mm(ctx[:, pl.ds(k2, half)], w2[...])
    ).astype(BF)


def out_forward(d, layer, sc, w, pieces, chunks, deps=()):
    wspec = pl.BlockSpec((None, d.W, d.H), lambda i: (layer, 0, 0))
    outs = [sds((d.T, d.W), BF), sds((d.T, d.D), BF)]
    return kernel_call(
        functools.partial(out_body, d),
        (sc, w, *pieces, chunks,),
        grid=(1,),
        in_specs=[SSPEC, wspec] + piece_specs((d.W // 2, d.H), pieces, 0)
        + [whole(chunks.shape)],
        out_specs=[whole(o.shape) for o in outs],
        out_shape=outs,
        work=cost(2 * d.T * d.D * d.W, 3e6),
        name="out_forward",
        deps=deps,
    )


FT = 512


def tile_of(f, sc, tiles, refs, use):
    half = tiles // 2
    mine = lax.rem(f, half) == sc[1]
    for number, (came, then) in enumerate((refs[:2], refs[2:])):
        here = lax.div(f, half) == number

        @pl.when(jnp.logical_and(here, mine))
        def _():
            use(came)

        @pl.when(jnp.logical_and(here, jnp.logical_not(mine)))
        def _():
            use(then)


def ffn_body(d, tiles, sc, hid, pa, pb, bias, gain, shift,
             u, u1, u2, u3, u4, ub, w, w1, w2, w3, w4,
             mid, no, act_p, act_q, dg, part, n2, acc, pre):
    f = pl.program_id(0)
    own, oth, _, _ = offs(sc, d)

    @pl.when(f == 0)
    def _():
        m = hid[...] + ((pa[...].astype(F32) + pb[...].astype(F32)) + bias[...])
        mid[...] = m
        xhat, _ = norm_rows(m)
        n2[...] = (xhat * gain[...] + shift[...]).astype(BF)
        no[...] = n2[:, pl.ds(own, d.H)]
        act_p[0] = n2[:, pl.ds(oth, d.H)]
        acc[...] = jnp.zeros_like(acc)

    def up(ref):
        pre[...] = mm(act_p[0], ref[...])

    tile_of(f, sc, tiles, (u1, u2, u3, u4), up)
    v = pre[...] + mm(no[...], u[...]) + ub[...]
    sq = v * v
    th = jnp.tanh(GELU_A * v * (1.0 + GELU_B * sq))
    half = 0.5 * (1.0 + th)
    a = (v * half).astype(BF)

    @pl.when(f < tiles // 2)
    def _():
        act_p[1 + f] = a

    @pl.when(f >= tiles // 2)
    def _():
        act_q[f - tiles // 2] = a

    dg[...] = (
        half + 0.5 * v * (1.0 - th * th) * (GELU_A * (1.0 + 3.0 * GELU_B * sq))
    ).astype(BF)
    acc[0] += mm(a, w[...])

    def down(ref):
        acc[1] += mm(a, ref[...])

    tile_of(f, sc, tiles, (w1, w2, w3, w4), down)

    @pl.when(f == tiles - 1)
    def _():
        part[:, pl.ds(own, d.H)] = acc[0].astype(BF)
        part[:, pl.ds(oth, d.H)] = acc[1].astype(BF)


def ffn_specs(d, layer):
    u = pl.BlockSpec((None, d.H, FT), lambda f: (layer, 0, f))
    w = pl.BlockSpec((None, FT, d.H), lambda f: (layer, f, 0))
    return [u] + [whole((d.H, FT))] * 4, [w] + [whole((FT, d.H))] * 4


def ffn_forward(d, layer, sc, hid, pa, pb, bias, gain, shift,
                up_w, up_p, ub, dn_w, dn_p, deps=()):
    tiles = d.F // FT
    us, ws = ffn_specs(d, layer)
    side = whole((d.T, d.H))
    col = pl.BlockSpec((d.T, FT), lambda f: (0, f))
    row = whole((1, d.D))
    full = whole((d.T, d.D))
    act_p = sds((1 + tiles // 2, d.T, FT), BF)
    act_q = sds((tiles // 2, d.T, FT), BF)
    return kernel_call(
        functools.partial(ffn_body, d, tiles),
        (sc, hid, pa, pb, bias, gain, shift, up_w, *up_p, ub, dn_w, *dn_p),
        [SSPEC, full, full, full, row, row, row, *us,
         pl.BlockSpec((1, FT), lambda f: (0, f)), *ws],
        [full, side, whole(act_p.shape), whole(act_q.shape), col, full],
        [sds((d.T, d.D), F32), sds((d.T, d.H), BF), act_p, act_q,
         sds((d.T, d.F), BF), sds((d.T, d.D), BF)],
        "ffn_forward",
        scratch=[pltpu.VMEM((d.T, d.D), BF), pltpu.VMEM((2, d.T, d.H), F32),
                 pltpu.VMEM((d.T, FT), F32)],
        grid=(tiles,), deps=deps, work=cost(4 * d.T * d.D * d.F, 14e6))


def ffn_back_body(d, tiles, sc, grad, dg, u, u1, u2, u3, u4, w, w1, w2, w3, w4,
                  dbo, xba, xbb, usum, bsum, part, acc, dact):
    f = pl.program_id(0)
    own, oth, _, _ = offs(sc, d)

    @pl.when(f == 0)
    def _():
        dbo[...] = grad[:, pl.ds(own, d.H)].astype(BF)
        xba[0] = grad[:, pl.ds(oth, d.H)].astype(BF)
        bsum[...] = jnp.sum(grad[...].astype(BF).astype(F32), axis=0, keepdims=True)
        acc[...] = jnp.zeros_like(acc)

    def down(ref):
        dact[...] = mm(xba[0], ref[...], NT)

    tile_of(f, sc, tiles, (w1, w2, w3, w4), down)
    da = dact[...] + mm(dbo[...], w[...], NT)
    dp = (da * dg[...].astype(F32)).astype(BF)

    @pl.when(f == 0)
    def _():
        xba[1] = dp

    @pl.when(f > 0)
    def _():
        xbb[f - 1] = dp

    usum[...] = jnp.sum(dp.astype(F32), axis=0, keepdims=True)
    acc[0] += mm(dp, u[...], NT)

    def up(ref):
        acc[1] += mm(dp, ref[...], NT)

    tile_of(f, sc, tiles, (u1, u2, u3, u4), up)

    @pl.when(f == tiles - 1)
    def _():
        part[:, pl.ds(own, d.H)] = acc[0].astype(BF)
        part[:, pl.ds(oth, d.H)] = acc[1].astype(BF)


def ffn_backward(d, layer, sc, grad, dg, up_w, up_p, dn_w, dn_p, deps=()):
    tiles = d.F // FT
    us, ws = ffn_specs(d, layer)
    side = whole((d.T, d.H))
    col = pl.BlockSpec((d.T, FT), lambda f: (0, f))
    full = whole((d.T, d.D))
    xba = sds((2, d.T, FT), BF)
    xbb = sds((tiles - 1, d.T, FT), BF)
    return kernel_call(
        functools.partial(ffn_back_body, d, tiles),
        (sc, grad, dg, up_w, *up_p, dn_w, *dn_p),
        [SSPEC, full, col, *us, *ws],
        [side, whole(xba.shape), whole(xbb.shape),
         pl.BlockSpec((1, FT), lambda f: (0, f)), whole((1, d.D)), full],
        [sds((d.T, d.H), BF), xba, xbb,
         sds((1, d.F), F32), sds((1, d.D), F32), sds((d.T, d.D), BF)],
        "ffn_backward",
        scratch=[pltpu.VMEM((2, d.T, d.H), F32), pltpu.VMEM((d.T, FT), F32)],
        grid=(tiles,), deps=deps, work=cost(4 * d.T * d.D * d.F, 14e6))


def context_back_body(d, *refs):
    sc, grad, pa, pb, mid, gain, w, w1, w2 = refs[:9]
    dmid, dao, das, gsum, ssum, asum, chunks, da, dctx = refs[9:]
    own, oth, _, _ = offs(sc, d)
    back, g, s = norm_back(pa[...].astype(F32) + pb[...].astype(F32), mid[...], gain[...])
    gsum[...] = g
    ssum[...] = s
    total = grad[...].astype(F32) + back
    dmid[...] = total
    da[...] = total.astype(BF)
    dao[...] = da[:, pl.ds(own, d.H)]
    das[...] = da[:, pl.ds(oth, d.H)]
    asum[...] = jnp.sum(da[...].astype(F32), axis=0, keepdims=True)
    half = d.W // 2
    k1 = pl.multiple_of(sc[1] * half, half)
    k2 = pl.multiple_of((1 - sc[1]) * half, half)
    dctx[...] = mm(da[:, pl.ds(own, d.H)], w[...], NT)
    dctx[:, pl.ds(k1, half)] += mm(da[:, pl.ds(oth, d.H)], w1[...], NT)
    dctx[:, pl.ds(k2, half)] += mm(da[:, pl.ds(oth, d.H)], w2[...], NT)
    for to in range(d.C):
        chunks[to] = dctx[spot_of(d, to)].astype(BF)


def context_backward(d, layer, sc, grad, pa, pb, mid, gain, w, pieces, deps=()):
    wspec = pl.BlockSpec((None, d.W, d.H), lambda i: (layer, 0, 0))
    outs = [sds((d.T, d.D), F32), sds((d.T, d.H), BF), sds((d.T, d.H), BF)]
    outs += [sds((1, d.D), F32)] * 3 + [sds((d.C, d.rq, HEAD_DIM), BF)]
    return kernel_call(
        functools.partial(context_back_body, d),
        (sc, grad, pa, pb, mid, gain, w, *pieces,),
        grid=(1,),
        in_specs=[SSPEC] + [whole(a.shape) for a in (grad, pa, pb, mid, gain)]
        + [wspec] + piece_specs((d.W // 2, d.H), pieces, 0),
        out_specs=[whole(o.shape) for o in outs],
        out_shape=outs,
        scratch=[pltpu.VMEM((d.T, d.D), BF), pltpu.VMEM((d.T, d.W), F32)],
        work=cost(2 * d.T * d.D * d.W, 6e6),
        name="context_backward",
        deps=deps,
    )


def attend_back_body(d, *refs):
    sc, kb, chunks, cs, outs, qs, ks, vs, dks, dvs = refs
    load_chunks(d, sc, chunks, qs, ks, vs)
    dks[...] = jnp.zeros_like(dks)
    dvs[...] = jnp.zeros_like(dvs)
    def one(s, seen):
        ext = seen * d.T
        k = ks[0:seen].reshape(ext, HEAD_DIM)
        v = vs[0:seen].reshape(ext, HEAD_DIM)
        q = qs[s]
        dc = cs[s]
        scores = score_block(d, sc, kb, q, k, s, ext)
        e = jnp.exp(scores - jnp.max(scores, axis=-1, keepdims=True))
        p = e / jnp.sum(e, axis=-1, keepdims=True)
        dp = mm(dc, v, NT)
        ds = (p * (dp - jnp.sum(p * dp, axis=-1, keepdims=True))).astype(BF)
        outs[s, 0 : d.rq, :] = (mm(ds, k) * SCALE).astype(BF)
        dks[0:seen] += mm(ds, q, TN).reshape(seen, d.T, HEAD_DIM)
        dvs[0:seen] += mm(p.astype(BF), dc, TN).reshape(seen, d.T, HEAD_DIM)

    each_source(d, one)
    outs[:, d.rq : d.rq + d.T, :] = (dks[...] * SCALE).astype(BF)
    outs[:, d.rq + d.T :, :] = dvs[...].astype(BF)


def attend_backward(d, sc, kb, chunks, dchunks, deps=()):
    return kernel_call(
        functools.partial(attend_back_body, d),
        (sc, kb, chunks, dchunks,),
        in_specs=[SSPEC] + [VSPEC] * 3,
        out_specs=VSPEC,
        out_shape=sds((d.C, d.chunk, HEAD_DIM), BF),
        scratch=[
            pltpu.VMEM((d.C, d.rq, HEAD_DIM), BF),
            pltpu.VMEM((d.C, d.T, HEAD_DIM), BF),
            pltpu.VMEM((d.C, d.T, HEAD_DIM), BF),
            pltpu.VMEM((d.C, d.T, HEAD_DIM), F32),
            pltpu.VMEM((d.C, d.T, HEAD_DIM), F32),
        ],
        work=cost(5 * d.C * d.rq * d.C * d.T * HEAD_DIM * 2, 4e6),
        name="attend_backward",
        deps=deps,
    )


def qkv_back_body(d, sc, w, w1, w2, chunks, xb, qvsum, part, dk, dv):
    dk[...] = jnp.zeros_like(dk)
    dv[...] = jnp.zeros_like(dv)
    for src in range(d.C):
        row, col = spot_of(d, src)
        xb[0, row, col] = chunks[src, 0 : d.rq, :]
        dk[:, col] += chunks[src, d.rq : d.rq + d.T, :].astype(F32)
        dv[:, col] += chunks[src, d.rq + d.T :, :].astype(F32)
    xb[1] = dk[...].astype(BF)
    xb[2] = dv[...].astype(BF)
    qvsum[0:1, :] = jnp.sum(xb[0].astype(F32), axis=0, keepdims=True)
    qvsum[1:2, :] = jnp.sum(xb[2].astype(F32), axis=0, keepdims=True)
    own, _, p1, p2 = offs(sc, d)
    for ref, at, width in ((w, own, d.H), (w1, p1, d.Q), (w2, p2, d.Q)):
        total = mm(xb[0], ref[0], NT) + mm(xb[1], ref[1], NT) + mm(xb[2], ref[2], NT)
        part[:, pl.ds(at, width)] = total.astype(BF)


def qkv_backward(d, layer, sc, w, pieces, chunks, deps=()):
    wspec = pl.BlockSpec((None, 3, d.H, d.W), lambda i: (layer, 0, 0, 0))
    outs = [sds((3, d.T, d.W), BF), sds((2, d.W), F32), sds((d.T, d.D), BF)]
    return kernel_call(
        functools.partial(qkv_back_body, d),
        (sc, w, *pieces, chunks),
        [SSPEC, wspec] + [whole((3, d.Q, d.W))] * 2 + [whole(chunks.shape)],
        [whole(o.shape) for o in outs],
        outs,
        "qkv_backward",
        scratch=[pltpu.VMEM((d.T, d.W), F32)] * 2,
        grid=(1,), deps=deps, work=cost(2 * d.T * d.D * 3 * d.W, 7e6))


def input_back_body(dmid, pa, pb, hid, gain, grad, gsum, ssum):
    back, g, s = norm_back(pa[...].astype(F32) + pb[...].astype(F32), hid[...], gain[...])
    grad[...] = dmid[...] + back
    gsum[...] = g
    ssum[...] = s


def input_backward(d, dmid, pa, pb, hid, gain, deps=()):
    return kernel_call(
        input_back_body,
        (dmid, pa, pb, hid, gain,),
        in_specs=[VSPEC] * 5,
        out_specs=[VSPEC] * 3,
        out_shape=[sds((d.T, d.D), F32)] + [sds((1, d.D), F32)] * 2,
        work=cost(3e6, 5e6),
        name="input_backward",
        deps=deps,
    )


def spot_bits(value, shifts, bits):
    out = 0
    for k in range(bits):
        bit = lax.bitwise_and(lax.shift_right_logical(value, shifts[k]), 1)
        out = out + bit * (1 << (bits - 1 - k))
    return out


EXTRA = 16


def shift_at(d, mix):
    return SHIFT if mix else SHIFT + d.bits


def wgrad_body(d, tiles, mix, flat, sc, *refs):
    ins = refs[:-2]
    keep, send = refs[-2:]
    c = sc[2]
    shifts = [sc[shift_at(d, mix) + k] for k in range(d.bits)]
    rb = FT // d.C
    spots = [spot_bits(lax.bitwise_xor(c, b), shifts, d.bits) for b in range(d.C)]

    def pick(item):
        ref, at = item
        return ins[ref][...] if at is None else ins[ref][at]

    def put(spot, low, piece):
        @pl.when(spot < d.C // 2)
        def _():
            keep[spot, low : low + piece.shape[0]] = piece

        @pl.when(spot >= d.C // 2)
        def _():
            send[spot - d.C // 2, low : low + piece.shape[0]] = piece

    for m, (a, b, a2, b2) in enumerate(tiles):
        total = mm(pick(a), pick(b), TN) + mm(pick(a2), pick(b2), TN)
        total = total.astype(BF)
        for block, spot in enumerate(spots):
            put(spot, m * rb, total[block * rb : (block + 1) * rb, :])
    if flat is not None:
        for block, spot in enumerate(spots):
            put(spot, len(tiles) * rb, ins[flat][block].astype(BF))


def weight_grad(d, name, sc, ins, tiles, mix, flat=None, deps=()):
    rows = len(tiles) * (FT // d.C)
    if flat is not None:
        ins = (*ins, flat)
        rows += EXTRA
    return kernel_call(
        functools.partial(wgrad_body, d, tiles, mix, None if flat is None else len(ins) - 1),
        (sc, *ins),
        [SSPEC] + [VSPEC] * len(ins),
        [VSPEC] * 2,
        [sds((d.C // 2, rows, FT), BF)] * 2,
        "weight_grad_" + name,
        deps=deps, work=cost(4 * d.T * len(tiles) * FT * FT, 8e6))


def small_rows(d):
    return (2, 1, 2, 4), (d.W // FT, d.F // FT, d.D // FT, d.D // FT)


def place_body(d, wide, count_in, extra, layer, owner, flat, sc, *refs):
    ins = refs[:count_in]
    outs = refs[count_in + extra : -3]
    buf, small, sems = refs[-3:]
    rb = FT // d.C
    nt = buf.shape[0]
    r = 0
    for part in ins:
        for n in range(part.shape[0]):
            block = owner(sc, r)
            row = pl.multiple_of(block * rb, rb)
            for m in range(nt):
                buf[m, pl.ds(row, rb), :] = part[n, m * rb : (m + 1) * rb].astype(F32)
            if flat:
                small[block] = part[n, nt * rb :].astype(F32)
            r += 1
    if flat:
        at = 0
        for k in range(LAYERS):
            for out, rows, pieces in zip(outs[len(wide) :], *small_rows(d)):
                for row in range(rows):
                    for piece in range(pieces):
                        line = small[at // EXTRA, at % EXTRA : at % EXTRA + 1, :]
                        lanes = slice(piece * FT, (piece + 1) * FT)
                        if rows == 1:
                            out[k : k + 1, lanes] = line
                        else:
                            out[k, row : row + 1, lanes] = line
                        at += 1
    copies = []
    m = 0
    for out, (kind, count) in zip(outs, wide):
        if kind == "cols":
            for k in range(count):
                copies.append((buf.at[m + k], out.at[layer, :, pl.ds(k * FT, FT)]))
        else:
            copies.append((buf.at[pl.ds(m, count)], out.at[layer]))
        m += count
    going = [pltpu.make_async_copy(a, b, sems.at[k]) for k, (a, b) in enumerate(copies)]
    for one in going:
        one.start()
    for one in going:
        one.wait()


def place(d, layer, sc, unit, before, wide, name, deps=()):
    parts = unit.finish()
    nt = sum(n for _, n in wide)
    flat = parts[0].shape[1] > nt * (FT // d.C)
    extra = tuple(before or ()) + tuple(deps)
    alias = {1 + len(parts) + k: k for k in range(len(before or ()))}
    shapes = [
        sds((LAYERS, FT, n * FT) if kind == "cols" else (LAYERS, n, FT, FT), F32)
        for kind, n in wide
    ]
    specs = [pl.BlockSpec(memory_space=pl.ANY)] * len(wide)
    if flat:
        for rows, pieces in zip(*small_rows(d)):
            one = (rows, pieces * FT) if rows > 1 else (pieces * FT,)
            shapes.append(sds((LAYERS, *one), F32))
            specs.append(VSPEC)
    moves = sum(n if kind == "cols" else 1 for kind, n in wide)
    at = shift_at(d, unit.mix)

    def owner(scalars, r):
        turned = 0
        for k in range(d.bits):
            if r >> (d.bits - 1 - k) & 1:
                turned = turned + lax.shift_left(jnp.int32(1), scalars[at + k])
        return lax.bitwise_xor(scalars[2], jnp.int32(turned))

    return pl.pallas_call(
        functools.partial(place_body, d, wide, len(parts), len(extra), layer, owner, flat),
        in_specs=[SSPEC] + [VSPEC] * len(parts) + [pl.BlockSpec(memory_space=pl.ANY)] * len(extra),
        out_specs=specs,
        out_shape=shapes,
        scratch_shapes=[
            pltpu.VMEM((nt, FT, FT), F32),
            pltpu.VMEM((d.C, EXTRA, FT), F32),
            pltpu.SemaphoreType.DMA((moves,)),
        ],
        input_output_aliases=alias,
        compiler_params=pltpu.CompilerParams(vmem_limit_bytes=VLIM),
        name="place_" + name,
    )(sc, *parts, *extra)


def swap(values, axis):
    return lax.ppermute(values, axis, [(0, 1), (1, 0)])


def way(d, core, step, mix=True):
    if mix and step < 2 and d.bits > 1:
        return step if core == 0 else 1 - step
    return step


def cross(d, values, step, mix=True):
    pairs = []
    for i in range(d.C):
        for core in range(d.tp):
            to = i ^ (1 << way(d, core, step, mix))
            pairs.append((i * d.tp + core, to * d.tp + core))
    return lax.ppermute(values, ("ctx", "tp"), pairs)


def take_body(sc, w, *refs):
    refs[-1][...] = w[...]


def take(sc, w, block, index, shape, steps=1, deps=()):
    out_block = shape if steps == 1 else (None, *shape[1:])
    return pl.pallas_call(
        take_body,
        grid_spec=pltpu.PrefetchScalarGridSpec(
            num_scalar_prefetch=1,
            grid=(steps,),
            in_specs=[pl.BlockSpec(block, lambda n, s: index(n, s[1]))]
            + [pl.BlockSpec(memory_space=pl.ANY)] * len(deps),
            out_specs=pl.BlockSpec(out_block, lambda n, s: (n,) + (0,) * (len(shape) - 1)),
        ),
        out_shape=sds(shape, BF),
        compiler_params=pltpu.CompilerParams(vmem_limit_bytes=VLIM),
        name="take",
    )(sc, w, *deps)


def fold_body(keep, got, *outs):
    total = (keep[...].astype(F32) + got[...].astype(F32)).astype(BF)
    if len(outs) == 1:
        outs[0][...] = total
    else:
        half = total.shape[0] // 2
        outs[0][...] = total[:half]
        outs[1][...] = total[half:]


def fold(keep, got, deps=()):
    count = keep.shape[0]
    shapes = [keep.shape] if count == 1 else [(count // 2, *keep.shape[1:])] * 2
    return kernel_call(
        fold_body, (keep, got), [VSPEC] * 2, [VSPEC] * len(shapes),
        [sds(v, BF) for v in shapes], "fold", deps=deps, work=cost(1e6, 3e6))


def join_body(*refs):
    out = refs[-1]
    at = 0
    for ref in refs[:-1]:
        out[at : at + ref.shape[0]] = ref[...]
        at += ref.shape[0]


def join(parts, deps=()):
    if len(parts) == 1:
        return parts[0]
    count = sum(p.shape[0] for p in parts)
    return kernel_call(
        join_body, tuple(parts), [VSPEC] * len(parts), VSPEC,
        sds((count, *parts[0].shape[1:]), BF), "join", deps=deps, work=cost(1e5, 3e6))


class Sum:
    def __init__(self, d, mix, keep, send):
        self.d, self.mix = d, mix
        self.keep = keep
        self.got = cross(d, send, 0, mix)
        self.at = 0
        self.parts = None

    def step(self, *deps):
        self.at += 1
        n = self.d.bits
        if self.at < n:
            keep, send = fold(self.keep, self.got, deps)
            self.keep = keep
            self.got = cross(self.d, send, self.at, self.mix)
            return keep
        if self.at == n:
            (keep,) = fold(self.keep, self.got, deps)
            self.parts = [keep]
            self.got = cross(self.d, keep, n - 1, self.mix)
            return keep
        self.parts.append(self.got)
        if self.at < 2 * n:
            full = join(self.parts, deps)
            self.got = cross(self.d, full, 2 * n - 1 - self.at, self.mix)
            return full
        return self.got

    def finish(self):
        while self.at < 2 * self.d.bits:
            self.step()
        return self.parts


def all_to_all(values):
    return lax.all_to_all(values, "ctx", 0, 0)


def key_table(d, parent_ids, depth_offsets):
    segs = parent_ids.shape[0] // lax.axis_size("fsdp")
    start = lax.axis_index("fsdp") * segs
    parents = lax.dynamic_slice_in_dim(parent_ids, start, segs) - start
    depths = lax.dynamic_slice_in_dim(depth_offsets, start, segs).astype(F32)
    ids = jnp.arange(segs, dtype=jnp.int32)
    reach = jnp.maximum(
        (parents[:, None] == ids[None, :]).astype(F32), (ids[:, None] == ids[None, :]).astype(F32)
    )
    for _ in range((segs - 1).bit_length()):
        reach = jnp.minimum(jnp.dot(reach, reach), 1.0)
    head = lax.axis_index("tp") * d.lh + lax.axis_index("ctx") // d.g
    slope = jnp.exp2(-(head + 1).astype(F32))
    level = jnp.where(reach > 0.5, slope * (depths[None, :] - depths[:, None]), MASKED)
    spots = slope * jnp.arange(SEG, dtype=jnp.int32).astype(F32)
    return (level[:, :, None] + spots[None, None, :]).reshape(segs, segs * SEG)


def on_device(tokens, qkv_weight, out_weight, up_weight, down_weight, qv_bias, up_bias,
              norm_gains, row_biases, parent_ids, depth_offsets, cotangent):
    d = Dims(tokens, qkv_weight, up_weight)
    x = lax.axis_index("fsdp")
    c = lax.axis_index("ctx")
    t = lax.axis_index("tp")
    first = [jnp.where(t == 0, way(d, 0, k), way(d, 1, k)) for k in range(d.bits)]
    bit = (c >> first[0]) % 2
    sc = jnp.stack([x, bit, c, *first, *range(d.bits)]).astype(jnp.int32)
    w_qkv = qkv_weight.transpose(0, 2, 1, 3)
    tiles = d.F // FT
    half = tiles // 2

    class Pieces:
        def __init__(self, layer, deps):
            def over(values):
                first = swap(values, "fsdp")
                return first, cross(d, first, 0)

            tile = (None, FT, FT)
            qkv = take(sc, w_qkv, (None, 3, d.Q, d.W), lambda n, b: (layer, 0, b, 0),
                       (3, d.Q, d.W), deps=deps)
            out = take(sc, out_weight, (None, d.W // 2, d.H), lambda n, b: (layer, b, 0),
                       (d.W // 2, d.H), deps=(qkv,))
            up_a = take(sc, up_weight, tile, lambda n, b: (layer, 0, b), (FT, FT), deps=(out,))
            up_b = take(sc, up_weight, tile, lambda n, b: (layer, 0, half + b), (FT, FT),
                        deps=(up_a,))
            dn_a = take(sc, down_weight, tile, lambda n, b: (layer, b, 0), (FT, FT), deps=(up_b,))
            dn_b = take(sc, down_weight, tile, lambda n, b: (layer, half + b, 0), (FT, FT),
                        deps=(dn_a,))
            self.last = dn_b
            self.qkv, self.out = over(qkv), over(out)
            self.dn_a, self.dn_b = over(dn_a), over(dn_b)
            self.up_a, self.up_b = over(up_a), over(up_b)
            self.up = (*self.up_a, *self.up_b)
            self.down = (*self.dn_a, *self.dn_b)

    p0 = Pieces(0, ())
    p = [p0]
    kb = key_table(d, parent_ids, depth_offsets)

    def both(rows):
        got = swap(rows, "tp")
        return jnp.where(
            t == 0,
            jnp.concatenate([rows, got], axis=0),
            jnp.concatenate([got, rows], axis=0),
        )

    def row(values):
        return values.reshape(1, -1)

    def swapped(values):
        return swap(values, "tp")

    def fsdp(values):
        return swap(values, "fsdp")

    class Kept:
        pass

    def forward(layer, state, needs):
        k = kept[layer]
        before = [needs(n) for n in range(1)]
        k.hidden, k.n_o, n_s, chunks = qkv_forward(
            d, layer, sc, state, row(norm_gains[layer, 0]), row(row_biases[layer, 0]),
            w_qkv, p[layer].qkv, qv_bias[layer], deps=before[0])
        k.n_r = fsdp(n_s)
        if layer == 0:
            p.append(Pieces(1, (k.hidden,)))
        before += [needs(n) for n in range(1, 3)]
        k.chunks = all_to_all(chunks)
        outs = all_to_all(attend_forward(d, sc, kb, k.chunks, deps=before[1]))
        k.ctx, part = out_forward(d, layer, sc, out_weight, p[layer].out, outs, deps=before[2])
        k.ctx_r = fsdp(k.ctx)
        before.append(needs(3))
        k.middle, k.n2_o, k.act_p, k.act_q, k.dg, part2 = ffn_forward(
            d, layer, sc, k.hidden, part, swapped(part), row(row_biases[layer, 1]),
            row(norm_gains[layer, 1]), row(row_biases[layer, 2]), up_weight,
            p[layer].up, row(up_bias[layer]), down_weight, p[layer].down, deps=before[3])
        state = (k.middle, part2, swapped(part2), row(row_biases[layer, 3]))
        k.act_pr, k.act_qr = fsdp(k.act_p), fsdp(k.act_q)
        return state

    state = both(tokens)
    p0 = p[0]
    kept = [Kept() for _ in range(LAYERS)]
    k0, k1 = kept
    state = forward(0, state, lambda n: (
        (p0.out[0], p0.up_a[0], p0.last) if n == 0
        else (p0.out[1], p0.up_a[1], p0.up_b[0], p0.dn_a[0], p[1].last) if n == 1
        else (p0.dn_b[0], p[1].qkv[0], p[1].out[0]) if n == 2
        else ()
    ))
    p1 = p[1]
    state = forward(1, state, lambda n: (
        (p1.up_a[0],) if n == 0
        else (p1.out[1], p1.up_a[1], p1.up_b[0], p1.dn_a[0]) if n == 1
        else (p1.dn_b[0], k1.n_r, k0.act_pr) if n == 2
        else ()
    ))
    own_rows = tokens.shape[0]

    def mine(values):
        return lax.dynamic_slice_in_dim(values, t * own_rows, own_rows, 0)

    output = mine(state[0]) + (
        (mine(state[1]).astype(F32) + mine(state[2]).astype(F32)) + state[3]
    )
    output = output.astype(BF)
    grad = both(cotangent)
    sums = [None] * LAYERS
    def grad_ffn(k, more, mix, deps=()):
        ins = (k.n2_o, k.act_p, k.act_pr, k.act_q, k.act_qr, k.xba, k.xba_r, k.xbb, k.xbb_r,
               k.db_o)
        jobs = []
        for f in range(tiles):
            at = (5, 1) if f == 0 else (7, f - 1)
            jobs.append(((0, None), at, (2, 0), (at[0] + 1, at[1])))
        for f in range(tiles):
            at = (1, 1 + f) if f < half else (3, f - half)
            jobs.append((at, (9, None), (at[0] + 1, at[1]), (6, 0)))
        if more:
            ins += (k.ctx, k.ctx_r, k.da_o, k.da_r)
            jobs += [((10, None), (12, None), (11, None), (13, None))]
        return Sum(d, mix, *weight_grad(d, "ffn", sc, ins, jobs, mix, deps=deps))

    def grad_qkv(k, more, mix, flat=None, deps=()):
        ins = (k.n_o, k.n_r, k.xc, k.xc_r)
        jobs = [((0, None), (2, n), (1, None), (3, n)) for n in range(3)]
        if more:
            ins += (k.ctx, k.da_o, k.ctx_r, k.da_r)
            jobs += [((4, None), (5, None), (6, None), (7, None))]
        return Sum(d, mix, *weight_grad(d, "qkv", sc, ins, jobs, mix, flat, deps))

    def back_ffn(layer, k, grad, deps=()):
        k.db_o, k.xba, k.xbb, k.usum, k.bsum, part = ffn_backward(
            d, layer, sc, grad, k.dg, up_weight, p[layer].up, down_weight, p[layer].down,
            deps=deps)
        k.xba_r, k.xbb_r = fsdp(k.xba), fsdp(k.xbb)
        return part

    def back_context(layer, k, grad, part, deps=()):
        k.dmid, k.da_o, k.da_s, k.gsum2, k.ssum2, k.asum, dchunks = context_backward(
            d, layer, sc, grad, part, swapped(part), k.middle, row(norm_gains[layer, 1]),
            out_weight, p[layer].out, deps=deps)
        k.da_r = fsdp(k.da_s)
        return dchunks

    def back_qkv(layer, k, dparts, deps=()):
        k.xc, k.qvsum, part = qkv_backward(
            d, layer, sc, w_qkv, p[layer].qkv, dparts, deps=deps)
        k.xc_r = fsdp(k.xc)
        return part

    def back_input(layer, k, part, deps=()):
        grad, k.gsum1, k.ssum1 = input_backward(
            d, k.dmid, part, swapped(part), k.hidden, row(norm_gains[layer, 0]), deps=deps)
        sums[layer] = (k.qvsum, k.usum, k.gsum1, k.gsum2, k.ssum1, k.asum, k.ssum2, k.bsum)
        return grad

    total = LAYERS * (2 * d.W + d.F + 6 * d.D)

    def small_sums():
        flat = jnp.concatenate([v.reshape(-1) for layer in sums for v in layer])
        return jnp.pad(flat, (0, d.C * EXTRA * FT - total)).reshape(d.C, EXTRA, FT)

    part = back_ffn(1, k1, grad, (k0.act_qr, k1.ctx_r))
    dchunks = back_context(1, k1, grad, part, (state[2],))
    dback = attend_backward(d, sc, kb, k1.chunks, all_to_all(dchunks),
                            deps=(k1.act_pr, k1.act_qr))
    dparts = all_to_all(dback)
    f1 = grad_ffn(k1, False, True, (dback,))
    part = back_qkv(1, k1, dparts, (f1.keep,))
    grad = back_input(1, k1, part)
    part = back_ffn(0, k0, grad)
    a = f1.step(part)
    dchunks = back_context(0, k0, grad, part, (a, k1.xc_r))
    q1 = grad_qkv(k1, True, True, None, (dchunks,))
    a = f1.step(q1.keep)
    dback = attend_backward(d, sc, kb, k0.chunks, all_to_all(dchunks),
                            deps=(a, k0.xba_r, k0.ctx_r, k0.n_r))
    dparts = all_to_all(dback)
    f0 = grad_ffn(k0, True, True, (dback,))
    part = back_qkv(0, k0, dparts, (f0.keep,))
    grad = back_input(0, k0, part)
    flat = small_sums()
    flat = flat + swap(flat, "fsdp")
    q0 = grad_qkv(k0, False, False, flat, (grad,))
    a = q0.keep
    ffn_kinds = (("cols", tiles), ("mats", tiles))
    qkv_kinds = (("mats", 3), ("mats", 1))
    last = 2 * d.bits - 1
    for unit in (f1, f0, q1, q0, f1, f0, q1, f1, q0, f0, q1, q0, f0, q1, q0):
        if unit.at < last:
            a = unit.step(a)
    while f1.at < last:
        a = f1.step(a)
    g_ffn = place(d, 1, sc, f1, None, ffn_kinds, "ffn", (a,))
    a = g_ffn[0]
    for unit in (q1, q0, f0):
        while unit.at < last:
            a = unit.step(a)
    g_qkv = place(d, 1, sc, q1, None, qkv_kinds, "qkv", (a,))
    a = g_qkv[0]
    g_up, g_down, g_out = place(d, 0, sc, f0, (*g_ffn, g_qkv[1]), (*ffn_kinds, ("mats", 1)),
                                "ffn", (a,))
    g_qkv, qv_grad, up_grad, gain_grad, bias_grad = place(d, 0, sc, q0, (g_qkv[0],), (("mats", 3),), "qkv", (g_up,))
    return (
        output,
        mine(grad),
        g_qkv.transpose(0, 2, 1, 3),
        g_out.reshape(LAYERS, d.W, d.H),
        g_up.reshape(LAYERS, d.H, d.F),
        g_down.reshape(LAYERS, d.F, d.H),
        qv_grad,
        up_grad,
        gain_grad,
        bias_grad,
    )


def solution(mesh):
    in_specs = (
        P(("fsdp", "ctx", "tp"), None),
        P(None, "fsdp", None, "tp"),
        P(None, "tp", "fsdp"),
        P(None, "fsdp", "tp"),
        P(None, "tp", "fsdp"),
        P(None, None, "tp"),
        P(None, "tp"),
        P(),
        P(),
        P(),
        P(),
        P(("fsdp", "ctx", "tp"), None),
    )
    out_specs = (
        P(("fsdp", "ctx", "tp"), None),
        P(("fsdp", "ctx", "tp"), None),
        P(None, "fsdp", None, "tp"),
        P(None, "tp", "fsdp"),
        P(None, "fsdp", "tp"),
        P(None, "tp", "fsdp"),
        P(None, None, "tp"),
        P(None, "tp"),
        P(),
        P(),
    )
    return jax.shard_map(
        on_device, mesh=mesh, in_specs=in_specs, out_specs=out_specs, check_vma=False
    )
```

```python
import functools

import jax
import jax.numpy as jnp
from jax import lax
from jax.experimental import pallas as pl
from jax.experimental.pallas import tpu as pltpu
from jax.sharding import PartitionSpec as P

HEAD_DIM = 128
LAYERS = 2
SEG = 128
EPSILON = 1e-05
MASKED = -1e30
SCALE = HEAD_DIM ** (-0.5)
GELU_A = 0.7978845608028654
GELU_B = 0.044715
BF = jnp.bfloat16
F32 = jnp.float32
VLIM = 56 * 1024 * 1024

NN = (((1,), (0,)), ((), ()))
NT = (((1,), (1,)), ((), ()))
TN = (((0,), (0,)), ((), ()))


def mm(a, b, dims=NN):
    return lax.dot_general(a, b, dims, preferred_element_type=F32)


def sds(shape, dtype):
    return jax.ShapeDtypeStruct(shape, dtype)


VSPEC = pl.BlockSpec(memory_space=pltpu.VMEM)
SSPEC = pl.BlockSpec(memory_space=pltpu.SMEM)


def cost(flops, nbytes):
    return pl.CostEstimate(flops=int(flops), bytes_accessed=int(nbytes), transcendentals=0)


def kernel_call(body, args, in_specs, out_specs, out_shape, name, scratch=(), grid=None,
                deps=(), work=None, aliases=None):
    count, extra = len(args), len(deps)

    def ordered(*refs):
        body(*refs[:count], *refs[count + extra :])

    kwargs = {} if grid is None else {"grid": grid}
    return pl.pallas_call(
        ordered,
        in_specs=list(in_specs) + [pl.BlockSpec(memory_space=pl.ANY)] * extra,
        out_specs=out_specs,
        out_shape=out_shape,
        scratch_shapes=list(scratch),
        input_output_aliases=aliases or {},
        compiler_params=pltpu.CompilerParams(vmem_limit_bytes=VLIM),
        cost_estimate=work,
        name=name,
        **kwargs,
    )(*args, *deps)


def norm_rows(v):
    centered = v - jnp.mean(v, axis=-1, keepdims=True)
    rstd = lax.rsqrt(jnp.mean(centered * centered, axis=-1, keepdims=True) + EPSILON)
    return centered * rstd, rstd


def norm_back(d, v, gain):
    xhat, rstd = norm_rows(v)
    dx = d * gain
    back = rstd * (
        dx
        - jnp.mean(dx, axis=-1, keepdims=True)
        - xhat * jnp.mean(dx * xhat, axis=-1, keepdims=True)
    )
    d_gain = jnp.sum(d * xhat, axis=0, keepdims=True)
    d_shift = jnp.sum(d, axis=0, keepdims=True)
    return back, d_gain, d_shift


class Dims:
    def __init__(self, tokens, qkv_weight, up_weight):
        self.tp = lax.axis_size("tp")
        self.C = lax.axis_size("ctx")
        self.T = tokens.shape[0] * self.tp
        self.D = tokens.shape[1]
        self.H = self.D // lax.axis_size("fsdp")
        self.Q = self.H // 2
        self.W = qkv_weight.shape[3]
        self.F = up_weight.shape[2]
        self.lh = self.W // HEAD_DIM
        self.g = self.C // self.lh
        self.rq = self.T // self.g
        self.chunk = self.rq + 2 * self.T
        self.bits = self.C.bit_length() - 1


def offs(sc, d):
    x = sc[0]
    y = sc[1]
    own = pl.multiple_of(x * d.H, d.H)
    oth = pl.multiple_of((1 - x) * d.H, d.H)
    first = pl.multiple_of((1 - x) * d.H + y * d.Q, d.Q)
    second = pl.multiple_of((1 - x) * d.H + (1 - y) * d.Q, d.Q)
    return own, oth, first, second


def spot_of(d, chip):
    row, head = (chip % d.g) * d.rq, (chip // d.g) * HEAD_DIM
    return slice(row, row + d.rq), slice(head, head + HEAD_DIM)


def qkv_body(d, first, *refs):
    if first:
        sc, hid, gain, shift, w, w1, w2, qvb = refs[:8]
        rest = refs[8:]
        hidden = hid[...].astype(F32)
    else:
        sc, mid, pa, pb, bias, gain, shift, w, w1, w2, qvb = refs[:11]
        rest = refs[11:]
        hidden = mid[...] + ((pa[...].astype(F32) + pb[...].astype(F32)) + bias[...])
    h_out, no_out, ns_out, chunks, n_out, scr = rest
    own, oth, p1, p2 = offs(sc, d)
    h_out[...] = hidden
    xhat, _ = norm_rows(hidden)
    n_out[...] = (xhat * gain[...] + shift[...]).astype(BF)
    ns_out[...] = n_out[:, pl.ds(oth, d.H)]
    a0 = n_out[:, pl.ds(own, d.H)]
    no_out[...] = a0
    a1 = n_out[:, pl.ds(p1, d.Q)]
    a2 = n_out[:, pl.ds(p2, d.Q)]
    for n in range(3):
        proj = mm(a0, w[n]) + mm(a1, w1[n]) + mm(a2, w2[n])
        if n == 0:
            proj = proj + qvb[0:1, :]
        if n == 2:
            proj = proj + qvb[1:2, :]
        scr[n] = proj.astype(BF)
    for to in range(d.C):
        row, col = spot_of(d, to)
        chunks[to, 0 : d.rq, :] = scr[0, row, col]
        chunks[to, d.rq : d.rq + d.T, :] = scr[1, :, col]
        chunks[to, d.rq + d.T :, :] = scr[2, :, col]


def whole(shape):
    return pl.BlockSpec(shape, lambda *_: (0,) * len(shape))


def piece_specs(shape, pieces, axis):
    if pieces[0] is not pieces[1]:
        return [whole(shape), whole(shape)]
    second = tuple(1 if k == axis else 0 for k in range(len(shape)))
    return [whole(shape), pl.BlockSpec(shape, lambda *_: second)]


def qkv_forward(d, layer, sc, hid, gain, shift, w, pieces, qvb, deps=()):
    first = not isinstance(hid, tuple)
    hid = (hid,) if first else hid
    wspec = pl.BlockSpec((None, 3, d.H, d.W), lambda i: (layer, 0, 0, 0))
    in_specs = [SSPEC] + [whole(a.shape) for a in hid]
    in_specs += [whole(gain.shape), whole(shift.shape), wspec]
    in_specs += piece_specs((3, d.Q, d.W), pieces, 1) + [whole(qvb.shape)]
    outs = [sds((d.T, d.D), F32), sds((d.T, d.H), BF), sds((d.T, d.H), BF)]
    outs += [sds((d.C, d.chunk, HEAD_DIM), BF)]
    return kernel_call(
        functools.partial(qkv_body, d, first),
        (sc, *hid, gain, shift, w, *pieces, qvb,),
        grid=(1,),
        in_specs=in_specs,
        out_specs=[whole(o.shape) for o in outs],
        out_shape=outs,
        scratch=[pltpu.VMEM((d.T, d.D), BF), pltpu.VMEM((3, d.T, d.W), BF)],
        work=cost(2 * d.T * d.D * 3 * d.W, 8e6),
        name="qkv_forward",
        deps=deps,
    )


def load_chunks(d, sc, chunks, qs, ks, vs):
    qs[...] = chunks[:, 0 : d.rq, :]
    ks[...] = chunks[:, d.rq : d.rq + d.T, :]
    vs[...] = chunks[:, d.rq + d.T :, :]


def score_block(d, sc, kb, q, k, s, ext):
    part = lax.rem(sc[2], d.g)
    seg = s * (d.T // SEG) + lax.div(part * d.rq, SEG)
    scores = mm(q, k, NT) * SCALE + kb[pl.ds(seg, 1), 0:ext]
    col = lax.broadcasted_iota(jnp.int32, (d.rq, ext), 1) - s * d.T
    row = lax.broadcasted_iota(jnp.int32, (d.rq, ext), 0) + part * d.rq
    return jnp.where(col <= row, scores, MASKED)


UNROLL = 8
SHIFT = 3


def each_source(d, one):
    if d.C <= UNROLL:
        for s in range(d.C):
            one(s, s + 1)
    else:
        lax.fori_loop(0, d.C, lambda s, carry: (one(s, d.C), carry)[1], 0)


def attend_body(d, *refs):
    sc, kb, chunks, cs, qs, ks, vs = refs
    load_chunks(d, sc, chunks, qs, ks, vs)
    def one(s, seen):
        ext = seen * d.T
        k = ks[0:seen].reshape(ext, HEAD_DIM)
        v = vs[0:seen].reshape(ext, HEAD_DIM)
        scores = score_block(d, sc, kb, qs[s], k, s, ext)
        e = jnp.exp(scores - jnp.max(scores, axis=-1, keepdims=True))
        total = jnp.sum(e, axis=-1, keepdims=True)
        cs[s] = (mm(e.astype(BF), v) / total).astype(BF)

    each_source(d, one)


def attend_forward(d, sc, kb, chunks, deps=()):
    return kernel_call(
        functools.partial(attend_body, d),
        (sc, kb, chunks,),
        in_specs=[SSPEC] + [VSPEC] * 2,
        out_specs=VSPEC,
        out_shape=sds((d.C, d.rq, HEAD_DIM), BF),
        scratch=[
            pltpu.VMEM((d.C, d.rq, HEAD_DIM), BF),
            pltpu.VMEM((d.C, d.T, HEAD_DIM), BF),
            pltpu.VMEM((d.C, d.T, HEAD_DIM), BF),
        ],
        work=cost(2 * d.C * d.rq * d.C * d.T * HEAD_DIM * 2, 3e6),
        name="attend_forward",
        deps=deps,
    )


def out_body(d, *refs):
    sc, w, w1, w2, chunks, ctx, part = refs
    for src in range(d.C):
        ctx[spot_of(d, src)] = chunks[src]
    own, oth, _, _ = offs(sc, d)
    half = d.W // 2
    k1 = pl.multiple_of(sc[1] * half, half)
    k2 = pl.multiple_of((1 - sc[1]) * half, half)
    part[:, pl.ds(own, d.H)] = mm(ctx[...], w[...]).astype(BF)
    part[:, pl.ds(oth, d.H)] = (
        mm(ctx[:, pl.ds(k1, half)], w1[...]) + mm(ctx[:, pl.ds(k2, half)], w2[...])
    ).astype(BF)


def out_forward(d, layer, sc, w, pieces, chunks, deps=()):
    wspec = pl.BlockSpec((None, d.W, d.H), lambda i: (layer, 0, 0))
    outs = [sds((d.T, d.W), BF), sds((d.T, d.D), BF)]
    return kernel_call(
        functools.partial(out_body, d),
        (sc, w, *pieces, chunks,),
        grid=(1,),
        in_specs=[SSPEC, wspec] + piece_specs((d.W // 2, d.H), pieces, 0)
        + [whole(chunks.shape)],
        out_specs=[whole(o.shape) for o in outs],
        out_shape=outs,
        work=cost(2 * d.T * d.D * d.W, 3e6),
        name="out_forward",
        deps=deps,
    )


FT = 512


def tile_of(f, sc, tiles, refs, use):
    half = tiles // 2
    mine = lax.rem(f, half) == sc[1]
    for number, (came, then) in enumerate((refs[:2], refs[2:])):
        here = lax.div(f, half) == number

        @pl.when(jnp.logical_and(here, mine))
        def _():
            use(came)

        @pl.when(jnp.logical_and(here, jnp.logical_not(mine)))
        def _():
            use(then)


def ffn_body(d, tiles, sc, hid, pa, pb, bias, gain, shift,
             u, u1, u2, u3, u4, ub, w, w1, w2, w3, w4,
             mid, no, act_p, act_q, dg, part, n2, acc, pre):
    f = pl.program_id(0)
    own, oth, _, _ = offs(sc, d)

    @pl.when(f == 0)
    def _():
        m = hid[...] + ((pa[...].astype(F32) + pb[...].astype(F32)) + bias[...])
        mid[...] = m
        xhat, _ = norm_rows(m)
        n2[...] = (xhat * gain[...] + shift[...]).astype(BF)
        no[...] = n2[:, pl.ds(own, d.H)]
        act_p[0] = n2[:, pl.ds(oth, d.H)]
        acc[...] = jnp.zeros_like(acc)

    def up(ref):
        pre[...] = mm(act_p[0], ref[...])

    tile_of(f, sc, tiles, (u1, u2, u3, u4), up)
    v = pre[...] + mm(no[...], u[...]) + ub[...]
    sq = v * v
    th = jnp.tanh(GELU_A * v * (1.0 + GELU_B * sq))
    half = 0.5 * (1.0 + th)
    a = (v * half).astype(BF)

    @pl.when(f < tiles // 2)
    def _():
        act_p[1 + f] = a

    @pl.when(f >= tiles // 2)
    def _():
        act_q[f - tiles // 2] = a

    dg[...] = (
        half + 0.5 * v * (1.0 - th * th) * (GELU_A * (1.0 + 3.0 * GELU_B * sq))
    ).astype(BF)
    acc[0] += mm(a, w[...])

    def down(ref):
        acc[1] += mm(a, ref[...])

    tile_of(f, sc, tiles, (w1, w2, w3, w4), down)

    @pl.when(f == tiles - 1)
    def _():
        part[:, pl.ds(own, d.H)] = acc[0].astype(BF)
        part[:, pl.ds(oth, d.H)] = acc[1].astype(BF)


def ffn_specs(d, layer):
    u = pl.BlockSpec((None, d.H, FT), lambda f: (layer, 0, f))
    w = pl.BlockSpec((None, FT, d.H), lambda f: (layer, f, 0))
    return [u] + [whole((d.H, FT))] * 4, [w] + [whole((FT, d.H))] * 4


def ffn_forward(d, layer, sc, hid, pa, pb, bias, gain, shift,
                up_w, up_p, ub, dn_w, dn_p, deps=()):
    tiles = d.F // FT
    us, ws = ffn_specs(d, layer)
    side = whole((d.T, d.H))
    col = pl.BlockSpec((d.T, FT), lambda f: (0, f))
    row = whole((1, d.D))
    full = whole((d.T, d.D))
    act_p = sds((1 + tiles // 2, d.T, FT), BF)
    act_q = sds((tiles // 2, d.T, FT), BF)
    return kernel_call(
        functools.partial(ffn_body, d, tiles),
        (sc, hid, pa, pb, bias, gain, shift, up_w, *up_p, ub, dn_w, *dn_p),
        [SSPEC, full, full, full, row, row, row, *us,
         pl.BlockSpec((1, FT), lambda f: (0, f)), *ws],
        [full, side, whole(act_p.shape), whole(act_q.shape), col, full],
        [sds((d.T, d.D), F32), sds((d.T, d.H), BF), act_p, act_q,
         sds((d.T, d.F), BF), sds((d.T, d.D), BF)],
        "ffn_forward",
        scratch=[pltpu.VMEM((d.T, d.D), BF), pltpu.VMEM((2, d.T, d.H), F32),
                 pltpu.VMEM((d.T, FT), F32)],
        grid=(tiles,), deps=deps, work=cost(4 * d.T * d.D * d.F, 14e6))


def ffn_back_body(d, tiles, sc, grad, dg, u, u1, u2, u3, u4, w, w1, w2, w3, w4,
                  dbo, xba, xbb, usum, bsum, part, acc, dact):
    f = pl.program_id(0)
    own, oth, _, _ = offs(sc, d)

    @pl.when(f == 0)
    def _():
        dbo[...] = grad[:, pl.ds(own, d.H)].astype(BF)
        xba[0] = grad[:, pl.ds(oth, d.H)].astype(BF)
        bsum[...] = jnp.sum(grad[...].astype(BF).astype(F32), axis=0, keepdims=True)
        acc[...] = jnp.zeros_like(acc)

    def down(ref):
        dact[...] = mm(xba[0], ref[...], NT)

    tile_of(f, sc, tiles, (w1, w2, w3, w4), down)
    da = dact[...] + mm(dbo[...], w[...], NT)
    dp = (da * dg[...].astype(F32)).astype(BF)

    @pl.when(f == 0)
    def _():
        xba[1] = dp

    @pl.when(f > 0)
    def _():
        xbb[f - 1] = dp

    usum[...] = jnp.sum(dp.astype(F32), axis=0, keepdims=True)
    acc[0] += mm(dp, u[...], NT)

    def up(ref):
        acc[1] += mm(dp, ref[...], NT)

    tile_of(f, sc, tiles, (u1, u2, u3, u4), up)

    @pl.when(f == tiles - 1)
    def _():
        part[:, pl.ds(own, d.H)] = acc[0].astype(BF)
        part[:, pl.ds(oth, d.H)] = acc[1].astype(BF)


def ffn_backward(d, layer, sc, grad, dg, up_w, up_p, dn_w, dn_p, deps=()):
    tiles = d.F // FT
    us, ws = ffn_specs(d, layer)
    side = whole((d.T, d.H))
    col = pl.BlockSpec((d.T, FT), lambda f: (0, f))
    full = whole((d.T, d.D))
    xba = sds((2, d.T, FT), BF)
    xbb = sds((tiles - 1, d.T, FT), BF)
    return kernel_call(
        functools.partial(ffn_back_body, d, tiles),
        (sc, grad, dg, up_w, *up_p, dn_w, *dn_p),
        [SSPEC, full, col, *us, *ws],
        [side, whole(xba.shape), whole(xbb.shape),
         pl.BlockSpec((1, FT), lambda f: (0, f)), whole((1, d.D)), full],
        [sds((d.T, d.H), BF), xba, xbb,
         sds((1, d.F), F32), sds((1, d.D), F32), sds((d.T, d.D), BF)],
        "ffn_backward",
        scratch=[pltpu.VMEM((2, d.T, d.H), F32), pltpu.VMEM((d.T, FT), F32)],
        grid=(tiles,), deps=deps, work=cost(4 * d.T * d.D * d.F, 14e6))


def context_back_body(d, *refs):
    sc, grad, pa, pb, mid, gain, w, w1, w2 = refs[:9]
    dmid, dao, das, gsum, ssum, asum, chunks, da, dctx = refs[9:]
    own, oth, _, _ = offs(sc, d)
    back, g, s = norm_back(pa[...].astype(F32) + pb[...].astype(F32), mid[...], gain[...])
    gsum[...] = g
    ssum[...] = s
    total = grad[...].astype(F32) + back
    dmid[...] = total
    da[...] = total.astype(BF)
    dao[...] = da[:, pl.ds(own, d.H)]
    das[...] = da[:, pl.ds(oth, d.H)]
    asum[...] = jnp.sum(da[...].astype(F32), axis=0, keepdims=True)
    half = d.W // 2
    k1 = pl.multiple_of(sc[1] * half, half)
    k2 = pl.multiple_of((1 - sc[1]) * half, half)
    dctx[...] = mm(da[:, pl.ds(own, d.H)], w[...], NT)
    dctx[:, pl.ds(k1, half)] += mm(da[:, pl.ds(oth, d.H)], w1[...], NT)
    dctx[:, pl.ds(k2, half)] += mm(da[:, pl.ds(oth, d.H)], w2[...], NT)
    for to in range(d.C):
        chunks[to] = dctx[spot_of(d, to)].astype(BF)


def context_backward(d, layer, sc, grad, pa, pb, mid, gain, w, pieces, deps=()):
    wspec = pl.BlockSpec((None, d.W, d.H), lambda i: (layer, 0, 0))
    outs = [sds((d.T, d.D), F32), sds((d.T, d.H), BF), sds((d.T, d.H), BF)]
    outs += [sds((1, d.D), F32)] * 3 + [sds((d.C, d.rq, HEAD_DIM), BF)]
    return kernel_call(
        functools.partial(context_back_body, d),
        (sc, grad, pa, pb, mid, gain, w, *pieces,),
        grid=(1,),
        in_specs=[SSPEC] + [whole(a.shape) for a in (grad, pa, pb, mid, gain)]
        + [wspec] + piece_specs((d.W // 2, d.H), pieces, 0),
        out_specs=[whole(o.shape) for o in outs],
        out_shape=outs,
        scratch=[pltpu.VMEM((d.T, d.D), BF), pltpu.VMEM((d.T, d.W), F32)],
        work=cost(2 * d.T * d.D * d.W, 6e6),
        name="context_backward",
        deps=deps,
    )


def attend_back_body(d, *refs):
    sc, kb, chunks, cs, outs, qs, ks, vs, dks, dvs = refs
    load_chunks(d, sc, chunks, qs, ks, vs)
    dks[...] = jnp.zeros_like(dks)
    dvs[...] = jnp.zeros_like(dvs)
    def one(s, seen):
        ext = seen * d.T
        k = ks[0:seen].reshape(ext, HEAD_DIM)
        v = vs[0:seen].reshape(ext, HEAD_DIM)
        q = qs[s]
        dc = cs[s]
        scores = score_block(d, sc, kb, q, k, s, ext)
        e = jnp.exp(scores - jnp.max(scores, axis=-1, keepdims=True))
        p = e / jnp.sum(e, axis=-1, keepdims=True)
        dp = mm(dc, v, NT)
        ds = (p * (dp - jnp.sum(p * dp, axis=-1, keepdims=True))).astype(BF)
        outs[s, 0 : d.rq, :] = (mm(ds, k) * SCALE).astype(BF)
        dks[0:seen] += mm(ds, q, TN).reshape(seen, d.T, HEAD_DIM)
        dvs[0:seen] += mm(p.astype(BF), dc, TN).reshape(seen, d.T, HEAD_DIM)

    each_source(d, one)
    outs[:, d.rq : d.rq + d.T, :] = (dks[...] * SCALE).astype(BF)
    outs[:, d.rq + d.T :, :] = dvs[...].astype(BF)


def attend_backward(d, sc, kb, chunks, dchunks, deps=()):
    return kernel_call(
        functools.partial(attend_back_body, d),
        (sc, kb, chunks, dchunks,),
        in_specs=[SSPEC] + [VSPEC] * 3,
        out_specs=VSPEC,
        out_shape=sds((d.C, d.chunk, HEAD_DIM), BF),
        scratch=[
            pltpu.VMEM((d.C, d.rq, HEAD_DIM), BF),
            pltpu.VMEM((d.C, d.T, HEAD_DIM), BF),
            pltpu.VMEM((d.C, d.T, HEAD_DIM), BF),
            pltpu.VMEM((d.C, d.T, HEAD_DIM), F32),
            pltpu.VMEM((d.C, d.T, HEAD_DIM), F32),
        ],
        work=cost(5 * d.C * d.rq * d.C * d.T * HEAD_DIM * 2, 4e6),
        name="attend_backward",
        deps=deps,
    )


def qkv_back_body(d, sc, w, w1, w2, chunks, xb, qvsum, part, dk, dv):
    dk[...] = jnp.zeros_like(dk)
    dv[...] = jnp.zeros_like(dv)
    for src in range(d.C):
        row, col = spot_of(d, src)
        xb[0, row, col] = chunks[src, 0 : d.rq, :]
        dk[:, col] += chunks[src, d.rq : d.rq + d.T, :].astype(F32)
        dv[:, col] += chunks[src, d.rq + d.T :, :].astype(F32)
    xb[1] = dk[...].astype(BF)
    xb[2] = dv[...].astype(BF)
    qvsum[0:1, :] = jnp.sum(xb[0].astype(F32), axis=0, keepdims=True)
    qvsum[1:2, :] = jnp.sum(xb[2].astype(F32), axis=0, keepdims=True)
    own, _, p1, p2 = offs(sc, d)
    for ref, at, width in ((w, own, d.H), (w1, p1, d.Q), (w2, p2, d.Q)):
        total = mm(xb[0], ref[0], NT) + mm(xb[1], ref[1], NT) + mm(xb[2], ref[2], NT)
        part[:, pl.ds(at, width)] = total.astype(BF)


def qkv_backward(d, layer, sc, w, pieces, chunks, deps=()):
    wspec = pl.BlockSpec((None, 3, d.H, d.W), lambda i: (layer, 0, 0, 0))
    outs = [sds((3, d.T, d.W), BF), sds((2, d.W), F32), sds((d.T, d.D), BF)]
    return kernel_call(
        functools.partial(qkv_back_body, d),
        (sc, w, *pieces, chunks),
        [SSPEC, wspec] + [whole((3, d.Q, d.W))] * 2 + [whole(chunks.shape)],
        [whole(o.shape) for o in outs],
        outs,
        "qkv_backward",
        scratch=[pltpu.VMEM((d.T, d.W), F32)] * 2,
        grid=(1,), deps=deps, work=cost(2 * d.T * d.D * 3 * d.W, 7e6))


def input_back_body(dmid, pa, pb, hid, gain, grad, gsum, ssum):
    back, g, s = norm_back(pa[...].astype(F32) + pb[...].astype(F32), hid[...], gain[...])
    grad[...] = dmid[...] + back
    gsum[...] = g
    ssum[...] = s


def input_backward(d, dmid, pa, pb, hid, gain, deps=()):
    return kernel_call(
        input_back_body,
        (dmid, pa, pb, hid, gain,),
        in_specs=[VSPEC] * 5,
        out_specs=[VSPEC] * 3,
        out_shape=[sds((d.T, d.D), F32)] + [sds((1, d.D), F32)] * 2,
        work=cost(3e6, 5e6),
        name="input_backward",
        deps=deps,
    )


def spot_bits(value, shifts, bits):
    out = 0
    for k in range(bits):
        bit = lax.bitwise_and(lax.shift_right_logical(value, shifts[k]), 1)
        out = out + bit * (1 << (bits - 1 - k))
    return out


EXTRA = 16


def shift_at(d, mix):
    return SHIFT if mix else SHIFT + d.bits


def wgrad_body(d, tiles, mix, flat, sc, *refs):
    ins = refs[:-2]
    keep, send = refs[-2:]
    c = sc[2]
    shifts = [sc[shift_at(d, mix) + k] for k in range(d.bits)]
    rb = FT // d.C
    spots = [spot_bits(lax.bitwise_xor(c, b), shifts, d.bits) for b in range(d.C)]

    def pick(item):
        ref, at = item
        return ins[ref][...] if at is None else ins[ref][at]

    def put(spot, low, piece):
        @pl.when(spot < d.C // 2)
        def _():
            keep[spot, low : low + piece.shape[0]] = piece

        @pl.when(spot >= d.C // 2)
        def _():
            send[spot - d.C // 2, low : low + piece.shape[0]] = piece

    for m, (a, b, a2, b2) in enumerate(tiles):
        total = mm(pick(a), pick(b), TN) + mm(pick(a2), pick(b2), TN)
        total = total.astype(BF)
        for block, spot in enumerate(spots):
            put(spot, m * rb, total[block * rb : (block + 1) * rb, :])
    if flat is not None:
        for block, spot in enumerate(spots):
            put(spot, len(tiles) * rb, ins[flat][block].astype(BF))


def weight_grad(d, name, sc, ins, tiles, mix, flat=None, deps=()):
    rows = len(tiles) * (FT // d.C)
    if flat is not None:
        ins = (*ins, flat)
        rows += EXTRA
    return kernel_call(
        functools.partial(wgrad_body, d, tiles, mix, None if flat is None else len(ins) - 1),
        (sc, *ins),
        [SSPEC] + [VSPEC] * len(ins),
        [VSPEC] * 2,
        [sds((d.C // 2, rows, FT), BF)] * 2,
        "weight_grad_" + name,
        deps=deps, work=cost(4 * d.T * len(tiles) * FT * FT, 8e6))


def small_rows(d):
    return (2, 1, 2, 4), (d.W // FT, d.F // FT, d.D // FT, d.D // FT)


def place_body(d, wide, count_in, extra, layer, owner, flat, sc, *refs):
    ins = refs[:count_in]
    outs = refs[count_in + extra : -3]
    buf, small, sems = refs[-3:]
    rb = FT // d.C
    nt = buf.shape[0]
    r = 0
    for part in ins:
        for n in range(part.shape[0]):
            block = owner(sc, r)
            row = pl.multiple_of(block * rb, rb)
            for m in range(nt):
                buf[m, pl.ds(row, rb), :] = part[n, m * rb : (m + 1) * rb].astype(F32)
            if flat:
                small[block] = part[n, nt * rb :].astype(F32)
            r += 1
    if flat:
        at = 0
        for k in range(LAYERS):
            for out, rows, pieces in zip(outs[len(wide) :], *small_rows(d)):
                for row in range(rows):
                    for piece in range(pieces):
                        line = small[at // EXTRA, at % EXTRA : at % EXTRA + 1, :]
                        lanes = slice(piece * FT, (piece + 1) * FT)
                        if rows == 1:
                            out[k : k + 1, lanes] = line
                        else:
                            out[k, row : row + 1, lanes] = line
                        at += 1
    copies = []
    m = 0
    for out, (kind, count) in zip(outs, wide):
        if kind == "cols":
            for k in range(count):
                copies.append((buf.at[m + k], out.at[layer, :, pl.ds(k * FT, FT)]))
        else:
            copies.append((buf.at[pl.ds(m, count)], out.at[layer]))
        m += count
    going = [pltpu.make_async_copy(a, b, sems.at[k]) for k, (a, b) in enumerate(copies)]
    for one in going:
        one.start()
    for one in going:
        one.wait()


def place(d, layer, sc, unit, before, wide, name, deps=()):
    parts = unit.finish()
    nt = sum(n for _, n in wide)
    flat = parts[0].shape[1] > nt * (FT // d.C)
    held = [k for k, one in enumerate(before) if one is not None]
    extra = tuple(before[k] for k in held) + tuple(deps)
    alias = {1 + len(parts) + n: k for n, k in enumerate(held)}
    shapes = [
        sds((LAYERS, FT, n * FT) if kind == "cols" else (LAYERS, n, FT, FT), F32)
        for kind, n in wide
    ]
    specs = [pl.BlockSpec(memory_space=pl.ANY)] * len(wide)
    if flat:
        for rows, pieces in zip(*small_rows(d)):
            one = (rows, pieces * FT) if rows > 1 else (pieces * FT,)
            shapes.append(sds((LAYERS, *one), F32))
            specs.append(VSPEC)
    moves = sum(n if kind == "cols" else 1 for kind, n in wide)
    at = shift_at(d, unit.mix)

    def owner(scalars, r):
        turned = 0
        for k in range(d.bits):
            if r >> (d.bits - 1 - k) & 1:
                turned = turned + lax.shift_left(jnp.int32(1), scalars[at + k])
        return lax.bitwise_xor(scalars[2], jnp.int32(turned))

    return pl.pallas_call(
        functools.partial(place_body, d, wide, len(parts), len(extra), layer, owner, flat),
        in_specs=[SSPEC] + [VSPEC] * len(parts) + [pl.BlockSpec(memory_space=pl.ANY)] * len(extra),
        out_specs=specs,
        out_shape=shapes,
        scratch_shapes=[
            pltpu.VMEM((nt, FT, FT), F32),
            pltpu.VMEM((d.C, EXTRA, FT), F32),
            pltpu.SemaphoreType.DMA((moves,)),
        ],
        input_output_aliases=alias,
        compiler_params=pltpu.CompilerParams(vmem_limit_bytes=VLIM),
        name="place_" + name,
    )(sc, *parts, *extra)


def swap(values, axis):
    return lax.ppermute(values, axis, [(0, 1), (1, 0)])


def way(d, core, step, mix=True):
    if mix and step < 2 and d.bits > 1:
        return step if core == 0 else 1 - step
    return step


def cross(d, values, step, mix=True):
    pairs = []
    for i in range(d.C):
        for core in range(d.tp):
            to = i ^ (1 << way(d, core, step, mix))
            pairs.append((i * d.tp + core, to * d.tp + core))
    return lax.ppermute(values, ("ctx", "tp"), pairs)


def take_body(sc, w, *refs):
    refs[-1][...] = w[...]


def take(sc, w, block, index, shape, steps=1, deps=()):
    out_block = shape if steps == 1 else (None, *shape[1:])
    return pl.pallas_call(
        take_body,
        grid_spec=pltpu.PrefetchScalarGridSpec(
            num_scalar_prefetch=1,
            grid=(steps,),
            in_specs=[pl.BlockSpec(block, lambda n, s: index(n, s[1]))]
            + [pl.BlockSpec(memory_space=pl.ANY)] * len(deps),
            out_specs=pl.BlockSpec(out_block, lambda n, s: (n,) + (0,) * (len(shape) - 1)),
        ),
        out_shape=sds(shape, BF),
        compiler_params=pltpu.CompilerParams(vmem_limit_bytes=VLIM),
        name="take",
    )(sc, w, *deps)


def fold_body(keep, got, *outs):
    total = (keep[...].astype(F32) + got[...].astype(F32)).astype(BF)
    if len(outs) == 1:
        outs[0][...] = total
    else:
        half = total.shape[0] // 2
        outs[0][...] = total[:half]
        outs[1][...] = total[half:]


def fold(keep, got, deps=()):
    count = keep.shape[0]
    shapes = [keep.shape] if count == 1 else [(count // 2, *keep.shape[1:])] * 2
    return kernel_call(
        fold_body, (keep, got), [VSPEC] * 2, [VSPEC] * len(shapes),
        [sds(v, BF) for v in shapes], "fold", deps=deps, work=cost(1e6, 3e6))


def join_body(*refs):
    out = refs[-1]
    at = 0
    for ref in refs[:-1]:
        out[at : at + ref.shape[0]] = ref[...]
        at += ref.shape[0]


def join(parts, deps=()):
    if len(parts) == 1:
        return parts[0]
    count = sum(p.shape[0] for p in parts)
    return kernel_call(
        join_body, tuple(parts), [VSPEC] * len(parts), VSPEC,
        sds((count, *parts[0].shape[1:]), BF), "join", deps=deps, work=cost(1e5, 3e6))


class Sum:
    def __init__(self, d, mix, keep, send):
        self.d, self.mix = d, mix
        self.keep = keep
        self.got = cross(d, send, 0, mix)
        self.at = 0
        self.parts = None

    def step(self, *deps):
        self.at += 1
        n = self.d.bits
        if self.at < n:
            keep, send = fold(self.keep, self.got, deps)
            self.keep = keep
            self.got = cross(self.d, send, self.at, self.mix)
            return keep
        if self.at == n:
            (keep,) = fold(self.keep, self.got, deps)
            self.parts = [keep]
            self.got = cross(self.d, keep, n - 1, self.mix)
            return keep
        self.parts.append(self.got)
        if self.at < 2 * n:
            full = join(self.parts, deps)
            self.got = cross(self.d, full, 2 * n - 1 - self.at, self.mix)
            return full
        return self.got

    def finish(self):
        while self.at < 2 * self.d.bits:
            self.step()
        return self.parts


def all_to_all(values):
    return lax.all_to_all(values, "ctx", 0, 0)


def key_table(d, parent_ids, depth_offsets):
    segs = parent_ids.shape[0] // lax.axis_size("fsdp")
    start = lax.axis_index("fsdp") * segs
    parents = lax.dynamic_slice_in_dim(parent_ids, start, segs) - start
    depths = lax.dynamic_slice_in_dim(depth_offsets, start, segs).astype(F32)
    ids = jnp.arange(segs, dtype=jnp.int32)
    reach = jnp.maximum(
        (parents[:, None] == ids[None, :]).astype(F32), (ids[:, None] == ids[None, :]).astype(F32)
    )
    for _ in range((segs - 1).bit_length()):
        reach = jnp.minimum(jnp.dot(reach, reach), 1.0)
    head = lax.axis_index("tp") * d.lh + lax.axis_index("ctx") // d.g
    slope = jnp.exp2(-(head + 1).astype(F32))
    level = jnp.where(reach > 0.5, slope * (depths[None, :] - depths[:, None]), MASKED)
    spots = slope * jnp.arange(SEG, dtype=jnp.int32).astype(F32)
    return (level[:, :, None] + spots[None, None, :]).reshape(segs, segs * SEG)


def on_device(tokens, qkv_weight, out_weight, up_weight, down_weight, qv_bias, up_bias,
              norm_gains, row_biases, parent_ids, depth_offsets, cotangent):
    d = Dims(tokens, qkv_weight, up_weight)
    x = lax.axis_index("fsdp")
    c = lax.axis_index("ctx")
    t = lax.axis_index("tp")
    first = [jnp.where(t == 0, way(d, 0, k), way(d, 1, k)) for k in range(d.bits)]
    bit = (c >> first[0]) % 2
    sc = jnp.stack([x, bit, c, *first, *range(d.bits)]).astype(jnp.int32)
    w_qkv = qkv_weight.transpose(0, 2, 1, 3)
    tiles = d.F // FT
    half = tiles // 2

    class Pieces:
        def __init__(self, layer, deps):
            def over(values):
                first = swap(values, "fsdp")
                return first, cross(d, first, 0)

            tile = (None, FT, FT)
            qkv = take(sc, w_qkv, (None, 3, d.Q, d.W), lambda n, b: (layer, 0, b, 0),
                       (3, d.Q, d.W), deps=deps)
            out = take(sc, out_weight, (None, d.W // 2, d.H), lambda n, b: (layer, b, 0),
                       (d.W // 2, d.H), deps=(qkv,))
            up_a = take(sc, up_weight, tile, lambda n, b: (layer, 0, b), (FT, FT), deps=(out,))
            up_b = take(sc, up_weight, tile, lambda n, b: (layer, 0, half + b), (FT, FT),
                        deps=(up_a,))
            dn_a = take(sc, down_weight, tile, lambda n, b: (layer, b, 0), (FT, FT), deps=(up_b,))
            dn_b = take(sc, down_weight, tile, lambda n, b: (layer, half + b, 0), (FT, FT),
                        deps=(dn_a,))
            self.last = dn_b
            self.qkv, self.out = over(qkv), over(out)
            self.dn_a, self.dn_b = over(dn_a), over(dn_b)
            self.up_a, self.up_b = over(up_a), over(up_b)
            self.up = (*self.up_a, *self.up_b)
            self.down = (*self.dn_a, *self.dn_b)

    p0 = Pieces(0, ())
    p = [p0]
    kb = key_table(d, parent_ids, depth_offsets)

    def both(rows):
        got = swap(rows, "tp")
        return jnp.where(
            t == 0,
            jnp.concatenate([rows, got], axis=0),
            jnp.concatenate([got, rows], axis=0),
        )

    def row(values):
        return values.reshape(1, -1)

    def swapped(values):
        return swap(values, "tp")

    def fsdp(values):
        return swap(values, "fsdp")

    class Kept:
        pass

    def forward(layer, state, needs):
        k = kept[layer]
        before = [needs(n) for n in range(1)]
        k.hidden, k.n_o, n_s, chunks = qkv_forward(
            d, layer, sc, state, row(norm_gains[layer, 0]), row(row_biases[layer, 0]),
            w_qkv, p[layer].qkv, qv_bias[layer], deps=before[0])
        k.n_r = fsdp(n_s)
        if layer == 0:
            p.append(Pieces(1, (k.hidden,)))
        before += [needs(n) for n in range(1, 3)]
        k.chunks = all_to_all(chunks)
        outs = all_to_all(attend_forward(d, sc, kb, k.chunks, deps=before[1]))
        k.ctx, part = out_forward(d, layer, sc, out_weight, p[layer].out, outs, deps=before[2])
        k.ctx_r = fsdp(k.ctx)
        before.append(needs(3))
        k.middle, k.n2_o, k.act_p, k.act_q, k.dg, part2 = ffn_forward(
            d, layer, sc, k.hidden, part, swapped(part), row(row_biases[layer, 1]),
            row(norm_gains[layer, 1]), row(row_biases[layer, 2]), up_weight,
            p[layer].up, row(up_bias[layer]), down_weight, p[layer].down, deps=before[3])
        state = (k.middle, part2, swapped(part2), row(row_biases[layer, 3]))
        k.act_pr, k.act_qr = fsdp(k.act_p), fsdp(k.act_q)
        return state

    state = both(tokens)
    p0 = p[0]
    kept = [Kept() for _ in range(LAYERS)]
    k0, k1 = kept
    state = forward(0, state, lambda n: (
        (p0.out[0], p0.up_a[0], p0.last) if n == 0
        else (p0.out[1], p0.up_a[1], p0.up_b[0], p0.dn_a[0], p[1].last) if n == 1
        else (p0.dn_b[0], p[1].qkv[0], p[1].out[0]) if n == 2
        else ()
    ))
    p1 = p[1]
    state = forward(1, state, lambda n: (
        (p1.up_a[0],) if n == 0
        else (p1.out[1], p1.up_a[1], p1.up_b[0], p1.dn_a[0]) if n == 1
        else (p1.dn_b[0], k1.n_r, k0.act_pr) if n == 2
        else ()
    ))
    own_rows = tokens.shape[0]

    def mine(values):
        return lax.dynamic_slice_in_dim(values, t * own_rows, own_rows, 0)

    output = mine(state[0]) + (
        (mine(state[1]).astype(F32) + mine(state[2]).astype(F32)) + state[3]
    )
    output = output.astype(BF)
    grad = both(cotangent)
    sums = [None] * LAYERS
    def grad_ffn(k, more, mix, deps=()):
        ins = (k.n2_o, k.act_p, k.act_pr, k.act_q, k.act_qr, k.xba, k.xba_r, k.xbb, k.xbb_r,
               k.db_o)
        jobs = []
        for f in range(tiles):
            at = (5, 1) if f == 0 else (7, f - 1)
            jobs.append(((0, None), at, (2, 0), (at[0] + 1, at[1])))
        for f in range(tiles):
            at = (1, 1 + f) if f < half else (3, f - half)
            jobs.append((at, (9, None), (at[0] + 1, at[1]), (6, 0)))
        if more:
            ins += (k.ctx, k.ctx_r, k.da_o, k.da_r)
            jobs += [((10, None), (12, None), (11, None), (13, None))]
        return Sum(d, mix, *weight_grad(d, "ffn", sc, ins, jobs, mix, deps=deps))

    def grad_qkv(k, more, mix, flat=None, deps=()):
        ins = (k.n_o, k.n_r, k.xc, k.xc_r)
        jobs = [((0, None), (2, n), (1, None), (3, n)) for n in range(3)]
        if more:
            ins += (k.ctx, k.da_o, k.ctx_r, k.da_r)
            jobs += [((4, None), (5, None), (6, None), (7, None))]
        return Sum(d, mix, *weight_grad(d, "qkv", sc, ins, jobs, mix, flat, deps))

    def back_ffn(layer, k, grad, deps=()):
        k.db_o, k.xba, k.xbb, k.usum, k.bsum, part = ffn_backward(
            d, layer, sc, grad, k.dg, up_weight, p[layer].up, down_weight, p[layer].down,
            deps=deps)
        k.xba_r, k.xbb_r = fsdp(k.xba), fsdp(k.xbb)
        return part

    def back_context(layer, k, grad, part, deps=()):
        k.dmid, k.da_o, k.da_s, k.gsum2, k.ssum2, k.asum, dchunks = context_backward(
            d, layer, sc, grad, part, swapped(part), k.middle, row(norm_gains[layer, 1]),
            out_weight, p[layer].out, deps=deps)
        k.da_r = fsdp(k.da_s)
        return dchunks

    def back_qkv(layer, k, dparts, deps=()):
        k.xc, k.qvsum, part = qkv_backward(
            d, layer, sc, w_qkv, p[layer].qkv, dparts, deps=deps)
        k.xc_r = fsdp(k.xc)
        return part

    def back_input(layer, k, part, deps=()):
        grad, k.gsum1, k.ssum1 = input_backward(
            d, k.dmid, part, swapped(part), k.hidden, row(norm_gains[layer, 0]), deps=deps)
        sums[layer] = (k.qvsum, k.usum, k.gsum1, k.gsum2, k.ssum1, k.asum, k.ssum2, k.bsum)
        return grad

    total = LAYERS * (2 * d.W + d.F + 6 * d.D)

    def small_sums():
        flat = jnp.concatenate([v.reshape(-1) for layer in sums for v in layer])
        return jnp.pad(flat, (0, d.C * EXTRA * FT - total)).reshape(d.C, EXTRA, FT)

    part = back_ffn(1, k1, grad, (k0.act_qr, k1.ctx_r))
    dchunks = back_context(1, k1, grad, part, (state[2],))
    dback = attend_backward(d, sc, kb, k1.chunks, all_to_all(dchunks),
                            deps=(k1.act_pr, k1.act_qr))
    dparts = all_to_all(dback)
    f1 = grad_ffn(k1, False, True, (dback,))
    part = back_qkv(1, k1, dparts, (f1.keep,))
    grad = back_input(1, k1, part)
    part = back_ffn(0, k0, grad)
    a = f1.step(part)
    dchunks = back_context(0, k0, grad, part, (a, k1.xc_r))
    q1 = grad_qkv(k1, True, True, None, (dchunks,))
    a = f1.step(q1.keep)
    dback = attend_backward(d, sc, kb, k0.chunks, all_to_all(dchunks),
                            deps=(a, k0.xba_r, k0.ctx_r, k0.n_r))
    dparts = all_to_all(dback)
    f0 = grad_ffn(k0, True, True, (dback,))
    part = back_qkv(0, k0, dparts, (f0.keep,))
    grad = back_input(0, k0, part)
    flat = small_sums()
    flat = flat + swap(flat, "fsdp")
    a = f1.step(grad)
    q0 = grad_qkv(k0, False, False, flat, (a,))
    a = q0.keep
    ffn_kinds = (("cols", tiles), ("mats", tiles))
    qkv_kinds = (("mats", 3), ("mats", 1))
    last = 2 * d.bits - 1
    for unit in (f0, q1, q0, f1, f0, q1, f1, q0, q1, q0, f0, q1, q0):
        if unit.at < last:
            a = unit.step(a)
    while f1.at < last:
        a = f1.step(a)
    g_ffn = place(d, 1, sc, f1, (), ffn_kinds, "ffn", (a,))
    a = g_ffn[0]
    for unit in (q1, q0):
        while unit.at < last:
            a = unit.step(a)
    while f0.at < last - 1:
        a = f0.step(a)
    g_qkv, g_out = place(d, 1, sc, q1, (), qkv_kinds, "qkv", (a,))
    g_qkv, qv_grad, up_grad, gain_grad, bias_grad = place(
        d, 0, sc, q0, (g_qkv,), (("mats", 3),), "qkv", (g_out,))
    a = f0.step(g_qkv)
    g_up, g_down, g_out = place(d, 0, sc, f0, (*g_ffn, g_out), (*ffn_kinds, ("mats", 1)),
                                "ffn", (a,))
    return (
        output,
        mine(grad),
        g_qkv.transpose(0, 2, 1, 3),
        g_out.reshape(LAYERS, d.W, d.H),
        g_up.reshape(LAYERS, d.H, d.F),
        g_down.reshape(LAYERS, d.F, d.H),
        qv_grad,
        up_grad,
        gain_grad,
        bias_grad,
    )


def solution(mesh):
    in_specs = (
        P(("fsdp", "ctx", "tp"), None),
        P(None, "fsdp", None, "tp"),
        P(None, "tp", "fsdp"),
        P(None, "fsdp", "tp"),
        P(None, "tp", "fsdp"),
        P(None, None, "tp"),
        P(None, "tp"),
        P(),
        P(),
        P(),
        P(),
        P(("fsdp", "ctx", "tp"), None),
    )
    out_specs = (
        P(("fsdp", "ctx", "tp"), None),
        P(("fsdp", "ctx", "tp"), None),
        P(None, "fsdp", None, "tp"),
        P(None, "tp", "fsdp"),
        P(None, "fsdp", "tp"),
        P(None, "tp", "fsdp"),
        P(None, None, "tp"),
        P(None, "tp"),
        P(),
        P(),
    )
    return jax.shard_map(
        on_device, mesh=mesh, in_specs=in_specs, out_specs=out_specs, check_vma=False
    )
```

```python
import functools

import jax
import jax.numpy as jnp
from jax import lax
from jax.experimental import pallas as pl
from jax.experimental.pallas import tpu as pltpu
from jax.sharding import PartitionSpec as P

HEAD_DIM = 128
LAYERS = 2
SEG = 128
EPSILON = 1e-05
MASKED = -1e30
SCALE = HEAD_DIM ** (-0.5)
GELU_A = 0.7978845608028654
GELU_B = 0.044715
BF = jnp.bfloat16
F32 = jnp.float32
VLIM = 56 * 1024 * 1024

NN = (((1,), (0,)), ((), ()))
NT = (((1,), (1,)), ((), ()))
TN = (((0,), (0,)), ((), ()))


def mm(a, b, dims=NN):
    return lax.dot_general(a, b, dims, preferred_element_type=F32)


def sds(shape, dtype):
    return jax.ShapeDtypeStruct(shape, dtype)


VSPEC = pl.BlockSpec(memory_space=pltpu.VMEM)
SSPEC = pl.BlockSpec(memory_space=pltpu.SMEM)


def cost(flops, nbytes):
    return pl.CostEstimate(flops=int(flops), bytes_accessed=int(nbytes), transcendentals=0)


def kernel_call(body, args, in_specs, out_specs, out_shape, name, scratch=(), grid=None,
                deps=(), work=None, aliases=None):
    count, extra = len(args), len(deps)

    def ordered(*refs):
        body(*refs[:count], *refs[count + extra :])

    kwargs = {} if grid is None else {"grid": grid}
    return pl.pallas_call(
        ordered,
        in_specs=list(in_specs) + [pl.BlockSpec(memory_space=pl.ANY)] * extra,
        out_specs=out_specs,
        out_shape=out_shape,
        scratch_shapes=list(scratch),
        input_output_aliases=aliases or {},
        compiler_params=pltpu.CompilerParams(vmem_limit_bytes=VLIM),
        cost_estimate=work,
        name=name,
        **kwargs,
    )(*args, *deps)


def norm_rows(v):
    centered = v - jnp.mean(v, axis=-1, keepdims=True)
    rstd = lax.rsqrt(jnp.mean(centered * centered, axis=-1, keepdims=True) + EPSILON)
    return centered * rstd, rstd


def norm_back(d, v, gain):
    xhat, rstd = norm_rows(v)
    dx = d * gain
    back = rstd * (
        dx
        - jnp.mean(dx, axis=-1, keepdims=True)
        - xhat * jnp.mean(dx * xhat, axis=-1, keepdims=True)
    )
    d_gain = jnp.sum(d * xhat, axis=0, keepdims=True)
    d_shift = jnp.sum(d, axis=0, keepdims=True)
    return back, d_gain, d_shift


class Dims:
    def __init__(self, tokens, qkv_weight, up_weight):
        self.tp = lax.axis_size("tp")
        self.C = lax.axis_size("ctx")
        self.T = tokens.shape[0] * self.tp
        self.D = tokens.shape[1]
        self.H = self.D // lax.axis_size("fsdp")
        self.Q = self.H // 2
        self.W = qkv_weight.shape[3]
        self.F = up_weight.shape[2]
        self.lh = self.W // HEAD_DIM
        self.g = self.C // self.lh
        self.rq = self.T // self.g
        self.chunk = self.rq + 2 * self.T
        self.bits = self.C.bit_length() - 1


def offs(sc, d):
    x = sc[0]
    y = sc[1]
    own = pl.multiple_of(x * d.H, d.H)
    oth = pl.multiple_of((1 - x) * d.H, d.H)
    first = pl.multiple_of((1 - x) * d.H + y * d.Q, d.Q)
    second = pl.multiple_of((1 - x) * d.H + (1 - y) * d.Q, d.Q)
    return own, oth, first, second


def spot_of(d, chip):
    row, head = (chip % d.g) * d.rq, (chip // d.g) * HEAD_DIM
    return slice(row, row + d.rq), slice(head, head + HEAD_DIM)


def qkv_body(d, first, *refs):
    if first:
        sc, hid, gain, shift, w, w1, w2, qvb = refs[:8]
        rest = refs[8:]
        hidden = hid[...].astype(F32)
    else:
        sc, mid, pa, pb, bias, gain, shift, w, w1, w2, qvb = refs[:11]
        rest = refs[11:]
        hidden = mid[...] + ((pa[...].astype(F32) + pb[...].astype(F32)) + bias[...])
    h_out, no_out, ns_out, chunks, n_out, scr = rest
    own, oth, p1, p2 = offs(sc, d)
    h_out[...] = hidden
    xhat, _ = norm_rows(hidden)
    n_out[...] = (xhat * gain[...] + shift[...]).astype(BF)
    ns_out[...] = n_out[:, pl.ds(oth, d.H)]
    a0 = n_out[:, pl.ds(own, d.H)]
    no_out[...] = a0
    a1 = n_out[:, pl.ds(p1, d.Q)]
    a2 = n_out[:, pl.ds(p2, d.Q)]
    for n in range(3):
        proj = mm(a0, w[n]) + mm(a1, w1[n]) + mm(a2, w2[n])
        if n == 0:
            proj = proj + qvb[0:1, :]
        if n == 2:
            proj = proj + qvb[1:2, :]
        scr[n] = proj.astype(BF)
    for to in range(d.C):
        row, col = spot_of(d, to)
        chunks[to, 0 : d.rq, :] = scr[0, row, col]
        chunks[to, d.rq : d.rq + d.T, :] = scr[1, :, col]
        chunks[to, d.rq + d.T :, :] = scr[2, :, col]


def whole(shape):
    return pl.BlockSpec(shape, lambda *_: (0,) * len(shape))


def piece_specs(shape, pieces, axis):
    if pieces[0] is not pieces[1]:
        return [whole(shape), whole(shape)]
    second = tuple(1 if k == axis else 0 for k in range(len(shape)))
    return [whole(shape), pl.BlockSpec(shape, lambda *_: second)]


def qkv_forward(d, layer, sc, hid, gain, shift, w, pieces, qvb, deps=()):
    first = not isinstance(hid, tuple)
    hid = (hid,) if first else hid
    wspec = pl.BlockSpec((None, 3, d.H, d.W), lambda i: (layer, 0, 0, 0))
    in_specs = [SSPEC] + [whole(a.shape) for a in hid]
    in_specs += [whole(gain.shape), whole(shift.shape), wspec]
    in_specs += piece_specs((3, d.Q, d.W), pieces, 1) + [whole(qvb.shape)]
    outs = [sds((d.T, d.D), F32), sds((d.T, d.H), BF), sds((d.T, d.H), BF)]
    outs += [sds((d.C, d.chunk, HEAD_DIM), BF)]
    return kernel_call(
        functools.partial(qkv_body, d, first),
        (sc, *hid, gain, shift, w, *pieces, qvb,),
        grid=(1,),
        in_specs=in_specs,
        out_specs=[whole(o.shape) for o in outs],
        out_shape=outs,
        scratch=[pltpu.VMEM((d.T, d.D), BF), pltpu.VMEM((3, d.T, d.W), BF)],
        work=cost(2 * d.T * d.D * 3 * d.W, 8e6),
        name="qkv_forward",
        deps=deps,
    )


def load_chunks(d, sc, chunks, qs, ks, vs):
    qs[...] = chunks[:, 0 : d.rq, :]
    ks[...] = chunks[:, d.rq : d.rq + d.T, :]
    vs[...] = chunks[:, d.rq + d.T :, :]


def score_block(d, sc, kb, q, k, s, ext):
    part = lax.rem(sc[2], d.g)
    seg = s * (d.T // SEG) + lax.div(part * d.rq, SEG)
    scores = mm(q, k, NT) * SCALE + kb[pl.ds(seg, 1), 0:ext]
    col = lax.broadcasted_iota(jnp.int32, (d.rq, ext), 1) - s * d.T
    row = lax.broadcasted_iota(jnp.int32, (d.rq, ext), 0) + part * d.rq
    return jnp.where(col <= row, scores, MASKED)


UNROLL = 8
SHIFT = 3


def each_source(d, one):
    if d.C <= UNROLL:
        for s in range(d.C):
            one(s, s + 1)
    else:
        lax.fori_loop(0, d.C, lambda s, carry: (one(s, d.C), carry)[1], 0)


def attend_body(d, *refs):
    sc, kb, chunks, cs, qs, ks, vs = refs
    load_chunks(d, sc, chunks, qs, ks, vs)
    def one(s, seen):
        ext = seen * d.T
        k = ks[0:seen].reshape(ext, HEAD_DIM)
        v = vs[0:seen].reshape(ext, HEAD_DIM)
        scores = score_block(d, sc, kb, qs[s], k, s, ext)
        e = jnp.exp(scores - jnp.max(scores, axis=-1, keepdims=True))
        total = jnp.sum(e, axis=-1, keepdims=True)
        cs[s] = (mm(e.astype(BF), v) / total).astype(BF)

    each_source(d, one)


def attend_forward(d, sc, kb, chunks, deps=()):
    return kernel_call(
        functools.partial(attend_body, d),
        (sc, kb, chunks,),
        in_specs=[SSPEC] + [VSPEC] * 2,
        out_specs=VSPEC,
        out_shape=sds((d.C, d.rq, HEAD_DIM), BF),
        scratch=[
            pltpu.VMEM((d.C, d.rq, HEAD_DIM), BF),
            pltpu.VMEM((d.C, d.T, HEAD_DIM), BF),
            pltpu.VMEM((d.C, d.T, HEAD_DIM), BF),
        ],
        work=cost(2 * d.C * d.rq * d.C * d.T * HEAD_DIM * 2, 3e6),
        name="attend_forward",
        deps=deps,
    )


def out_body(d, *refs):
    sc, w, w1, w2, chunks, ctx, part = refs
    for src in range(d.C):
        ctx[spot_of(d, src)] = chunks[src]
    own, oth, _, _ = offs(sc, d)
    half = d.W // 2
    k1 = pl.multiple_of(sc[1] * half, half)
    k2 = pl.multiple_of((1 - sc[1]) * half, half)
    part[:, pl.ds(own, d.H)] = mm(ctx[...], w[...]).astype(BF)
    part[:, pl.ds(oth, d.H)] = (
        mm(ctx[:, pl.ds(k1, half)], w1[...]) + mm(ctx[:, pl.ds(k2, half)], w2[...])
    ).astype(BF)


def out_forward(d, layer, sc, w, pieces, chunks, deps=()):
    wspec = pl.BlockSpec((None, d.W, d.H), lambda i: (layer, 0, 0))
    outs = [sds((d.T, d.W), BF), sds((d.T, d.D), BF)]
    return kernel_call(
        functools.partial(out_body, d),
        (sc, w, *pieces, chunks,),
        grid=(1,),
        in_specs=[SSPEC, wspec] + piece_specs((d.W // 2, d.H), pieces, 0)
        + [whole(chunks.shape)],
        out_specs=[whole(o.shape) for o in outs],
        out_shape=outs,
        work=cost(2 * d.T * d.D * d.W, 3e6),
        name="out_forward",
        deps=deps,
    )


FT = 512


def tile_of(f, sc, tiles, refs, use):
    half = tiles // 2
    mine = lax.rem(f, half) == sc[1]
    for number, (came, then) in enumerate((refs[:2], refs[2:])):
        here = lax.div(f, half) == number

        @pl.when(jnp.logical_and(here, mine))
        def _():
            use(came)

        @pl.when(jnp.logical_and(here, jnp.logical_not(mine)))
        def _():
            use(then)


def ffn_body(d, tiles, sc, hid, pa, pb, bias, gain, shift,
             u, u1, u2, u3, u4, ub, w, w1, w2, w3, w4,
             mid, no, act_p, act_q, dg, part, n2, acc, pre):
    f = pl.program_id(0)
    own, oth, _, _ = offs(sc, d)

    @pl.when(f == 0)
    def _():
        m = hid[...] + ((pa[...].astype(F32) + pb[...].astype(F32)) + bias[...])
        mid[...] = m
        xhat, _ = norm_rows(m)
        n2[...] = (xhat * gain[...] + shift[...]).astype(BF)
        no[...] = n2[:, pl.ds(own, d.H)]
        act_p[0] = n2[:, pl.ds(oth, d.H)]
        acc[...] = jnp.zeros_like(acc)

    def up(ref):
        pre[...] = mm(act_p[0], ref[...])

    tile_of(f, sc, tiles, (u1, u2, u3, u4), up)
    v = pre[...] + mm(no[...], u[...]) + ub[...]
    sq = v * v
    th = jnp.tanh(GELU_A * v * (1.0 + GELU_B * sq))
    half = 0.5 * (1.0 + th)
    a = (v * half).astype(BF)

    @pl.when(f < tiles // 2)
    def _():
        act_p[1 + f] = a

    @pl.when(f >= tiles // 2)
    def _():
        act_q[f - tiles // 2] = a

    dg[...] = (
        half + 0.5 * v * (1.0 - th * th) * (GELU_A * (1.0 + 3.0 * GELU_B * sq))
    ).astype(BF)
    acc[0] += mm(a, w[...])

    def down(ref):
        acc[1] += mm(a, ref[...])

    tile_of(f, sc, tiles, (w1, w2, w3, w4), down)

    @pl.when(f == tiles - 1)
    def _():
        part[:, pl.ds(own, d.H)] = acc[0].astype(BF)
        part[:, pl.ds(oth, d.H)] = acc[1].astype(BF)


def ffn_specs(d, layer):
    u = pl.BlockSpec((None, d.H, FT), lambda f: (layer, 0, f))
    w = pl.BlockSpec((None, FT, d.H), lambda f: (layer, f, 0))
    return [u] + [whole((d.H, FT))] * 4, [w] + [whole((FT, d.H))] * 4


def ffn_forward(d, layer, sc, hid, pa, pb, bias, gain, shift,
                up_w, up_p, ub, dn_w, dn_p, deps=()):
    tiles = d.F // FT
    us, ws = ffn_specs(d, layer)
    side = whole((d.T, d.H))
    col = pl.BlockSpec((d.T, FT), lambda f: (0, f))
    row = whole((1, d.D))
    full = whole((d.T, d.D))
    act_p = sds((1 + tiles // 2, d.T, FT), BF)
    act_q = sds((tiles // 2, d.T, FT), BF)
    return kernel_call(
        functools.partial(ffn_body, d, tiles),
        (sc, hid, pa, pb, bias, gain, shift, up_w, *up_p, ub, dn_w, *dn_p),
        [SSPEC, full, full, full, row, row, row, *us,
         pl.BlockSpec((1, FT), lambda f: (0, f)), *ws],
        [full, side, whole(act_p.shape), whole(act_q.shape), col, full],
        [sds((d.T, d.D), F32), sds((d.T, d.H), BF), act_p, act_q,
         sds((d.T, d.F), BF), sds((d.T, d.D), BF)],
        "ffn_forward",
        scratch=[pltpu.VMEM((d.T, d.D), BF), pltpu.VMEM((2, d.T, d.H), F32),
                 pltpu.VMEM((d.T, FT), F32)],
        grid=(tiles,), deps=deps, work=cost(4 * d.T * d.D * d.F, 14e6))


def ffn_back_body(d, tiles, sc, grad, dg, u, u1, u2, u3, u4, w, w1, w2, w3, w4,
                  dbo, xba, xbb, usum, bsum, part, acc, dact):
    f = pl.program_id(0)
    own, oth, _, _ = offs(sc, d)

    @pl.when(f == 0)
    def _():
        dbo[...] = grad[:, pl.ds(own, d.H)].astype(BF)
        xba[0] = grad[:, pl.ds(oth, d.H)].astype(BF)
        bsum[...] = jnp.sum(grad[...].astype(BF).astype(F32), axis=0, keepdims=True)
        acc[...] = jnp.zeros_like(acc)

    def down(ref):
        dact[...] = mm(xba[0], ref[...], NT)

    tile_of(f, sc, tiles, (w1, w2, w3, w4), down)
    da = dact[...] + mm(dbo[...], w[...], NT)
    dp = (da * dg[...].astype(F32)).astype(BF)

    @pl.when(f == 0)
    def _():
        xba[1] = dp

    @pl.when(f > 0)
    def _():
        xbb[f - 1] = dp

    usum[...] = jnp.sum(dp.astype(F32), axis=0, keepdims=True)
    acc[0] += mm(dp, u[...], NT)

    def up(ref):
        acc[1] += mm(dp, ref[...], NT)

    tile_of(f, sc, tiles, (u1, u2, u3, u4), up)

    @pl.when(f == tiles - 1)
    def _():
        part[:, pl.ds(own, d.H)] = acc[0].astype(BF)
        part[:, pl.ds(oth, d.H)] = acc[1].astype(BF)


def ffn_backward(d, layer, sc, grad, dg, up_w, up_p, dn_w, dn_p, deps=()):
    tiles = d.F // FT
    us, ws = ffn_specs(d, layer)
    side = whole((d.T, d.H))
    col = pl.BlockSpec((d.T, FT), lambda f: (0, f))
    full = whole((d.T, d.D))
    xba = sds((2, d.T, FT), BF)
    xbb = sds((tiles - 1, d.T, FT), BF)
    return kernel_call(
        functools.partial(ffn_back_body, d, tiles),
        (sc, grad, dg, up_w, *up_p, dn_w, *dn_p),
        [SSPEC, full, col, *us, *ws],
        [side, whole(xba.shape), whole(xbb.shape),
         pl.BlockSpec((1, FT), lambda f: (0, f)), whole((1, d.D)), full],
        [sds((d.T, d.H), BF), xba, xbb,
         sds((1, d.F), F32), sds((1, d.D), F32), sds((d.T, d.D), BF)],
        "ffn_backward",
        scratch=[pltpu.VMEM((2, d.T, d.H), F32), pltpu.VMEM((d.T, FT), F32)],
        grid=(tiles,), deps=deps, work=cost(4 * d.T * d.D * d.F, 14e6))


def context_back_body(d, *refs):
    sc, grad, pa, pb, mid, gain, w, w1, w2 = refs[:9]
    dmid, dao, das, gsum, ssum, asum, chunks, da, dctx = refs[9:]
    own, oth, _, _ = offs(sc, d)
    back, g, s = norm_back(pa[...].astype(F32) + pb[...].astype(F32), mid[...], gain[...])
    gsum[...] = g
    ssum[...] = s
    total = grad[...].astype(F32) + back
    dmid[...] = total
    da[...] = total.astype(BF)
    dao[...] = da[:, pl.ds(own, d.H)]
    das[...] = da[:, pl.ds(oth, d.H)]
    asum[...] = jnp.sum(da[...].astype(F32), axis=0, keepdims=True)
    half = d.W // 2
    k1 = pl.multiple_of(sc[1] * half, half)
    k2 = pl.multiple_of((1 - sc[1]) * half, half)
    dctx[...] = mm(da[:, pl.ds(own, d.H)], w[...], NT)
    dctx[:, pl.ds(k1, half)] += mm(da[:, pl.ds(oth, d.H)], w1[...], NT)
    dctx[:, pl.ds(k2, half)] += mm(da[:, pl.ds(oth, d.H)], w2[...], NT)
    for to in range(d.C):
        chunks[to] = dctx[spot_of(d, to)].astype(BF)


def context_backward(d, layer, sc, grad, pa, pb, mid, gain, w, pieces, deps=()):
    wspec = pl.BlockSpec((None, d.W, d.H), lambda i: (layer, 0, 0))
    outs = [sds((d.T, d.D), F32), sds((d.T, d.H), BF), sds((d.T, d.H), BF)]
    outs += [sds((1, d.D), F32)] * 3 + [sds((d.C, d.rq, HEAD_DIM), BF)]
    return kernel_call(
        functools.partial(context_back_body, d),
        (sc, grad, pa, pb, mid, gain, w, *pieces,),
        grid=(1,),
        in_specs=[SSPEC] + [whole(a.shape) for a in (grad, pa, pb, mid, gain)]
        + [wspec] + piece_specs((d.W // 2, d.H), pieces, 0),
        out_specs=[whole(o.shape) for o in outs],
        out_shape=outs,
        scratch=[pltpu.VMEM((d.T, d.D), BF), pltpu.VMEM((d.T, d.W), F32)],
        work=cost(2 * d.T * d.D * d.W, 6e6),
        name="context_backward",
        deps=deps,
    )


def attend_back_body(d, *refs):
    sc, kb, chunks, cs, outs, qs, ks, vs, dks, dvs = refs
    load_chunks(d, sc, chunks, qs, ks, vs)
    dks[...] = jnp.zeros_like(dks)
    dvs[...] = jnp.zeros_like(dvs)
    def one(s, seen):
        ext = seen * d.T
        k = ks[0:seen].reshape(ext, HEAD_DIM)
        v = vs[0:seen].reshape(ext, HEAD_DIM)
        q = qs[s]
        dc = cs[s]
        scores = score_block(d, sc, kb, q, k, s, ext)
        e = jnp.exp(scores - jnp.max(scores, axis=-1, keepdims=True))
        p = e / jnp.sum(e, axis=-1, keepdims=True)
        dp = mm(dc, v, NT)
        ds = (p * (dp - jnp.sum(p * dp, axis=-1, keepdims=True))).astype(BF)
        outs[s, 0 : d.rq, :] = (mm(ds, k) * SCALE).astype(BF)
        dks[0:seen] += mm(ds, q, TN).reshape(seen, d.T, HEAD_DIM)
        dvs[0:seen] += mm(p.astype(BF), dc, TN).reshape(seen, d.T, HEAD_DIM)

    each_source(d, one)
    outs[:, d.rq : d.rq + d.T, :] = (dks[...] * SCALE).astype(BF)
    outs[:, d.rq + d.T :, :] = dvs[...].astype(BF)


def attend_backward(d, sc, kb, chunks, dchunks, deps=()):
    return kernel_call(
        functools.partial(attend_back_body, d),
        (sc, kb, chunks, dchunks,),
        in_specs=[SSPEC] + [VSPEC] * 3,
        out_specs=VSPEC,
        out_shape=sds((d.C, d.chunk, HEAD_DIM), BF),
        scratch=[
            pltpu.VMEM((d.C, d.rq, HEAD_DIM), BF),
            pltpu.VMEM((d.C, d.T, HEAD_DIM), BF),
            pltpu.VMEM((d.C, d.T, HEAD_DIM), BF),
            pltpu.VMEM((d.C, d.T, HEAD_DIM), F32),
            pltpu.VMEM((d.C, d.T, HEAD_DIM), F32),
        ],
        work=cost(5 * d.C * d.rq * d.C * d.T * HEAD_DIM * 2, 4e6),
        name="attend_backward",
        deps=deps,
    )


def qkv_back_body(d, sc, w, w1, w2, chunks, xb, qvsum, part, dk, dv):
    dk[...] = jnp.zeros_like(dk)
    dv[...] = jnp.zeros_like(dv)
    for src in range(d.C):
        row, col = spot_of(d, src)
        xb[0, row, col] = chunks[src, 0 : d.rq, :]
        dk[:, col] += chunks[src, d.rq : d.rq + d.T, :].astype(F32)
        dv[:, col] += chunks[src, d.rq + d.T :, :].astype(F32)
    xb[1] = dk[...].astype(BF)
    xb[2] = dv[...].astype(BF)
    qvsum[0:1, :] = jnp.sum(xb[0].astype(F32), axis=0, keepdims=True)
    qvsum[1:2, :] = jnp.sum(xb[2].astype(F32), axis=0, keepdims=True)
    own, _, p1, p2 = offs(sc, d)
    for ref, at, width in ((w, own, d.H), (w1, p1, d.Q), (w2, p2, d.Q)):
        total = mm(xb[0], ref[0], NT) + mm(xb[1], ref[1], NT) + mm(xb[2], ref[2], NT)
        part[:, pl.ds(at, width)] = total.astype(BF)


def qkv_backward(d, layer, sc, w, pieces, chunks, deps=()):
    wspec = pl.BlockSpec((None, 3, d.H, d.W), lambda i: (layer, 0, 0, 0))
    outs = [sds((3, d.T, d.W), BF), sds((2, d.W), F32), sds((d.T, d.D), BF)]
    return kernel_call(
        functools.partial(qkv_back_body, d),
        (sc, w, *pieces, chunks),
        [SSPEC, wspec] + [whole((3, d.Q, d.W))] * 2 + [whole(chunks.shape)],
        [whole(o.shape) for o in outs],
        outs,
        "qkv_backward",
        scratch=[pltpu.VMEM((d.T, d.W), F32)] * 2,
        grid=(1,), deps=deps, work=cost(2 * d.T * d.D * 3 * d.W, 7e6))


def input_back_body(dmid, pa, pb, hid, gain, grad, gsum, ssum):
    back, g, s = norm_back(pa[...].astype(F32) + pb[...].astype(F32), hid[...], gain[...])
    grad[...] = dmid[...] + back
    gsum[...] = g
    ssum[...] = s


def input_backward(d, dmid, pa, pb, hid, gain, deps=()):
    return kernel_call(
        input_back_body,
        (dmid, pa, pb, hid, gain,),
        in_specs=[VSPEC] * 5,
        out_specs=[VSPEC] * 3,
        out_shape=[sds((d.T, d.D), F32)] + [sds((1, d.D), F32)] * 2,
        work=cost(3e6, 5e6),
        name="input_backward",
        deps=deps,
    )


def spot_bits(value, shifts, bits):
    out = 0
    for k in range(bits):
        bit = lax.bitwise_and(lax.shift_right_logical(value, shifts[k]), 1)
        out = out + bit * (1 << (bits - 1 - k))
    return out


EXTRA = 16


def shift_at(d, mix):
    return SHIFT if mix else SHIFT + d.bits


def wgrad_body(d, tiles, mix, flat, sc, *refs):
    ins = refs[:-2]
    keep, send = refs[-2:]
    c = sc[2]
    shifts = [sc[shift_at(d, mix) + k] for k in range(d.bits)]
    rb = FT // d.C
    spots = [spot_bits(lax.bitwise_xor(c, b), shifts, d.bits) for b in range(d.C)]

    def pick(item):
        ref, at = item
        return ins[ref][...] if at is None else ins[ref][at]

    def put(spot, low, piece):
        @pl.when(spot < d.C // 2)
        def _():
            keep[spot, low : low + piece.shape[0]] = piece

        @pl.when(spot >= d.C // 2)
        def _():
            send[spot - d.C // 2, low : low + piece.shape[0]] = piece

    for m, (a, b, a2, b2) in enumerate(tiles):
        total = mm(pick(a), pick(b), TN) + mm(pick(a2), pick(b2), TN)
        total = total.astype(BF)
        for block, spot in enumerate(spots):
            put(spot, m * rb, total[block * rb : (block + 1) * rb, :])
    if flat is not None:
        for block, spot in enumerate(spots):
            put(spot, len(tiles) * rb, ins[flat][block].astype(BF))


def weight_grad(d, name, sc, ins, tiles, mix, flat=None, deps=()):
    rows = len(tiles) * (FT // d.C)
    if flat is not None:
        ins = (*ins, flat)
        rows += EXTRA
    return kernel_call(
        functools.partial(wgrad_body, d, tiles, mix, None if flat is None else len(ins) - 1),
        (sc, *ins),
        [SSPEC] + [VSPEC] * len(ins),
        [VSPEC] * 2,
        [sds((d.C // 2, rows, FT), BF)] * 2,
        "weight_grad_" + name,
        deps=deps, work=cost(4 * d.T * len(tiles) * FT * FT, 8e6))


def small_rows(d):
    return (2, 1, 2, 4), (d.W // FT, d.F // FT, d.D // FT, d.D // FT)


def place_body(d, wide, count_in, extra, layer, owner, flat, sc, *refs):
    ins = refs[:count_in]
    outs = refs[count_in + extra : -3]
    buf, small, sems = refs[-3:]
    rb = FT // d.C
    nt = buf.shape[0]
    r = 0
    for part in ins:
        for n in range(part.shape[0]):
            block = owner(sc, r)
            row = pl.multiple_of(block * rb, rb)
            for m in range(nt):
                buf[m, pl.ds(row, rb), :] = part[n, m * rb : (m + 1) * rb].astype(F32)
            if flat:
                small[block] = part[n, nt * rb :].astype(F32)
            r += 1
    if flat:
        at = 0
        for k in range(LAYERS):
            for out, rows, pieces in zip(outs[len(wide) :], *small_rows(d)):
                for row in range(rows):
                    for piece in range(pieces):
                        line = small[at // EXTRA, at % EXTRA : at % EXTRA + 1, :]
                        lanes = slice(piece * FT, (piece + 1) * FT)
                        if rows == 1:
                            out[k : k + 1, lanes] = line
                        else:
                            out[k, row : row + 1, lanes] = line
                        at += 1
    copies = []
    m = 0
    for out, (kind, count) in zip(outs, wide):
        if kind == "cols":
            for k in range(count):
                copies.append((buf.at[m + k], out.at[layer, :, pl.ds(k * FT, FT)]))
        else:
            copies.append((buf.at[pl.ds(m, count)], out.at[layer]))
        m += count
    going = [pltpu.make_async_copy(a, b, sems.at[k]) for k, (a, b) in enumerate(copies)]
    for one in going:
        one.start()
    for one in going:
        one.wait()


def place(d, layer, sc, unit, before, wide, name, deps=()):
    parts = unit.finish()
    nt = sum(n for _, n in wide)
    flat = parts[0].shape[1] > nt * (FT // d.C)
    held = [k for k, one in enumerate(before) if one is not None]
    extra = tuple(before[k] for k in held) + tuple(deps)
    alias = {1 + len(parts) + n: k for n, k in enumerate(held)}
    shapes = [
        sds((LAYERS, FT, n * FT) if kind == "cols" else (LAYERS, n, FT, FT), F32)
        for kind, n in wide
    ]
    specs = [pl.BlockSpec(memory_space=pl.ANY)] * len(wide)
    if flat:
        for rows, pieces in zip(*small_rows(d)):
            one = (rows, pieces * FT) if rows > 1 else (pieces * FT,)
            shapes.append(sds((LAYERS, *one), F32))
            specs.append(VSPEC)
    moves = sum(n if kind == "cols" else 1 for kind, n in wide)
    at = shift_at(d, unit.mix)

    def owner(scalars, r):
        turned = 0
        for k in range(d.bits):
            if r >> (d.bits - 1 - k) & 1:
                turned = turned + lax.shift_left(jnp.int32(1), scalars[at + k])
        return lax.bitwise_xor(scalars[2], jnp.int32(turned))

    return pl.pallas_call(
        functools.partial(place_body, d, wide, len(parts), len(extra), layer, owner, flat),
        in_specs=[SSPEC] + [VSPEC] * len(parts) + [pl.BlockSpec(memory_space=pl.ANY)] * len(extra),
        out_specs=specs,
        out_shape=shapes,
        scratch_shapes=[
            pltpu.VMEM((nt, FT, FT), F32),
            pltpu.VMEM((d.C, EXTRA, FT), F32),
            pltpu.SemaphoreType.DMA((moves,)),
        ],
        input_output_aliases=alias,
        compiler_params=pltpu.CompilerParams(vmem_limit_bytes=VLIM),
        name="place_" + name,
    )(sc, *parts, *extra)


def swap(values, axis):
    return lax.ppermute(values, axis, [(0, 1), (1, 0)])


def way(d, core, step, mix=True):
    if mix and step < 2 and d.bits > 1:
        return step if core == 0 else 1 - step
    return step


def cross(d, values, step, mix=True):
    pairs = []
    for i in range(d.C):
        for core in range(d.tp):
            to = i ^ (1 << way(d, core, step, mix))
            pairs.append((i * d.tp + core, to * d.tp + core))
    return lax.ppermute(values, ("ctx", "tp"), pairs)


def take_body(sc, w, *refs):
    refs[-1][...] = w[...]


def take(sc, w, block, index, shape, steps=1, deps=()):
    out_block = shape if steps == 1 else (None, *shape[1:])
    return pl.pallas_call(
        take_body,
        grid_spec=pltpu.PrefetchScalarGridSpec(
            num_scalar_prefetch=1,
            grid=(steps,),
            in_specs=[pl.BlockSpec(block, lambda n, s: index(n, s[1]))]
            + [pl.BlockSpec(memory_space=pl.ANY)] * len(deps),
            out_specs=pl.BlockSpec(out_block, lambda n, s: (n,) + (0,) * (len(shape) - 1)),
        ),
        out_shape=sds(shape, BF),
        compiler_params=pltpu.CompilerParams(vmem_limit_bytes=VLIM),
        name="take",
    )(sc, w, *deps)


def fold_body(keep, got, *outs):
    total = (keep[...].astype(F32) + got[...].astype(F32)).astype(BF)
    if len(outs) == 1:
        outs[0][...] = total
    else:
        half = total.shape[0] // 2
        outs[0][...] = total[:half]
        outs[1][...] = total[half:]


def fold(keep, got, deps=()):
    count = keep.shape[0]
    shapes = [keep.shape] if count == 1 else [(count // 2, *keep.shape[1:])] * 2
    return kernel_call(
        fold_body, (keep, got), [VSPEC] * 2, [VSPEC] * len(shapes),
        [sds(v, BF) for v in shapes], "fold", deps=deps, work=cost(1e6, 3e6))


def join_body(*refs):
    out = refs[-1]
    at = 0
    for ref in refs[:-1]:
        out[at : at + ref.shape[0]] = ref[...]
        at += ref.shape[0]


def join(parts, deps=()):
    if len(parts) == 1:
        return parts[0]
    count = sum(p.shape[0] for p in parts)
    return kernel_call(
        join_body, tuple(parts), [VSPEC] * len(parts), VSPEC,
        sds((count, *parts[0].shape[1:]), BF), "join", deps=deps, work=cost(1e5, 3e6))


class Sum:
    def __init__(self, d, mix, keep, send):
        self.d, self.mix = d, mix
        self.keep = keep
        self.got = cross(d, send, 0, mix)
        self.at = 0
        self.parts = None

    def step(self, *deps):
        self.at += 1
        n = self.d.bits
        if self.at < n:
            keep, send = fold(self.keep, self.got, deps)
            self.keep = keep
            self.got = cross(self.d, send, self.at, self.mix)
            return keep
        if self.at == n:
            (keep,) = fold(self.keep, self.got, deps)
            self.parts = [keep]
            self.got = cross(self.d, keep, n - 1, self.mix)
            return keep
        self.parts.append(self.got)
        if self.at < 2 * n:
            full = join(self.parts, deps)
            self.got = cross(self.d, full, 2 * n - 1 - self.at, self.mix)
            return full
        return self.got

    def finish(self):
        while self.at < 2 * self.d.bits:
            self.step()
        return self.parts


def all_to_all(values):
    return lax.all_to_all(values, "ctx", 0, 0)


def key_table(d, parent_ids, depth_offsets):
    segs = parent_ids.shape[0] // lax.axis_size("fsdp")
    start = lax.axis_index("fsdp") * segs
    parents = lax.dynamic_slice_in_dim(parent_ids, start, segs) - start
    depths = lax.dynamic_slice_in_dim(depth_offsets, start, segs).astype(F32)
    ids = jnp.arange(segs, dtype=jnp.int32)
    reach = jnp.maximum(
        (parents[:, None] == ids[None, :]).astype(F32), (ids[:, None] == ids[None, :]).astype(F32)
    )
    for _ in range((segs - 1).bit_length()):
        reach = jnp.minimum(jnp.dot(reach, reach), 1.0)
    head = lax.axis_index("tp") * d.lh + lax.axis_index("ctx") // d.g
    slope = jnp.exp2(-(head + 1).astype(F32))
    level = jnp.where(reach > 0.5, slope * (depths[None, :] - depths[:, None]), MASKED)
    spots = slope * jnp.arange(SEG, dtype=jnp.int32).astype(F32)
    return (level[:, :, None] + spots[None, None, :]).reshape(segs, segs * SEG)


def on_device(tokens, qkv_weight, out_weight, up_weight, down_weight, qv_bias, up_bias,
              norm_gains, row_biases, parent_ids, depth_offsets, cotangent):
    d = Dims(tokens, qkv_weight, up_weight)
    x = lax.axis_index("fsdp")
    c = lax.axis_index("ctx")
    t = lax.axis_index("tp")
    first = [jnp.where(t == 0, way(d, 0, k), way(d, 1, k)) for k in range(d.bits)]
    bit = (c >> first[0]) % 2
    sc = jnp.stack([x, bit, c, *first, *range(d.bits)]).astype(jnp.int32)
    w_qkv = qkv_weight.transpose(0, 2, 1, 3)
    tiles = d.F // FT
    half = tiles // 2

    class Pieces:
        def __init__(self, layer, deps):
            def over(values):
                first = swap(values, "fsdp")
                return first, cross(d, first, 0)

            tile = (None, FT, FT)
            qkv = take(sc, w_qkv, (None, 3, d.Q, d.W), lambda n, b: (layer, 0, b, 0),
                       (3, d.Q, d.W), deps=deps)
            out = take(sc, out_weight, (None, d.W // 2, d.H), lambda n, b: (layer, b, 0),
                       (d.W // 2, d.H), deps=(qkv,))
            up_a = take(sc, up_weight, tile, lambda n, b: (layer, 0, b), (FT, FT), deps=(out,))
            up_b = take(sc, up_weight, tile, lambda n, b: (layer, 0, half + b), (FT, FT),
                        deps=(up_a,))
            dn_a = take(sc, down_weight, tile, lambda n, b: (layer, b, 0), (FT, FT), deps=(up_b,))
            dn_b = take(sc, down_weight, tile, lambda n, b: (layer, half + b, 0), (FT, FT),
                        deps=(dn_a,))
            self.last = dn_b
            self.qkv, self.out = over(qkv), over(out)
            self.dn_a, self.dn_b = over(dn_a), over(dn_b)
            self.up_a, self.up_b = over(up_a), over(up_b)
            self.up = (*self.up_a, *self.up_b)
            self.down = (*self.dn_a, *self.dn_b)

    p0 = Pieces(0, ())
    p = [p0]
    kb = key_table(d, parent_ids, depth_offsets)

    def both(rows):
        got = swap(rows, "tp")
        return jnp.where(
            t == 0,
            jnp.concatenate([rows, got], axis=0),
            jnp.concatenate([got, rows], axis=0),
        )

    def row(values):
        return values.reshape(1, -1)

    def swapped(values):
        return swap(values, "tp")

    def fsdp(values):
        return swap(values, "fsdp")

    class Kept:
        pass

    def forward(layer, state, needs):
        k = kept[layer]
        before = [needs(n) for n in range(1)]
        k.hidden, k.n_o, n_s, chunks = qkv_forward(
            d, layer, sc, state, row(norm_gains[layer, 0]), row(row_biases[layer, 0]),
            w_qkv, p[layer].qkv, qv_bias[layer], deps=before[0])
        k.n_r = fsdp(n_s)
        if layer == 0:
            p.append(Pieces(1, (k.hidden,)))
        before += [needs(n) for n in range(1, 3)]
        k.chunks = all_to_all(chunks)
        outs = all_to_all(attend_forward(d, sc, kb, k.chunks, deps=before[1]))
        k.ctx, part = out_forward(d, layer, sc, out_weight, p[layer].out, outs, deps=before[2])
        k.ctx_r = fsdp(k.ctx)
        before.append(needs(3))
        k.middle, k.n2_o, k.act_p, k.act_q, k.dg, part2 = ffn_forward(
            d, layer, sc, k.hidden, part, swapped(part), row(row_biases[layer, 1]),
            row(norm_gains[layer, 1]), row(row_biases[layer, 2]), up_weight,
            p[layer].up, row(up_bias[layer]), down_weight, p[layer].down, deps=before[3])
        state = (k.middle, part2, swapped(part2), row(row_biases[layer, 3]))
        k.act_pr, k.act_qr = fsdp(k.act_p), fsdp(k.act_q)
        return state

    state = both(tokens)
    p0 = p[0]
    kept = [Kept() for _ in range(LAYERS)]
    k0, k1 = kept
    state = forward(0, state, lambda n: (
        (p0.out[0], p0.up_a[0], p0.last) if n == 0
        else (p0.out[1], p0.up_a[1], p0.up_b[0], p0.dn_a[0], p[1].last) if n == 1
        else (p0.dn_b[0], p[1].qkv[0], p[1].out[0]) if n == 2
        else ()
    ))
    p1 = p[1]
    state = forward(1, state, lambda n: (
        (p1.up_a[0],) if n == 0
        else (p1.out[1], p1.up_a[1], p1.up_b[0], p1.dn_a[0]) if n == 1
        else (p1.dn_b[0], k1.n_r, k0.act_pr) if n == 2
        else ()
    ))
    own_rows = tokens.shape[0]

    def mine(values):
        return lax.dynamic_slice_in_dim(values, t * own_rows, own_rows, 0)

    output = mine(state[0]) + (
        (mine(state[1]).astype(F32) + mine(state[2]).astype(F32)) + state[3]
    )
    output = output.astype(BF)
    grad = both(cotangent)
    sums = [None] * LAYERS
    def grad_ffn(k, more, mix, deps=()):
        ins = (k.n2_o, k.act_p, k.act_pr, k.act_q, k.act_qr, k.xba, k.xba_r, k.xbb, k.xbb_r,
               k.db_o)
        jobs = []
        for f in range(tiles):
            at = (5, 1) if f == 0 else (7, f - 1)
            jobs.append(((0, None), at, (2, 0), (at[0] + 1, at[1])))
        for f in range(tiles):
            at = (1, 1 + f) if f < half else (3, f - half)
            jobs.append((at, (9, None), (at[0] + 1, at[1]), (6, 0)))
        if more:
            ins += (k.ctx, k.ctx_r, k.da_o, k.da_r)
            jobs += [((10, None), (12, None), (11, None), (13, None))]
        return Sum(d, mix, *weight_grad(d, "ffn", sc, ins, jobs, mix, deps=deps))

    def grad_qkv(k, more, mix, flat=None, deps=()):
        ins = (k.n_o, k.n_r, k.xc, k.xc_r)
        jobs = [((0, None), (2, n), (1, None), (3, n)) for n in range(3)]
        if more:
            ins += (k.ctx, k.da_o, k.ctx_r, k.da_r)
            jobs += [((4, None), (5, None), (6, None), (7, None))]
        return Sum(d, mix, *weight_grad(d, "qkv", sc, ins, jobs, mix, flat, deps))

    def back_ffn(layer, k, grad, deps=()):
        k.db_o, k.xba, k.xbb, k.usum, k.bsum, part = ffn_backward(
            d, layer, sc, grad, k.dg, up_weight, p[layer].up, down_weight, p[layer].down,
            deps=deps)
        k.xba_r, k.xbb_r = fsdp(k.xba), fsdp(k.xbb)
        return part

    def back_context(layer, k, grad, part, deps=()):
        k.dmid, k.da_o, k.da_s, k.gsum2, k.ssum2, k.asum, dchunks = context_backward(
            d, layer, sc, grad, part, swapped(part), k.middle, row(norm_gains[layer, 1]),
            out_weight, p[layer].out, deps=deps)
        k.da_r = fsdp(k.da_s)
        return dchunks

    def back_qkv(layer, k, dparts, deps=()):
        k.xc, k.qvsum, part = qkv_backward(
            d, layer, sc, w_qkv, p[layer].qkv, dparts, deps=deps)
        k.xc_r = fsdp(k.xc)
        return part

    def back_input(layer, k, part, deps=()):
        grad, k.gsum1, k.ssum1 = input_backward(
            d, k.dmid, part, swapped(part), k.hidden, row(norm_gains[layer, 0]), deps=deps)
        sums[layer] = (k.qvsum, k.usum, k.gsum1, k.gsum2, k.ssum1, k.asum, k.ssum2, k.bsum)
        return grad

    total = LAYERS * (2 * d.W + d.F + 6 * d.D)

    def small_sums():
        flat = jnp.concatenate([v.reshape(-1) for layer in sums for v in layer])
        return jnp.pad(flat, (0, d.C * EXTRA * FT - total)).reshape(d.C, EXTRA, FT)

    part = back_ffn(1, k1, grad, (k0.act_qr, k1.ctx_r))
    dchunks = back_context(1, k1, grad, part, (state[2],))
    dback = attend_backward(d, sc, kb, k1.chunks, all_to_all(dchunks),
                            deps=(k1.act_pr, k1.act_qr))
    dparts = all_to_all(dback)
    f1 = grad_ffn(k1, False, True, (dback,))
    part = back_qkv(1, k1, dparts, (f1.keep,))
    grad = back_input(1, k1, part)
    part = back_ffn(0, k0, grad)
    a = f1.step(part)
    dchunks = back_context(0, k0, grad, part, (a, k1.xc_r))
    q1 = grad_qkv(k1, True, True, None, (dchunks,))
    a = f1.step(q1.keep)
    dback = attend_backward(d, sc, kb, k0.chunks, all_to_all(dchunks),
                            deps=(a, k0.xba_r, k0.ctx_r, k0.n_r))
    dparts = all_to_all(dback)
    f0 = grad_ffn(k0, True, True, (dback,))
    part = back_qkv(0, k0, dparts, (f0.keep,))
    grad = back_input(0, k0, part)
    flat = small_sums()
    flat = flat + swap(flat, "fsdp")
    a = f1.step(grad)
    q0 = grad_qkv(k0, False, False, flat, (a,))
    a = q0.keep
    ffn_kinds = (("cols", tiles), ("mats", tiles))
    qkv_kinds = (("mats", 3), ("mats", 1))
    last = 2 * d.bits - 1
    for unit in (f0, q1, q0, f1, f0, q1, f1, q0, f0, q1, q0, f0, q1, q0):
        if unit.at < last:
            a = unit.step(a)
    while f1.at < last:
        a = f1.step(a)
    g_ffn = place(d, 1, sc, f1, (), ffn_kinds, "ffn", (a,))
    a = g_ffn[0]
    for unit in (q1, q0, f0):
        while unit.at < last:
            a = unit.step(a)
    g_up, g_down, g_out = place(d, 0, sc, f0, (*g_ffn, None), (*ffn_kinds, ("mats", 1)),
                                "ffn", (a,))
    g_qkv, g_out = place(d, 1, sc, q1, (None, g_out), qkv_kinds, "qkv", (g_up,))
    g_qkv, qv_grad, up_grad, gain_grad, bias_grad = place(
        d, 0, sc, q0, (g_qkv,), (("mats", 3),), "qkv", (g_out,))
    return (
        output,
        mine(grad),
        g_qkv.transpose(0, 2, 1, 3),
        g_out.reshape(LAYERS, d.W, d.H),
        g_up.reshape(LAYERS, d.H, d.F),
        g_down.reshape(LAYERS, d.F, d.H),
        qv_grad,
        up_grad,
        gain_grad,
        bias_grad,
    )


def solution(mesh):
    in_specs = (
        P(("fsdp", "ctx", "tp"), None),
        P(None, "fsdp", None, "tp"),
        P(None, "tp", "fsdp"),
        P(None, "fsdp", "tp"),
        P(None, "tp", "fsdp"),
        P(None, None, "tp"),
        P(None, "tp"),
        P(),
        P(),
        P(),
        P(),
        P(("fsdp", "ctx", "tp"), None),
    )
    out_specs = (
        P(("fsdp", "ctx", "tp"), None),
        P(("fsdp", "ctx", "tp"), None),
        P(None, "fsdp", None, "tp"),
        P(None, "tp", "fsdp"),
        P(None, "fsdp", "tp"),
        P(None, "tp", "fsdp"),
        P(None, None, "tp"),
        P(None, "tp"),
        P(),
        P(),
    )
    return jax.shard_map(
        on_device, mesh=mesh, in_specs=in_specs, out_specs=out_specs, check_vma=False
    )
```

```python
import functools

import jax
import jax.numpy as jnp
from jax import lax
from jax.experimental import pallas as pl
from jax.experimental.pallas import tpu as pltpu
from jax.sharding import PartitionSpec as P

HEAD_DIM = 128
LAYERS = 2
SEG = 128
EPSILON = 1e-05
MASKED = -1e30
SCALE = HEAD_DIM ** (-0.5)
GELU_A = 0.7978845608028654
GELU_B = 0.044715
BF = jnp.bfloat16
F32 = jnp.float32
VLIM = 56 * 1024 * 1024

NN = (((1,), (0,)), ((), ()))
NT = (((1,), (1,)), ((), ()))
TN = (((0,), (0,)), ((), ()))


def mm(a, b, dims=NN):
    return lax.dot_general(a, b, dims, preferred_element_type=F32)


def sds(shape, dtype):
    return jax.ShapeDtypeStruct(shape, dtype)


VSPEC = pl.BlockSpec(memory_space=pltpu.VMEM)
SSPEC = pl.BlockSpec(memory_space=pltpu.SMEM)


def cost(flops, nbytes):
    return pl.CostEstimate(flops=int(flops), bytes_accessed=int(nbytes), transcendentals=0)


def kernel_call(body, args, in_specs, out_specs, out_shape, name, scratch=(), grid=None,
                deps=(), work=None, aliases=None):
    count, extra = len(args), len(deps)

    def ordered(*refs):
        body(*refs[:count], *refs[count + extra :])

    kwargs = {} if grid is None else {"grid": grid}
    return pl.pallas_call(
        ordered,
        in_specs=list(in_specs) + [pl.BlockSpec(memory_space=pl.ANY)] * extra,
        out_specs=out_specs,
        out_shape=out_shape,
        scratch_shapes=list(scratch),
        input_output_aliases=aliases or {},
        compiler_params=pltpu.CompilerParams(vmem_limit_bytes=VLIM),
        cost_estimate=work,
        name=name,
        **kwargs,
    )(*args, *deps)


def norm_rows(v):
    centered = v - jnp.mean(v, axis=-1, keepdims=True)
    rstd = lax.rsqrt(jnp.mean(centered * centered, axis=-1, keepdims=True) + EPSILON)
    return centered * rstd, rstd


def norm_back(d, v, gain):
    xhat, rstd = norm_rows(v)
    dx = d * gain
    back = rstd * (
        dx
        - jnp.mean(dx, axis=-1, keepdims=True)
        - xhat * jnp.mean(dx * xhat, axis=-1, keepdims=True)
    )
    d_gain = jnp.sum(d * xhat, axis=0, keepdims=True)
    d_shift = jnp.sum(d, axis=0, keepdims=True)
    return back, d_gain, d_shift


class Dims:
    def __init__(self, tokens, qkv_weight, up_weight):
        self.tp = lax.axis_size("tp")
        self.C = lax.axis_size("ctx")
        self.T = tokens.shape[0] * self.tp
        self.D = tokens.shape[1]
        self.H = self.D // lax.axis_size("fsdp")
        self.Q = self.H // 2
        self.W = qkv_weight.shape[3]
        self.F = up_weight.shape[2]
        self.lh = self.W // HEAD_DIM
        self.g = self.C // self.lh
        self.rq = self.T // self.g
        self.chunk = self.rq + 2 * self.T
        self.bits = self.C.bit_length() - 1


def offs(sc, d):
    x = sc[0]
    y = sc[1]
    own = pl.multiple_of(x * d.H, d.H)
    oth = pl.multiple_of((1 - x) * d.H, d.H)
    first = pl.multiple_of((1 - x) * d.H + y * d.Q, d.Q)
    second = pl.multiple_of((1 - x) * d.H + (1 - y) * d.Q, d.Q)
    return own, oth, first, second


def spot_of(d, chip):
    row, head = (chip % d.g) * d.rq, (chip // d.g) * HEAD_DIM
    return slice(row, row + d.rq), slice(head, head + HEAD_DIM)


def qkv_body(d, first, *refs):
    if first:
        sc, hid, gain, shift, w, w1, w2, qvb = refs[:8]
        rest = refs[8:]
        hidden = hid[...].astype(F32)
    else:
        sc, mid, pa, pb, bias, gain, shift, w, w1, w2, qvb = refs[:11]
        rest = refs[11:]
        hidden = mid[...] + ((pa[...].astype(F32) + pb[...].astype(F32)) + bias[...])
    h_out, no_out, ns_out, chunks, n_out, scr = rest
    own, oth, p1, p2 = offs(sc, d)
    h_out[...] = hidden
    xhat, _ = norm_rows(hidden)
    n_out[...] = (xhat * gain[...] + shift[...]).astype(BF)
    ns_out[...] = n_out[:, pl.ds(oth, d.H)]
    a0 = n_out[:, pl.ds(own, d.H)]
    no_out[...] = a0
    a1 = n_out[:, pl.ds(p1, d.Q)]
    a2 = n_out[:, pl.ds(p2, d.Q)]
    for n in range(3):
        proj = mm(a0, w[n]) + mm(a1, w1[n]) + mm(a2, w2[n])
        if n == 0:
            proj = proj + qvb[0:1, :]
        if n == 2:
            proj = proj + qvb[1:2, :]
        scr[n] = proj.astype(BF)
    for to in range(d.C):
        row, col = spot_of(d, to)
        chunks[to, 0 : d.rq, :] = scr[0, row, col]
        chunks[to, d.rq : d.rq + d.T, :] = scr[1, :, col]
        chunks[to, d.rq + d.T :, :] = scr[2, :, col]


def whole(shape):
    return pl.BlockSpec(shape, lambda *_: (0,) * len(shape))


def piece_specs(shape, pieces, axis):
    if pieces[0] is not pieces[1]:
        return [whole(shape), whole(shape)]
    second = tuple(1 if k == axis else 0 for k in range(len(shape)))
    return [whole(shape), pl.BlockSpec(shape, lambda *_: second)]


def qkv_forward(d, layer, sc, hid, gain, shift, w, pieces, qvb, deps=()):
    first = not isinstance(hid, tuple)
    hid = (hid,) if first else hid
    wspec = pl.BlockSpec((None, 3, d.H, d.W), lambda i: (layer, 0, 0, 0))
    in_specs = [SSPEC] + [whole(a.shape) for a in hid]
    in_specs += [whole(gain.shape), whole(shift.shape), wspec]
    in_specs += piece_specs((3, d.Q, d.W), pieces, 1) + [whole(qvb.shape)]
    outs = [sds((d.T, d.D), F32), sds((d.T, d.H), BF), sds((d.T, d.H), BF)]
    outs += [sds((d.C, d.chunk, HEAD_DIM), BF)]
    return kernel_call(
        functools.partial(qkv_body, d, first),
        (sc, *hid, gain, shift, w, *pieces, qvb,),
        grid=(1,),
        in_specs=in_specs,
        out_specs=[whole(o.shape) for o in outs],
        out_shape=outs,
        scratch=[pltpu.VMEM((d.T, d.D), BF), pltpu.VMEM((3, d.T, d.W), BF)],
        work=cost(2 * d.T * d.D * 3 * d.W, 8e6),
        name="qkv_forward",
        deps=deps,
    )


def load_chunks(d, sc, chunks, qs, ks, vs):
    qs[...] = chunks[:, 0 : d.rq, :]
    ks[...] = chunks[:, d.rq : d.rq + d.T, :]
    vs[...] = chunks[:, d.rq + d.T :, :]


def score_block(d, sc, kb, q, k, s, ext):
    part = lax.rem(sc[2], d.g)
    seg = s * (d.T // SEG) + lax.div(part * d.rq, SEG)
    scores = mm(q, k, NT) * SCALE + kb[pl.ds(seg, 1), 0:ext]
    col = lax.broadcasted_iota(jnp.int32, (d.rq, ext), 1) - s * d.T
    row = lax.broadcasted_iota(jnp.int32, (d.rq, ext), 0) + part * d.rq
    return jnp.where(col <= row, scores, MASKED)


UNROLL = 8
SHIFT = 3


def each_source(d, one):
    if d.C <= UNROLL:
        for s in range(d.C):
            one(s, s + 1)
    else:
        lax.fori_loop(0, d.C, lambda s, carry: (one(s, d.C), carry)[1], 0)


def attend_body(d, *refs):
    sc, kb, chunks, cs, qs, ks, vs = refs
    load_chunks(d, sc, chunks, qs, ks, vs)
    def one(s, seen):
        ext = seen * d.T
        k = ks[0:seen].reshape(ext, HEAD_DIM)
        v = vs[0:seen].reshape(ext, HEAD_DIM)
        scores = score_block(d, sc, kb, qs[s], k, s, ext)
        e = jnp.exp(scores - jnp.max(scores, axis=-1, keepdims=True))
        total = jnp.sum(e, axis=-1, keepdims=True)
        cs[s] = (mm(e.astype(BF), v) / total).astype(BF)

    each_source(d, one)


def attend_forward(d, sc, kb, chunks, deps=()):
    return kernel_call(
        functools.partial(attend_body, d),
        (sc, kb, chunks,),
        in_specs=[SSPEC] + [VSPEC] * 2,
        out_specs=VSPEC,
        out_shape=sds((d.C, d.rq, HEAD_DIM), BF),
        scratch=[
            pltpu.VMEM((d.C, d.rq, HEAD_DIM), BF),
            pltpu.VMEM((d.C, d.T, HEAD_DIM), BF),
            pltpu.VMEM((d.C, d.T, HEAD_DIM), BF),
        ],
        work=cost(2 * d.C * d.rq * d.C * d.T * HEAD_DIM * 2, 3e6),
        name="attend_forward",
        deps=deps,
    )


def out_body(d, *refs):
    sc, w, w1, w2, chunks, ctx, part = refs
    for src in range(d.C):
        ctx[spot_of(d, src)] = chunks[src]
    own, oth, _, _ = offs(sc, d)
    half = d.W // 2
    k1 = pl.multiple_of(sc[1] * half, half)
    k2 = pl.multiple_of((1 - sc[1]) * half, half)
    part[:, pl.ds(own, d.H)] = mm(ctx[...], w[...]).astype(BF)
    part[:, pl.ds(oth, d.H)] = (
        mm(ctx[:, pl.ds(k1, half)], w1[...]) + mm(ctx[:, pl.ds(k2, half)], w2[...])
    ).astype(BF)


def out_forward(d, layer, sc, w, pieces, chunks, deps=()):
    wspec = pl.BlockSpec((None, d.W, d.H), lambda i: (layer, 0, 0))
    outs = [sds((d.T, d.W), BF), sds((d.T, d.D), BF)]
    return kernel_call(
        functools.partial(out_body, d),
        (sc, w, *pieces, chunks,),
        grid=(1,),
        in_specs=[SSPEC, wspec] + piece_specs((d.W // 2, d.H), pieces, 0)
        + [whole(chunks.shape)],
        out_specs=[whole(o.shape) for o in outs],
        out_shape=outs,
        work=cost(2 * d.T * d.D * d.W, 3e6),
        name="out_forward",
        deps=deps,
    )


FT = 512


def tile_of(f, sc, tiles, refs, use):
    half = tiles // 2
    mine = lax.rem(f, half) == sc[1]
    for number, (came, then) in enumerate((refs[:2], refs[2:])):
        here = lax.div(f, half) == number

        @pl.when(jnp.logical_and(here, mine))
        def _():
            use(came)

        @pl.when(jnp.logical_and(here, jnp.logical_not(mine)))
        def _():
            use(then)


def ffn_body(d, tiles, sc, hid, pa, pb, bias, gain, shift,
             u, u1, u2, u3, u4, ub, w, w1, w2, w3, w4,
             mid, no, act_p, act_q, dg, part, n2, acc, pre):
    f = pl.program_id(0)
    own, oth, _, _ = offs(sc, d)

    @pl.when(f == 0)
    def _():
        m = hid[...] + ((pa[...].astype(F32) + pb[...].astype(F32)) + bias[...])
        mid[...] = m
        xhat, _ = norm_rows(m)
        n2[...] = (xhat * gain[...] + shift[...]).astype(BF)
        no[...] = n2[:, pl.ds(own, d.H)]
        act_p[0] = n2[:, pl.ds(oth, d.H)]
        acc[...] = jnp.zeros_like(acc)

    def up(ref):
        pre[...] = mm(act_p[0], ref[...])

    tile_of(f, sc, tiles, (u1, u2, u3, u4), up)
    v = pre[...] + mm(no[...], u[...]) + ub[...]
    sq = v * v
    th = jnp.tanh(GELU_A * v * (1.0 + GELU_B * sq))
    half = 0.5 * (1.0 + th)
    a = (v * half).astype(BF)

    @pl.when(f < tiles // 2)
    def _():
        act_p[1 + f] = a

    @pl.when(f >= tiles // 2)
    def _():
        act_q[f - tiles // 2] = a

    dg[...] = (
        half + 0.5 * v * (1.0 - th * th) * (GELU_A * (1.0 + 3.0 * GELU_B * sq))
    ).astype(BF)
    acc[0] += mm(a, w[...])

    def down(ref):
        acc[1] += mm(a, ref[...])

    tile_of(f, sc, tiles, (w1, w2, w3, w4), down)

    @pl.when(f == tiles - 1)
    def _():
        part[:, pl.ds(own, d.H)] = acc[0].astype(BF)
        part[:, pl.ds(oth, d.H)] = acc[1].astype(BF)


def ffn_specs(d, layer):
    u = pl.BlockSpec((None, d.H, FT), lambda f: (layer, 0, f))
    w = pl.BlockSpec((None, FT, d.H), lambda f: (layer, f, 0))
    return [u] + [whole((d.H, FT))] * 4, [w] + [whole((FT, d.H))] * 4


def ffn_forward(d, layer, sc, hid, pa, pb, bias, gain, shift,
                up_w, up_p, ub, dn_w, dn_p, deps=()):
    tiles = d.F // FT
    us, ws = ffn_specs(d, layer)
    side = whole((d.T, d.H))
    col = pl.BlockSpec((d.T, FT), lambda f: (0, f))
    row = whole((1, d.D))
    full = whole((d.T, d.D))
    act_p = sds((1 + tiles // 2, d.T, FT), BF)
    act_q = sds((tiles // 2, d.T, FT), BF)
    return kernel_call(
        functools.partial(ffn_body, d, tiles),
        (sc, hid, pa, pb, bias, gain, shift, up_w, *up_p, ub, dn_w, *dn_p),
        [SSPEC, full, full, full, row, row, row, *us,
         pl.BlockSpec((1, FT), lambda f: (0, f)), *ws],
        [full, side, whole(act_p.shape), whole(act_q.shape), col, full],
        [sds((d.T, d.D), F32), sds((d.T, d.H), BF), act_p, act_q,
         sds((d.T, d.F), BF), sds((d.T, d.D), BF)],
        "ffn_forward",
        scratch=[pltpu.VMEM((d.T, d.D), BF), pltpu.VMEM((2, d.T, d.H), F32),
                 pltpu.VMEM((d.T, FT), F32)],
        grid=(tiles,), deps=deps, work=cost(4 * d.T * d.D * d.F, 14e6))


def ffn_back_body(d, tiles, sc, grad, dg, u, u1, u2, u3, u4, w, w1, w2, w3, w4,
                  dbo, xba, xbb, usum, bsum, part, acc, dact):
    f = pl.program_id(0)
    own, oth, _, _ = offs(sc, d)

    @pl.when(f == 0)
    def _():
        dbo[...] = grad[:, pl.ds(own, d.H)].astype(BF)
        xba[0] = grad[:, pl.ds(oth, d.H)].astype(BF)
        bsum[...] = jnp.sum(grad[...].astype(BF).astype(F32), axis=0, keepdims=True)
        acc[...] = jnp.zeros_like(acc)

    def down(ref):
        dact[...] = mm(xba[0], ref[...], NT)

    tile_of(f, sc, tiles, (w1, w2, w3, w4), down)
    da = dact[...] + mm(dbo[...], w[...], NT)
    dp = (da * dg[...].astype(F32)).astype(BF)

    @pl.when(f == 0)
    def _():
        xba[1] = dp

    @pl.when(f > 0)
    def _():
        xbb[f - 1] = dp

    usum[...] = jnp.sum(dp.astype(F32), axis=0, keepdims=True)
    acc[0] += mm(dp, u[...], NT)

    def up(ref):
        acc[1] += mm(dp, ref[...], NT)

    tile_of(f, sc, tiles, (u1, u2, u3, u4), up)

    @pl.when(f == tiles - 1)
    def _():
        part[:, pl.ds(own, d.H)] = acc[0].astype(BF)
        part[:, pl.ds(oth, d.H)] = acc[1].astype(BF)


def ffn_backward(d, layer, sc, grad, dg, up_w, up_p, dn_w, dn_p, deps=()):
    tiles = d.F // FT
    us, ws = ffn_specs(d, layer)
    side = whole((d.T, d.H))
    col = pl.BlockSpec((d.T, FT), lambda f: (0, f))
    full = whole((d.T, d.D))
    xba = sds((2, d.T, FT), BF)
    xbb = sds((tiles - 1, d.T, FT), BF)
    return kernel_call(
        functools.partial(ffn_back_body, d, tiles),
        (sc, grad, dg, up_w, *up_p, dn_w, *dn_p),
        [SSPEC, full, col, *us, *ws],
        [side, whole(xba.shape), whole(xbb.shape),
         pl.BlockSpec((1, FT), lambda f: (0, f)), whole((1, d.D)), full],
        [sds((d.T, d.H), BF), xba, xbb,
         sds((1, d.F), F32), sds((1, d.D), F32), sds((d.T, d.D), BF)],
        "ffn_backward",
        scratch=[pltpu.VMEM((2, d.T, d.H), F32), pltpu.VMEM((d.T, FT), F32)],
        grid=(tiles,), deps=deps, work=cost(4 * d.T * d.D * d.F, 14e6))


def context_back_body(d, *refs):
    sc, grad, pa, pb, mid, gain, w, w1, w2 = refs[:9]
    dmid, dao, das, gsum, ssum, asum, chunks, da, dctx = refs[9:]
    own, oth, _, _ = offs(sc, d)
    back, g, s = norm_back(pa[...].astype(F32) + pb[...].astype(F32), mid[...], gain[...])
    gsum[...] = g
    ssum[...] = s
    total = grad[...].astype(F32) + back
    dmid[...] = total
    da[...] = total.astype(BF)
    dao[...] = da[:, pl.ds(own, d.H)]
    das[...] = da[:, pl.ds(oth, d.H)]
    asum[...] = jnp.sum(da[...].astype(F32), axis=0, keepdims=True)
    half = d.W // 2
    k1 = pl.multiple_of(sc[1] * half, half)
    k2 = pl.multiple_of((1 - sc[1]) * half, half)
    dctx[...] = mm(da[:, pl.ds(own, d.H)], w[...], NT)
    dctx[:, pl.ds(k1, half)] += mm(da[:, pl.ds(oth, d.H)], w1[...], NT)
    dctx[:, pl.ds(k2, half)] += mm(da[:, pl.ds(oth, d.H)], w2[...], NT)
    for to in range(d.C):
        chunks[to] = dctx[spot_of(d, to)].astype(BF)


def context_backward(d, layer, sc, grad, pa, pb, mid, gain, w, pieces, deps=()):
    wspec = pl.BlockSpec((None, d.W, d.H), lambda i: (layer, 0, 0))
    outs = [sds((d.T, d.D), F32), sds((d.T, d.H), BF), sds((d.T, d.H), BF)]
    outs += [sds((1, d.D), F32)] * 3 + [sds((d.C, d.rq, HEAD_DIM), BF)]
    return kernel_call(
        functools.partial(context_back_body, d),
        (sc, grad, pa, pb, mid, gain, w, *pieces,),
        grid=(1,),
        in_specs=[SSPEC] + [whole(a.shape) for a in (grad, pa, pb, mid, gain)]
        + [wspec] + piece_specs((d.W // 2, d.H), pieces, 0),
        out_specs=[whole(o.shape) for o in outs],
        out_shape=outs,
        scratch=[pltpu.VMEM((d.T, d.D), BF), pltpu.VMEM((d.T, d.W), F32)],
        work=cost(2 * d.T * d.D * d.W, 6e6),
        name="context_backward",
        deps=deps,
    )


def attend_back_body(d, *refs):
    sc, kb, chunks, cs, outs, qs, ks, vs, dks, dvs = refs
    load_chunks(d, sc, chunks, qs, ks, vs)
    dks[...] = jnp.zeros_like(dks)
    dvs[...] = jnp.zeros_like(dvs)
    def one(s, seen):
        ext = seen * d.T
        k = ks[0:seen].reshape(ext, HEAD_DIM)
        v = vs[0:seen].reshape(ext, HEAD_DIM)
        q = qs[s]
        dc = cs[s]
        scores = score_block(d, sc, kb, q, k, s, ext)
        e = jnp.exp(scores - jnp.max(scores, axis=-1, keepdims=True))
        p = e / jnp.sum(e, axis=-1, keepdims=True)
        dp = mm(dc, v, NT)
        ds = (p * (dp - jnp.sum(p * dp, axis=-1, keepdims=True))).astype(BF)
        outs[s, 0 : d.rq, :] = (mm(ds, k) * SCALE).astype(BF)
        dks[0:seen] += mm(ds, q, TN).reshape(seen, d.T, HEAD_DIM)
        dvs[0:seen] += mm(p.astype(BF), dc, TN).reshape(seen, d.T, HEAD_DIM)

    each_source(d, one)
    outs[:, d.rq : d.rq + d.T, :] = (dks[...] * SCALE).astype(BF)
    outs[:, d.rq + d.T :, :] = dvs[...].astype(BF)


def attend_backward(d, sc, kb, chunks, dchunks, deps=()):
    return kernel_call(
        functools.partial(attend_back_body, d),
        (sc, kb, chunks, dchunks,),
        in_specs=[SSPEC] + [VSPEC] * 3,
        out_specs=VSPEC,
        out_shape=sds((d.C, d.chunk, HEAD_DIM), BF),
        scratch=[
            pltpu.VMEM((d.C, d.rq, HEAD_DIM), BF),
            pltpu.VMEM((d.C, d.T, HEAD_DIM), BF),
            pltpu.VMEM((d.C, d.T, HEAD_DIM), BF),
            pltpu.VMEM((d.C, d.T, HEAD_DIM), F32),
            pltpu.VMEM((d.C, d.T, HEAD_DIM), F32),
        ],
        work=cost(5 * d.C * d.rq * d.C * d.T * HEAD_DIM * 2, 4e6),
        name="attend_backward",
        deps=deps,
    )


def qkv_back_body(d, sc, w, w1, w2, chunks, xb, qvsum, part, dk, dv):
    dk[...] = jnp.zeros_like(dk)
    dv[...] = jnp.zeros_like(dv)
    for src in range(d.C):
        row, col = spot_of(d, src)
        xb[0, row, col] = chunks[src, 0 : d.rq, :]
        dk[:, col] += chunks[src, d.rq : d.rq + d.T, :].astype(F32)
        dv[:, col] += chunks[src, d.rq + d.T :, :].astype(F32)
    xb[1] = dk[...].astype(BF)
    xb[2] = dv[...].astype(BF)
    qvsum[0:1, :] = jnp.sum(xb[0].astype(F32), axis=0, keepdims=True)
    qvsum[1:2, :] = jnp.sum(xb[2].astype(F32), axis=0, keepdims=True)
    own, _, p1, p2 = offs(sc, d)
    for ref, at, width in ((w, own, d.H), (w1, p1, d.Q), (w2, p2, d.Q)):
        total = mm(xb[0], ref[0], NT) + mm(xb[1], ref[1], NT) + mm(xb[2], ref[2], NT)
        part[:, pl.ds(at, width)] = total.astype(BF)


def qkv_backward(d, layer, sc, w, pieces, chunks, deps=()):
    wspec = pl.BlockSpec((None, 3, d.H, d.W), lambda i: (layer, 0, 0, 0))
    outs = [sds((3, d.T, d.W), BF), sds((2, d.W), F32), sds((d.T, d.D), BF)]
    return kernel_call(
        functools.partial(qkv_back_body, d),
        (sc, w, *pieces, chunks),
        [SSPEC, wspec] + [whole((3, d.Q, d.W))] * 2 + [whole(chunks.shape)],
        [whole(o.shape) for o in outs],
        outs,
        "qkv_backward",
        scratch=[pltpu.VMEM((d.T, d.W), F32)] * 2,
        grid=(1,), deps=deps, work=cost(2 * d.T * d.D * 3 * d.W, 7e6))


def input_back_body(dmid, pa, pb, hid, gain, grad, gsum, ssum):
    back, g, s = norm_back(pa[...].astype(F32) + pb[...].astype(F32), hid[...], gain[...])
    grad[...] = dmid[...] + back
    gsum[...] = g
    ssum[...] = s


def input_backward(d, dmid, pa, pb, hid, gain, deps=()):
    return kernel_call(
        input_back_body,
        (dmid, pa, pb, hid, gain,),
        in_specs=[VSPEC] * 5,
        out_specs=[VSPEC] * 3,
        out_shape=[sds((d.T, d.D), F32)] + [sds((1, d.D), F32)] * 2,
        work=cost(3e6, 5e6),
        name="input_backward",
        deps=deps,
    )


def spot_bits(value, shifts, bits):
    out = 0
    for k in range(bits):
        bit = lax.bitwise_and(lax.shift_right_logical(value, shifts[k]), 1)
        out = out + bit * (1 << (bits - 1 - k))
    return out


EXTRA = 16


def shift_at(d, mix):
    return SHIFT + d.bits * (2 if mix == "z" else 0 if mix else 1)


def wgrad_body(d, tiles, mix, flat, sc, *refs):
    ins = refs[:-2]
    keep, send = refs[-2:]
    c = sc[2]
    shifts = [sc[shift_at(d, mix) + k] for k in range(d.bits)]
    rb = FT // d.C
    spots = [spot_bits(lax.bitwise_xor(c, b), shifts, d.bits) for b in range(d.C)]

    def pick(item):
        ref, at = item
        return ins[ref][...] if at is None else ins[ref][at]

    def put(spot, low, piece):
        @pl.when(spot < d.C // 2)
        def _():
            keep[spot, low : low + piece.shape[0]] = piece

        @pl.when(spot >= d.C // 2)
        def _():
            send[spot - d.C // 2, low : low + piece.shape[0]] = piece

    for m, (a, b, a2, b2) in enumerate(tiles):
        total = mm(pick(a), pick(b), TN) + mm(pick(a2), pick(b2), TN)
        total = total.astype(BF)
        for block, spot in enumerate(spots):
            put(spot, m * rb, total[block * rb : (block + 1) * rb, :])
    if flat is not None:
        for block, spot in enumerate(spots):
            put(spot, len(tiles) * rb, ins[flat][block].astype(BF))


def weight_grad(d, name, sc, ins, tiles, mix, flat=None, deps=()):
    rows = len(tiles) * (FT // d.C)
    if flat is not None:
        ins = (*ins, flat)
        rows += EXTRA
    return kernel_call(
        functools.partial(wgrad_body, d, tiles, mix, None if flat is None else len(ins) - 1),
        (sc, *ins),
        [SSPEC] + [VSPEC] * len(ins),
        [VSPEC] * 2,
        [sds((d.C // 2, rows, FT), BF)] * 2,
        "weight_grad_" + name,
        deps=deps, work=cost(4 * d.T * len(tiles) * FT * FT, 8e6))


def small_rows(d):
    return (2, 1, 2, 4), (d.W // FT, d.F // FT, d.D // FT, d.D // FT)


def place_body(d, wide, count_in, extra, layer, owner, flat, sc, *refs):
    ins = refs[:count_in]
    outs = refs[count_in + extra : -3]
    buf, small, sems = refs[-3:]
    rb = FT // d.C
    nt = buf.shape[0]
    r = 0
    for part in ins:
        for n in range(part.shape[0]):
            block = owner(sc, r)
            row = pl.multiple_of(block * rb, rb)
            for m in range(nt):
                buf[m, pl.ds(row, rb), :] = part[n, m * rb : (m + 1) * rb].astype(F32)
            if flat:
                small[block] = part[n, nt * rb :].astype(F32)
            r += 1
    if flat:
        at = 0
        for k in range(LAYERS):
            for out, rows, pieces in zip(outs[len(wide) :], *small_rows(d)):
                for row in range(rows):
                    for piece in range(pieces):
                        line = small[at // EXTRA, at % EXTRA : at % EXTRA + 1, :]
                        lanes = slice(piece * FT, (piece + 1) * FT)
                        if rows == 1:
                            out[k : k + 1, lanes] = line
                        else:
                            out[k, row : row + 1, lanes] = line
                        at += 1
    copies = []
    m = 0
    for out, (kind, count) in zip(outs, wide):
        if kind == "cols":
            for k in range(count):
                copies.append((buf.at[m + k], out.at[layer, :, pl.ds(k * FT, FT)]))
        else:
            copies.append((buf.at[pl.ds(m, count)], out.at[layer]))
        m += count
    going = [pltpu.make_async_copy(a, b, sems.at[k]) for k, (a, b) in enumerate(copies)]
    for one in going:
        one.start()
    for one in going:
        one.wait()


def place(d, layer, sc, unit, before, wide, name, deps=()):
    parts = unit.finish()
    nt = sum(n for _, n in wide)
    flat = parts[0].shape[1] > nt * (FT // d.C)
    held = [k for k, one in enumerate(before) if one is not None]
    extra = tuple(before[k] for k in held) + tuple(deps)
    alias = {1 + len(parts) + n: k for n, k in enumerate(held)}
    shapes = [
        sds((LAYERS, FT, n * FT) if kind == "cols" else (LAYERS, n, FT, FT), F32)
        for kind, n in wide
    ]
    specs = [pl.BlockSpec(memory_space=pl.ANY)] * len(wide)
    if flat:
        for rows, pieces in zip(*small_rows(d)):
            one = (rows, pieces * FT) if rows > 1 else (pieces * FT,)
            shapes.append(sds((LAYERS, *one), F32))
            specs.append(VSPEC)
    moves = sum(n if kind == "cols" else 1 for kind, n in wide)
    at = shift_at(d, unit.mix)

    def owner(scalars, r):
        turned = 0
        for k in range(d.bits):
            if r >> (d.bits - 1 - k) & 1:
                turned = turned + lax.shift_left(jnp.int32(1), scalars[at + k])
        return lax.bitwise_xor(scalars[2], jnp.int32(turned))

    return pl.pallas_call(
        functools.partial(place_body, d, wide, len(parts), len(extra), layer, owner, flat),
        in_specs=[SSPEC] + [VSPEC] * len(parts) + [pl.BlockSpec(memory_space=pl.ANY)] * len(extra),
        out_specs=specs,
        out_shape=shapes,
        scratch_shapes=[
            pltpu.VMEM((nt, FT, FT), F32),
            pltpu.VMEM((d.C, EXTRA, FT), F32),
            pltpu.SemaphoreType.DMA((moves,)),
        ],
        input_output_aliases=alias,
        compiler_params=pltpu.CompilerParams(vmem_limit_bytes=VLIM),
        name="place_" + name,
    )(sc, *parts, *extra)


def swap(values, axis):
    return lax.ppermute(values, axis, [(0, 1), (1, 0)])


def way(d, core, step, mix=True):
    if mix and step < 2 and d.bits > 1:
        return step if core == 0 and mix != "z" else 1 - step
    return step


def cross(d, values, step, mix=True):
    pairs = []
    for i in range(d.C):
        for core in range(d.tp):
            to = i ^ (1 << way(d, core, step, mix))
            pairs.append((i * d.tp + core, to * d.tp + core))
    return lax.ppermute(values, ("ctx", "tp"), pairs)


def take_body(sc, w, *refs):
    refs[-1][...] = w[...]


def take(sc, w, block, index, shape, steps=1, deps=()):
    out_block = shape if steps == 1 else (None, *shape[1:])
    return pl.pallas_call(
        take_body,
        grid_spec=pltpu.PrefetchScalarGridSpec(
            num_scalar_prefetch=1,
            grid=(steps,),
            in_specs=[pl.BlockSpec(block, lambda n, s: index(n, s[1]))]
            + [pl.BlockSpec(memory_space=pl.ANY)] * len(deps),
            out_specs=pl.BlockSpec(out_block, lambda n, s: (n,) + (0,) * (len(shape) - 1)),
        ),
        out_shape=sds(shape, BF),
        compiler_params=pltpu.CompilerParams(vmem_limit_bytes=VLIM),
        name="take",
    )(sc, w, *deps)


def fold_body(keep, got, *outs):
    total = (keep[...].astype(F32) + got[...].astype(F32)).astype(BF)
    if len(outs) == 1:
        outs[0][...] = total
    else:
        half = total.shape[0] // 2
        outs[0][...] = total[:half]
        outs[1][...] = total[half:]


def fold(keep, got, deps=()):
    count = keep.shape[0]
    shapes = [keep.shape] if count == 1 else [(count // 2, *keep.shape[1:])] * 2
    return kernel_call(
        fold_body, (keep, got), [VSPEC] * 2, [VSPEC] * len(shapes),
        [sds(v, BF) for v in shapes], "fold", deps=deps, work=cost(1e6, 3e6))


def join_body(*refs):
    out = refs[-1]
    at = 0
    for ref in refs[:-1]:
        out[at : at + ref.shape[0]] = ref[...]
        at += ref.shape[0]


def join(parts, deps=()):
    if len(parts) == 1:
        return parts[0]
    count = sum(p.shape[0] for p in parts)
    return kernel_call(
        join_body, tuple(parts), [VSPEC] * len(parts), VSPEC,
        sds((count, *parts[0].shape[1:]), BF), "join", deps=deps, work=cost(1e5, 3e6))


class Sum:
    def __init__(self, d, mix, keep, send):
        self.d, self.mix = d, mix
        self.keep = keep
        self.got = cross(d, send, 0, mix)
        self.at = 0
        self.parts = None

    def step(self, *deps):
        self.at += 1
        n = self.d.bits
        if self.at < n:
            keep, send = fold(self.keep, self.got, deps)
            self.keep = keep
            self.got = cross(self.d, send, self.at, self.mix)
            return keep
        if self.at == n:
            (keep,) = fold(self.keep, self.got, deps)
            self.parts = [keep]
            self.got = cross(self.d, keep, n - 1, self.mix)
            return keep
        self.parts.append(self.got)
        if self.at < 2 * n:
            full = join(self.parts, deps)
            self.got = cross(self.d, full, 2 * n - 1 - self.at, self.mix)
            return full
        return self.got

    def finish(self):
        while self.at < 2 * self.d.bits:
            self.step()
        return self.parts


def all_to_all(values):
    return lax.all_to_all(values, "ctx", 0, 0)


def key_table(d, parent_ids, depth_offsets):
    segs = parent_ids.shape[0] // lax.axis_size("fsdp")
    start = lax.axis_index("fsdp") * segs
    parents = lax.dynamic_slice_in_dim(parent_ids, start, segs) - start
    depths = lax.dynamic_slice_in_dim(depth_offsets, start, segs).astype(F32)
    ids = jnp.arange(segs, dtype=jnp.int32)
    reach = jnp.maximum(
        (parents[:, None] == ids[None, :]).astype(F32), (ids[:, None] == ids[None, :]).astype(F32)
    )
    for _ in range((segs - 1).bit_length()):
        reach = jnp.minimum(jnp.dot(reach, reach), 1.0)
    head = lax.axis_index("tp") * d.lh + lax.axis_index("ctx") // d.g
    slope = jnp.exp2(-(head + 1).astype(F32))
    level = jnp.where(reach > 0.5, slope * (depths[None, :] - depths[:, None]), MASKED)
    spots = slope * jnp.arange(SEG, dtype=jnp.int32).astype(F32)
    return (level[:, :, None] + spots[None, None, :]).reshape(segs, segs * SEG)


def on_device(tokens, qkv_weight, out_weight, up_weight, down_weight, qv_bias, up_bias,
              norm_gains, row_biases, parent_ids, depth_offsets, cotangent):
    d = Dims(tokens, qkv_weight, up_weight)
    x = lax.axis_index("fsdp")
    c = lax.axis_index("ctx")
    t = lax.axis_index("tp")
    first = [jnp.where(t == 0, way(d, 0, k), way(d, 1, k)) for k in range(d.bits)]
    bit = (c >> first[0]) % 2
    turned = [way(d, 0, k, "z") for k in range(d.bits)]
    sc = jnp.stack([x, bit, c, *first, *range(d.bits), *turned]).astype(jnp.int32)
    w_qkv = qkv_weight.transpose(0, 2, 1, 3)
    tiles = d.F // FT
    half = tiles // 2

    class Pieces:
        def __init__(self, layer, deps):
            def over(values):
                first = swap(values, "fsdp")
                return first, cross(d, first, 0)

            tile = (None, FT, FT)
            qkv = take(sc, w_qkv, (None, 3, d.Q, d.W), lambda n, b: (layer, 0, b, 0),
                       (3, d.Q, d.W), deps=deps)
            out = take(sc, out_weight, (None, d.W // 2, d.H), lambda n, b: (layer, b, 0),
                       (d.W // 2, d.H), deps=(qkv,))
            up_a = take(sc, up_weight, tile, lambda n, b: (layer, 0, b), (FT, FT), deps=(out,))
            up_b = take(sc, up_weight, tile, lambda n, b: (layer, 0, half + b), (FT, FT),
                        deps=(up_a,))
            dn_a = take(sc, down_weight, tile, lambda n, b: (layer, b, 0), (FT, FT), deps=(up_b,))
            dn_b = take(sc, down_weight, tile, lambda n, b: (layer, half + b, 0), (FT, FT),
                        deps=(dn_a,))
            self.last = dn_b
            self.qkv, self.out = over(qkv), over(out)
            self.dn_a, self.dn_b = over(dn_a), over(dn_b)
            self.up_a, self.up_b = over(up_a), over(up_b)
            self.up = (*self.up_a, *self.up_b)
            self.down = (*self.dn_a, *self.dn_b)

    p0 = Pieces(0, ())
    p = [p0]
    kb = key_table(d, parent_ids, depth_offsets)

    def both(rows):
        got = swap(rows, "tp")
        return jnp.where(
            t == 0,
            jnp.concatenate([rows, got], axis=0),
            jnp.concatenate([got, rows], axis=0),
        )

    def row(values):
        return values.reshape(1, -1)

    def swapped(values):
        return swap(values, "tp")

    def fsdp(values):
        return swap(values, "fsdp")

    class Kept:
        pass

    def forward(layer, state, needs):
        k = kept[layer]
        before = [needs(n) for n in range(1)]
        k.hidden, k.n_o, n_s, chunks = qkv_forward(
            d, layer, sc, state, row(norm_gains[layer, 0]), row(row_biases[layer, 0]),
            w_qkv, p[layer].qkv, qv_bias[layer], deps=before[0])
        k.n_r = fsdp(n_s)
        if layer == 0:
            p.append(Pieces(1, (k.hidden,)))
        before += [needs(n) for n in range(1, 3)]
        k.chunks = all_to_all(chunks)
        outs = all_to_all(attend_forward(d, sc, kb, k.chunks, deps=before[1]))
        k.ctx, part = out_forward(d, layer, sc, out_weight, p[layer].out, outs, deps=before[2])
        k.ctx_r = fsdp(k.ctx)
        before.append(needs(3))
        k.middle, k.n2_o, k.act_p, k.act_q, k.dg, part2 = ffn_forward(
            d, layer, sc, k.hidden, part, swapped(part), row(row_biases[layer, 1]),
            row(norm_gains[layer, 1]), row(row_biases[layer, 2]), up_weight,
            p[layer].up, row(up_bias[layer]), down_weight, p[layer].down, deps=before[3])
        state = (k.middle, part2, swapped(part2), row(row_biases[layer, 3]))
        k.act_pr, k.act_qr = fsdp(k.act_p), fsdp(k.act_q)
        return state

    state = both(tokens)
    p0 = p[0]
    kept = [Kept() for _ in range(LAYERS)]
    k0, k1 = kept
    state = forward(0, state, lambda n: (
        (p0.out[0], p0.up_a[0], p0.last) if n == 0
        else (p0.out[1], p0.up_a[1], p0.up_b[0], p0.dn_a[0], p[1].last) if n == 1
        else (p0.dn_b[0], p[1].qkv[0], p[1].out[0]) if n == 2
        else ()
    ))
    p1 = p[1]
    state = forward(1, state, lambda n: (
        (p1.up_a[0],) if n == 0
        else (p1.out[1], p1.up_a[1], p1.up_b[0], p1.dn_a[0]) if n == 1
        else (p1.dn_b[0], k1.n_r, k0.act_pr) if n == 2
        else ()
    ))
    own_rows = tokens.shape[0]

    def mine(values):
        return lax.dynamic_slice_in_dim(values, t * own_rows, own_rows, 0)

    output = mine(state[0]) + (
        (mine(state[1]).astype(F32) + mine(state[2]).astype(F32)) + state[3]
    )
    output = output.astype(BF)
    grad = both(cotangent)
    sums = [None] * LAYERS
    def grad_ffn(k, more, mix, deps=()):
        ins = (k.n2_o, k.act_p, k.act_pr, k.act_q, k.act_qr, k.xba, k.xba_r, k.xbb, k.xbb_r,
               k.db_o)
        jobs = []
        for f in range(tiles):
            at = (5, 1) if f == 0 else (7, f - 1)
            jobs.append(((0, None), at, (2, 0), (at[0] + 1, at[1])))
        for f in range(tiles):
            at = (1, 1 + f) if f < half else (3, f - half)
            jobs.append((at, (9, None), (at[0] + 1, at[1]), (6, 0)))
        if more:
            ins += (k.ctx, k.ctx_r, k.da_o, k.da_r)
            jobs += [((10, None), (12, None), (11, None), (13, None))]
        return Sum(d, mix, *weight_grad(d, "ffn", sc, ins, jobs, mix, deps=deps))

    def grad_qkv(k, more, mix, flat=None, deps=()):
        ins = (k.n_o, k.n_r, k.xc, k.xc_r)
        jobs = [((0, None), (2, n), (1, None), (3, n)) for n in range(3)]
        if more:
            ins += (k.ctx, k.da_o, k.ctx_r, k.da_r)
            jobs += [((4, None), (5, None), (6, None), (7, None))]
        return Sum(d, mix, *weight_grad(d, "qkv", sc, ins, jobs, mix, flat, deps))

    def back_ffn(layer, k, grad, deps=()):
        k.db_o, k.xba, k.xbb, k.usum, k.bsum, part = ffn_backward(
            d, layer, sc, grad, k.dg, up_weight, p[layer].up, down_weight, p[layer].down,
            deps=deps)
        k.xba_r, k.xbb_r = fsdp(k.xba), fsdp(k.xbb)
        return part

    def back_context(layer, k, grad, part, deps=()):
        k.dmid, k.da_o, k.da_s, k.gsum2, k.ssum2, k.asum, dchunks = context_backward(
            d, layer, sc, grad, part, swapped(part), k.middle, row(norm_gains[layer, 1]),
            out_weight, p[layer].out, deps=deps)
        k.da_r = fsdp(k.da_s)
        return dchunks

    def back_qkv(layer, k, dparts, deps=()):
        k.xc, k.qvsum, part = qkv_backward(
            d, layer, sc, w_qkv, p[layer].qkv, dparts, deps=deps)
        k.xc_r = fsdp(k.xc)
        return part

    def back_input(layer, k, part, deps=()):
        grad, k.gsum1, k.ssum1 = input_backward(
            d, k.dmid, part, swapped(part), k.hidden, row(norm_gains[layer, 0]), deps=deps)
        sums[layer] = (k.qvsum, k.usum, k.gsum1, k.gsum2, k.ssum1, k.asum, k.ssum2, k.bsum)
        return grad

    total = LAYERS * (2 * d.W + d.F + 6 * d.D)

    def small_sums():
        flat = jnp.concatenate([v.reshape(-1) for layer in sums for v in layer])
        return jnp.pad(flat, (0, d.C * EXTRA * FT - total)).reshape(d.C, EXTRA, FT)

    part = back_ffn(1, k1, grad, (k0.act_qr, k1.ctx_r))
    dchunks = back_context(1, k1, grad, part, (state[2],))
    dback = attend_backward(d, sc, kb, k1.chunks, all_to_all(dchunks),
                            deps=(k1.act_pr, k1.act_qr))
    dparts = all_to_all(dback)
    f1 = grad_ffn(k1, False, True, (dback,))
    part = back_qkv(1, k1, dparts, (f1.keep,))
    grad = back_input(1, k1, part)
    part = back_ffn(0, k0, grad)
    a = f1.step(part)
    dchunks = back_context(0, k0, grad, part, (a, k1.xc_r))
    q1 = grad_qkv(k1, True, False, None, (dchunks,))
    a = f1.step(q1.keep)
    dback = attend_backward(d, sc, kb, k0.chunks, all_to_all(dchunks),
                            deps=(a, k0.xba_r, k0.ctx_r, k0.n_r))
    dparts = all_to_all(dback)
    f0 = grad_ffn(k0, True, True, (dback,))
    part = back_qkv(0, k0, dparts, (f0.keep,))
    grad = back_input(0, k0, part)
    flat = small_sums()
    flat = flat + swap(flat, "fsdp")
    a = f1.step(grad)
    q0 = grad_qkv(k0, False, "z", flat, (a,))
    a = q0.keep
    ffn_kinds = (("cols", tiles), ("mats", tiles))
    qkv_kinds = (("mats", 3), ("mats", 1))
    last = 2 * d.bits - 1
    for unit in (f0, q1, q0, f1, f0, q1, f1, q0, f0, q1, q0, f0, q1, q0):
        if unit.at < last:
            a = unit.step(a)
    while f1.at < last:
        a = f1.step(a)
    g_ffn = place(d, 1, sc, f1, (), ffn_kinds, "ffn", (a,))
    a = g_ffn[0]
    for unit in (q1, q0, f0):
        while unit.at < last:
            a = unit.step(a)
    g_up, g_down, g_out = place(d, 0, sc, f0, (*g_ffn, None), (*ffn_kinds, ("mats", 1)),
                                "ffn", (a,))
    g_qkv, g_out = place(d, 1, sc, q1, (None, g_out), qkv_kinds, "qkv", (g_up,))
    g_qkv, qv_grad, up_grad, gain_grad, bias_grad = place(
        d, 0, sc, q0, (g_qkv,), (("mats", 3),), "qkv", (g_out,))
    return (
        output,
        mine(grad),
        g_qkv.transpose(0, 2, 1, 3),
        g_out.reshape(LAYERS, d.W, d.H),
        g_up.reshape(LAYERS, d.H, d.F),
        g_down.reshape(LAYERS, d.F, d.H),
        qv_grad,
        up_grad,
        gain_grad,
        bias_grad,
    )


def solution(mesh):
    in_specs = (
        P(("fsdp", "ctx", "tp"), None),
        P(None, "fsdp", None, "tp"),
        P(None, "tp", "fsdp"),
        P(None, "fsdp", "tp"),
        P(None, "tp", "fsdp"),
        P(None, None, "tp"),
        P(None, "tp"),
        P(),
        P(),
        P(),
        P(),
        P(("fsdp", "ctx", "tp"), None),
    )
    out_specs = (
        P(("fsdp", "ctx", "tp"), None),
        P(("fsdp", "ctx", "tp"), None),
        P(None, "fsdp", None, "tp"),
        P(None, "tp", "fsdp"),
        P(None, "fsdp", "tp"),
        P(None, "tp", "fsdp"),
        P(None, None, "tp"),
        P(None, "tp"),
        P(),
        P(),
    )
    return jax.shard_map(
        on_device, mesh=mesh, in_specs=in_specs, out_specs=out_specs, check_vma=False
    )
```
